512 devices in a mesh: sector: 64 (over y, z), axial: 8 (over x, core).
Axes of the slice: x: 4, y: 8, z: 8, core: 2. Of those that a mesh axis runs over, the one named last changes fastest.
Arguments:
- right_side: float32 [16, 32, 8192], P(None, 'axial', 'sector'), may hold values from -6 to 6
- mass_term: float32 [32, 8192], P('axial', 'sector'), may hold values from 0.05 to 2
- band_weight: float32 [8, 8192], P('axial', 'sector'), may hold values from 0.5 to 2
- band_shift: int32 [1], replicated, may hold values from 1 to 63
- local_solver: bfloat16 [8, 32768, 780], P('axial', 'sector'), may hold values from -0.25 to 0.25
- coarse_inverse: bfloat16 [8192, 8192], P(('sector', 'axial')), may hold values from -1 to 1
- coarse_basis: bfloat16 [16, 32, 8192], P(None, 'axial', 'sector'), may hold values from -0.25 to 0.25
Outputs:
- solution: float32 [16, 32, 8192], P(None, 'axial', 'sector')
- residual: float32 [16, 32, 8192], P(None, 'axial', 'sector')
The draws below stay inside these ranges and needn't reach their ends.
All inputs are finite; a program needn't handle non-finite values.
Results may differ from the reference program's by a relative error of at most 0.0027.
Values may be sent and summed in bfloat16 or wider, within the bound.
A program may use at most 64 MiB of HBM per device.

```python
import math
import jax
import jax.numpy as jnp
from jax import lax

RHS = 16
GA = 4
GS = 128
NV = 16
ITERS = 2
OWN = 512
NEXT = 780
NA = 32
NS = 8192
NCOARSE = 8192
N_SECTOR = 64
N_AXIAL = 8


def draw_local_solver(key, part):
    key = jax.random.fold_in(key, 11)
    key_diag, key_off = jax.random.split(key, 2)
    full_shape = (N_AXIAL, N_SECTOR * OWN, NEXT)
    row_index = lax.broadcasted_iota(jnp.int32, full_shape, 1) % OWN
    col_index = lax.broadcasted_iota(jnp.int32, full_shape, 2)
    centre = (row_index // GS + 1) * (GS + 2) + row_index % GS + 1
    off_scale = 0.05 / math.sqrt(NEXT)
    diag_vals = jax.random.uniform(key_diag, full_shape, jnp.float32, 0.12, 0.2)
    off_vals = jnp.clip(jax.random.normal(key_off, full_shape, jnp.float32), -4.0, 4.0) * off_scale
    return jnp.where(col_index == centre, diag_vals, off_vals).astype(jnp.bfloat16)


def draw_coarse_inverse(key, part):
    key = jax.random.fold_in(key, 23)
    key_diag, key_off = jax.random.split(key, 2)
    full_shape = (NCOARSE, NCOARSE)
    row_index = lax.broadcasted_iota(jnp.int32, full_shape, 0)
    col_index = lax.broadcasted_iota(jnp.int32, full_shape, 1)
    off_scale = 0.3 / math.sqrt(NCOARSE)
    diag_vals = jax.random.uniform(key_diag, full_shape, jnp.float32, 0.3, 0.6)
    off_vals = jnp.clip(jax.random.normal(key_off, full_shape, jnp.float32), -4.0, 4.0) * off_scale
    return jnp.where(col_index == row_index, diag_vals, off_vals).astype(jnp.bfloat16)


def shard_levels(stream_key, dims, cuts, low, largest):
    level = 1.0
    for axis_at, shards_of in cuts:
        heights = jax.random.uniform(jax.random.fold_in(jax.random.fold_in(stream_key, 6), axis_at), (shards_of,), jnp.float32, low / len(cuts), largest / len(cuts))
        level = level * jnp.repeat(jnp.exp(heights), dims[axis_at] // shards_of).reshape((-1,) + (1,) * (len(dims) - 1 - axis_at))
    return level


def scatter_about(stream_key, extent, scale, reach, shards=(), held_as=jnp.bfloat16):
    array = jax.random.normal(stream_key, extent, jnp.float32) * scale
    if len(shards) > 0:
        array = shard_levels(stream_key, extent, shards, -0.22, 0.18) * array
    return jnp.clip(array, min=-reach, max=reach).astype(held_as)


def setup_inputs(seed: int = 0) -> dict:
    arg_keys = jax.random.split(jax.random.key(seed), 8)
    right_side = scatter_about(arg_keys[0], (RHS, NA, NS), 1.0, 6.0, ((1, 8), (2, 64)), jnp.float32)
    mass_term = jnp.clip(jnp.exp(math.log(2.0) - 3.6888794 * jax.random.uniform(arg_keys[1], (NA, NS), jnp.float32) ** shard_levels(arg_keys[1], (NA, NS), ((0, 8), (1, 64)), -0.2, 0.2)), 0.05, 2.0)
    band_weight = jnp.clip(0.5 + 1.5 * jax.random.uniform(arg_keys[2], (N_AXIAL, NS), jnp.float32) ** shard_levels(arg_keys[2], (N_AXIAL, NS), ((0, 8), (1, 64)), -0.2, 0.2), 0.5, 2.0)
    band_shift = jax.random.randint(arg_keys[3], (1,), 1, N_SECTOR).astype(jnp.int32)
    local_solver = draw_local_solver(jax.random.fold_in(arg_keys[7], 71), 0)
    coarse_inverse = draw_coarse_inverse(jax.random.fold_in(arg_keys[7], 71), 0)
    coarse_basis = scatter_about(arg_keys[6], (NV, NA, NS), OWN ** -0.5, 0.25, ((1, 8), (2, 64)))
    return dict(right_side=right_side, mass_term=mass_term, band_weight=band_weight, band_shift=band_shift, local_solver=local_solver, coarse_inverse=coarse_inverse, coarse_basis=coarse_basis)


TOPMOST_ACCURACY = lax.Precision.HIGHEST
EPSILON = 1e-6


def apply_operator(field_in, mass_term, band_weight, band_shift):
    padded = jnp.pad(field_in, ((0, 0), (1, 1), (0, 0)))
    beside = padded[:, 2:, :] + padded[:, :-2, :]
    beside = beside + jnp.roll(field_in, 1, axis=2) + jnp.roll(field_in, -1, axis=2)
    result = (4.0 + mass_term)[None] * field_in - beside
    band_row = field_in[:, ::GA, :]
    rotated = jnp.roll(band_row, band_shift[0] * GS, axis=2)
    band_term = band_weight[None] * (band_row - rotated)
    return result.at[:, ::GA, :].add(band_term)


def schwarz(residual, local_solver):
    padded = jnp.pad(residual, ((0, 0), (1, 1), (0, 0)))
    padded = jnp.concatenate([padded[:, :, -1:], padded, padded[:, :, :1]], axis=2)
    row_index = jnp.arange(GA + 2, dtype=jnp.int32)[:, None]
    col_index = jnp.arange(GS + 2, dtype=jnp.int32)[None, :]
    corner = ((row_index == 0) | (row_index == GA + 1)) & ((col_index == 0) | (col_index == GS + 1))

    def one_window(flat_index):
        sector_pos = flat_index // N_AXIAL
        axial_location = flat_index % N_AXIAL
        window = lax.dynamic_slice(padded, (jnp.int32(0), (axial_location * GA).astype(jnp.int32), (sector_pos * GS).astype(jnp.int32)), (RHS, GA + 2, GS + 2))
        window = jnp.where(corner[None], 0.0, window).reshape(RHS, NEXT).astype(jnp.bfloat16)
        solver_rows = lax.dynamic_index_in_dim(local_solver, axial_location, 0, keepdims=False)
        solver_rows = lax.dynamic_slice_in_dim(solver_rows, (sector_pos * OWN).astype(jnp.int32), OWN, 0)
        return jnp.dot(window, solver_rows.T, preferred_element_type=jnp.float32)

    pieces = lax.map(one_window, jnp.arange(N_SECTOR * N_AXIAL, dtype=jnp.int32))
    pieces = pieces.reshape(N_SECTOR, N_AXIAL, RHS, GA, GS)
    return pieces.transpose(2, 1, 3, 0, 4).reshape(RHS, NA, NS)


def coarse_residual(residual, coarse_basis):
    resid_grid = residual.reshape(RHS, N_AXIAL, GA, N_SECTOR, GS)
    basis_lattice = coarse_basis.astype(jnp.float32).reshape(NV, N_AXIAL, GA, N_SECTOR, GS)
    coarse_vals = jnp.einsum('rAaSs,vAaSs->rSAv', resid_grid, basis_lattice, precision=TOPMOST_ACCURACY)
    return coarse_vals.reshape(RHS, NCOARSE)


def coarse_solve(coarse_combined, coarse_inverse):
    blocks = coarse_inverse.reshape(N_SECTOR * N_AXIAL, NV, NCOARSE)

    def one_block(row_block):
        return jnp.dot(coarse_combined, row_block.astype(jnp.float32).T, precision=TOPMOST_ACCURACY)

    return lax.map(one_block, blocks)


def prolong(coarse_answer, coarse_basis):
    coarse_lattice = coarse_answer.reshape(N_SECTOR, N_AXIAL, RHS, NV)
    basis_lattice = coarse_basis.astype(jnp.float32).reshape(NV, N_AXIAL, GA, N_SECTOR, GS)
    spread_extent = jnp.einsum('wjmk,kjuwl->mjuwl', coarse_lattice, basis_lattice, precision=TOPMOST_ACCURACY)
    return spread_extent.reshape(RHS, NA, NS)


def reference(right_side, mass_term, band_weight, band_shift, local_solver, coarse_inverse, coarse_basis):
    solution = jnp.zeros_like(right_side)
    residual = right_side
    for sweep in range(ITERS):
        coarse_combined = coarse_residual(residual, coarse_basis)
        correction = schwarz(residual, local_solver) + prolong(coarse_solve(coarse_combined, coarse_inverse), coarse_basis)
        image_field = apply_operator(correction, mass_term, band_weight, band_shift)
        cross_sum = jnp.sum(residual * image_field, axis=(1, 2))
        square_sum = jnp.sum(image_field * image_field, axis=(1, 2))
        step_len = cross_sum / (square_sum + EPSILON)
        solution = solution + step_len[:, None, None] * correction
        residual = residual - step_len[:, None, None] * image_field
    return solution, residual
```

```python
import jax
import jax.numpy as jnp
from jax import lax
from jax.experimental import pallas as pl
from jax.experimental.pallas import tpu as pltpu
from jax.sharding import PartitionSpec as P

EPSILON = 1e-06
MESH = pl.DeviceIdType.MESH
F32 = jnp.float32
BF16 = jnp.bfloat16

R = 16
GA = 4
GS = 128
NV = 16
NEXT = 780
NZ = 8
NY = 8
NSEC = NY * NZ
NAX = 8
YROWS = 3 * R
XROWS = 2 * R


def nt(a, b):
    return lax.dot_general(a, b, (((1,), (1,)), ((), ())), preferred_element_type=F32)


def nn(a, b):
    return lax.dot_general(a, b, (((1,), (0,)), ((), ())), preferred_element_type=F32)


def two_parts(x):
    high = x.astype(BF16)
    low = (x - high.astype(F32)).astype(BF16)
    return jnp.concatenate([high, low], axis=0)


def joined(x):
    half = x.shape[0] // 2
    return x[:half] + x[half:]


def body(
    rhs_ref, mass_ref, bw_ref, shift_ref, basis_ref, solver_hbm, inverse_hbm,
    sol_ref, res_ref,
    solver, turned, h_send, h_recv, x_send, x_recv, y_send, y_recv, z_send, z_recv,
    b1_first, b1_second, b2_first, b2_second, tiles,
    local_sems, t_ssem, t_rsem, h_ssem, h_rsem, x_ssem, x_rsem, y_ssem, y_rsem,
    z_ssem, z_rsem, b1_ssem, b1_rsem, b2_ssem, b2_rsem,
):
    b1s = (b1_first, b1_second)
    b2s = (b2_first, b2_second)
    s = lax.axis_index("sector")
    q = lax.axis_index("axial")
    y = s // NZ
    z = s % NZ

    def x_peer(k):
        return (s, (q + k) % NAX)

    def y_peer(k):
        return (((y + k) % NY) * NZ + z, q)

    def z_peer(k):
        return (y * NZ + (z + k) % NZ, q)

    def s_peer(k):
        return ((s + k) % NSEC, q)

    def wait_for(ref, sem):
        pltpu.make_async_copy(ref, ref, sem).wait()

    def remote(src, dst, ssem, rsem, device):
        pltpu.make_async_remote_copy(
            src_ref=src, dst_ref=dst, send_sem=ssem, recv_sem=rsem,
            device_id=device, device_id_type=MESH,
        ).start()

    solver_copy = pltpu.make_async_copy(solver_hbm.at[0], solver, local_sems.at[0])
    solver_copy.start()
    own_copy = pltpu.make_async_copy(
        inverse_hbm.at[:, pl.ds(pl.multiple_of(s * GS, GS), GS)], turned.at[NSEC - 1], local_sems.at[1]
    )
    own_copy.start()

    barrier = pltpu.get_barrier_semaphore()

    def greet(k, carry):
        pl.semaphore_signal(barrier, inc=1, device_id=s_peer(k), device_id_type=MESH)
        return carry

    lax.fori_loop(1, NSEC, greet, 0)
    for k in range(1, NAX):
        pl.semaphore_signal(barrier, inc=1, device_id=x_peer(k), device_id_type=MESH)

    lane = lax.broadcasted_iota(jnp.int32, (R, GS), 1)
    rows128 = lax.broadcasted_iota(jnp.int32, (NAX * NV, GS), 0) // NV
    rhs = rhs_ref[...]
    r0 = [rhs[:, a, :] for a in range(GA)]
    basis_all = basis_ref[...].astype(F32)
    basis = [basis_all[:, a, :] for a in range(GA)]
    mass = [mass_ref[a : a + 1, :] + 4.0 for a in range(GA)]
    weight = bw_ref[...]
    shift = shift_ref[0]
    shift_y = shift // NZ
    shift_z = shift % NZ

    def spread(tile, at):
        return jnp.where(rows128 == at, jnp.concatenate([tile] * 8, axis=0), 0.0).astype(BF16)

    basis_q = jnp.concatenate([spread(t, q) for t in basis], axis=1)
    basis_z = jnp.concatenate([spread(t, z) for t in basis], axis=1)

    def coarse_of(field):
        return joined(nt(two_parts(jnp.concatenate(field, axis=1)), basis_q))

    def edges(field):
        tile = jnp.zeros((R, GS), F32)
        for a in range(GA):
            at = 2 * (a + 1)
            tile = jnp.where(lane == at, pltpu.roll(field[a], at + 1, 1), tile)
            tile = jnp.where(lane == at + 1, pltpu.roll(field[a], at + 1, 1), tile)
        return tile

    def send_halo(n, field):
        h_send[n, 0] = edges(field)
        h_send[n, 1] = field[0]
        h_send[n, 2] = field[GA - 1]
        remote(h_send.at[n, 2], h_recv.at[n, 2], h_ssem.at[n], h_rsem.at[n], x_peer(1))
        remote(h_send.at[n, 1], h_recv.at[n, 3], h_ssem.at[n], h_rsem.at[n], x_peer(NAX - 1))
        remote(h_send.at[n, 0], h_recv.at[n, 0], h_ssem.at[n], h_rsem.at[n], s_peer(1))
        remote(h_send.at[n, 0], h_recv.at[n, 1], h_ssem.at[n], h_rsem.at[n], s_peer(NSEC - 1))

    def get_halo(n):
        wait_for(h_recv.at[n], h_rsem.at[n])
        above = jnp.where(q == 0, 0.0, h_recv[n, 2])
        below = jnp.where(q == NAX - 1, 0.0, h_recv[n, 3])
        return h_recv[n, 0], h_recv[n, 1], above, below

    def local_solve(field, halo):
        left, right, above, below = halo
        stack = [above] + field + [below]
        turned_rows = [pltpu.roll(stack[j], 2 * j + 1, 1) for j in range(GA + 2)]
        zero = jnp.zeros((R, GS), F32)
        parts = []
        for t in range(GA + 3):
            here = turned_rows[t] if t < GA + 2 else zero
            before = turned_rows[t - 1] if t > 0 else zero
            tile = jnp.where(lane == 2 * t - 1, right, before)
            tile = jnp.where(lane == 2 * t, left, tile)
            parts.append(jnp.where(lane > 2 * t, here, tile))
        window = jnp.concatenate(parts, axis=1)
        out = joined(nt(two_parts(window)[:, :NEXT], solver[...]))
        return [out[:, a * GS : (a + 1) * GS] for a in range(GA)]

    def apply_operator(field, halo, band):
        left, right, above, below = halo
        stack = [above] + field + [below]
        image = []
        for a in range(GA):
            u = field[a]
            before = jnp.where(lane == 0, pltpu.roll(left, GS - 2 * (a + 1), 1), pltpu.roll(u, 1, 1))
            after = jnp.where(
                lane == GS - 1, pltpu.roll(right, GS - 1 - (2 * a + 3), 1), pltpu.roll(u, GS - 1, 1)
            )
            value = mass[a] * u - ((stack[a + 2] + stack[a]) + before + after)
            if a == 0:
                value = value + weight * (u - band)
            image.append(value)
        return image

    def send_band(n, rows):
        b1s[n][0] = rows
        for k in range(1, NZ):
            remote(b1s[n].at[0], b1s[n].at[k], b1_ssem.at[n], b1_rsem.at[n], s_peer(k))

    def forward_band(n):
        wait_for(b1s[n].at[pl.ds(1, NZ - 1)], b1_rsem.at[n])
        b2s[n][0] = b1s[n][shift_z]
        for k in range(1, NY):
            remote(b2s[n].at[0], b2s[n].at[k], b2_ssem.at[n], b2_rsem.at[n], y_peer(k))

    def get_band(n):
        wait_for(b2s[n].at[pl.ds(1, NY - 1)], b2_rsem.at[n])
        return b2s[n][shift_y]

    def send_x(n, coarse, inner):
        x_send[n, pl.ds(0, R)] = coarse
        x_send[n, pl.ds(R, R)] = inner
        for k in range(1, NAX):
            remote(x_send.at[n], x_recv.at[n, k - 1], x_ssem.at[n], x_rsem.at[n], x_peer(k))

    def get_x(n):
        wait_for(x_recv.at[n], x_rsem.at[n])
        total = x_send[n]
        for k in range(NAX - 1):
            total = total + x_recv[n, k]
        return total[:R], total[R:]

    def send_y(n, coarse, inner):
        out = joined(nt(two_parts(coarse), turned_matrix))
        rolled = []
        for t in range(NY):
            tile = out[:, t * GS : (t + 1) * GS]
            y_send[n, t, pl.ds(0, R)] = tile
            y_send[n, t, pl.ds(2 * R, R)] = inner
            tiles[t] = pltpu.roll(tile, shift_z * NV, 1)
        for t in range(NY):
            here = tiles[(t + NY - shift_y) % NY]
            before = tiles[(t + NY - 1 - shift_y) % NY]
            y_send[n, t, pl.ds(R, R)] = jnp.where(lane >= shift_z * NV, here, before)
        for k in range(1, NY):
            remote(
                y_send.at[n, (y + k) % NY], y_recv.at[n, k - 1], y_ssem.at[n], y_rsem.at[n], y_peer(k)
            )

    def pass_z(n):
        wait_for(y_recv.at[n], y_rsem.at[n])
        total = y_send[n, y]
        for k in range(NY - 1):
            total = total + y_recv[n, k]
        z_send[n] = total
        for k in range(1, NZ):
            remote(z_send.at[n], z_recv.at[n, k - 1], z_ssem.at[n], z_rsem.at[n], z_peer(k))

    def get_z(n):
        wait_for(z_recv.at[n], z_rsem.at[n])
        total = z_send[n]
        for k in range(NZ - 1):
            total = total + z_recv[n, k]
        return total[:R], total[R : 2 * R], total[2 * R :]

    def prolong(coarse, rows):
        out = joined(nn(two_parts(coarse), rows))
        return [out[:, i * GS : (i + 1) * GS] for i in range(rows.shape[1] // GS)]

    def inner_products(residual, image):
        cross = residual[0] * image[0]
        square = image[0] * image[0]
        for a in range(1, GA):
            cross = cross + residual[a] * image[a]
            square = square + image[a] * image[a]
        cross = jnp.sum(cross, axis=1, keepdims=True)
        square = jnp.sum(square, axis=1, keepdims=True)
        return jnp.where(lane == 0, cross, jnp.where(lane == 1, square, 0.0))

    def step_of(inner):
        return inner[:, 0:1] / (inner[:, 1:2] + EPSILON)

    nothing = jnp.zeros((R, GS), F32)
    coarse_r0 = coarse_of(r0)

    pl.semaphore_wait(barrier, NSEC - 1 + NAX - 1)

    send_halo(0, r0)
    send_x(0, coarse_r0, nothing)

    def turn(j, carry):
        k = (j * 27) % NSEC
        to = (s + k) % NSEC
        remote(
            inverse_hbm.at[:, pl.ds(pl.multiple_of(to * GS, GS), GS)],
            turned.at[k - 1], t_ssem, t_rsem, (to, q),
        )
        return carry

    lax.fori_loop(1, NSEC, turn, 0)

    halo_r0 = get_halo(0)
    solver_copy.wait()
    local_r0 = local_solve(r0, halo_r0)
    send_band(0, jnp.concatenate([local_r0[0], basis[0]], axis=0))
    coarse_sum, _ = get_x(0)
    own_copy.wait()
    wait_for(turned.at[pl.ds(0, NSEC - 1)], t_rsem)
    blocks = [turned[(s - p + NSEC - 1) % NSEC] for p in range(NSEC)]
    turned_matrix = jnp.concatenate(blocks, axis=0)

    send_y(0, coarse_sum, nothing)
    forward_band(0)
    pass_z(0)
    band_rows = get_band(0)
    band_basis = spread(band_rows[R:], z)
    y_own, y_band, _ = get_z(0)
    corr0 = [u + v for u, v in zip(local_r0, prolong(y_own, basis_z))]
    send_halo(1, corr0)
    band_corr0 = band_rows[:R] + prolong(y_band, band_basis)[0]
    halo = get_halo(1)
    image0 = apply_operator(corr0, halo, band_corr0)

    send_halo(2, image0)
    send_x(1, coarse_of(image0), inner_products(r0, image0))
    local_im = local_solve(image0, get_halo(2))
    send_band(1, jnp.concatenate([local_im[0], nothing], axis=0))
    coarse_sum, inner = get_x(1)
    send_y(1, coarse_sum, inner)
    forward_band(1)
    pass_z(1)
    band_rows = get_band(1)
    y_own, y_band, inner = get_z(1)
    diff = [u + v for u, v in zip(local_im, prolong(y_own, basis_z))]
    send_halo(3, diff)
    band_diff = band_rows[:R] + prolong(y_band, band_basis)[0]
    step0 = step_of(inner)
    corr1 = [u - step0 * v for u, v in zip(corr0, diff)]
    res1 = [u - step0 * v for u, v in zip(r0, image0)]
    image_diff = apply_operator(diff, get_halo(3), band_diff)
    image1 = [u - step0 * v for u, v in zip(image0, image_diff)]

    inner = inner_products(res1, image1)
    send_x(2, nothing, inner)
    _, inner = get_x(2)
    for t in range(NY):
        y_send[2, t, pl.ds(0, R)] = nothing
        y_send[2, t, pl.ds(R, R)] = nothing
        y_send[2, t, pl.ds(2 * R, R)] = inner
    for k in range(1, NY):
        remote(y_send.at[2, (y + k) % NY], y_recv.at[2, k - 1], y_ssem.at[2], y_rsem.at[2], y_peer(k))
    pass_z(2)
    _, _, inner = get_z(2)
    step1 = step_of(inner)
    for a in range(GA):
        sol_ref[:, a, :] = step0 * corr0[a] + step1 * corr1[a]
        res_ref[:, a, :] = res1[a] - step1 * image1[a]

    wait_for(turned.at[pl.ds(0, NSEC - 1)], t_ssem)
    for n in range(4):
        wait_for(h_recv.at[n], h_ssem.at[n])
    for n in range(3):
        wait_for(x_recv.at[n], x_ssem.at[n])
        wait_for(y_recv.at[n], y_ssem.at[n])
        wait_for(z_recv.at[n], z_ssem.at[n])
    for n in range(2):
        wait_for(b1s[n].at[pl.ds(1, NZ - 1)], b1_ssem.at[n])
        wait_for(b2s[n].at[pl.ds(1, NY - 1)], b2_ssem.at[n])


def on_device(
    right_side, mass_term, band_weight, band_shift, local_solver, coarse_inverse, coarse_basis
):
    vmem = pl.BlockSpec(memory_space=pltpu.VMEM)
    smem = pl.BlockSpec(memory_space=pltpu.SMEM)
    hbm = pl.BlockSpec(memory_space=pl.ANY)
    dma = pltpu.SemaphoreType.DMA
    out = jax.ShapeDtypeStruct(right_side.shape, F32)
    return pl.pallas_call(
        body,
        name="schwarz_steps",
        out_shape=(out, out),
        in_specs=[vmem, vmem, vmem, smem, vmem, hbm, hbm],
        out_specs=(vmem, vmem),
        scratch_shapes=[
            pltpu.VMEM((GA * GS, NEXT), BF16),
            pltpu.VMEM((NSEC, NV, GS), BF16),
            pltpu.VMEM((4, 3, R, GS), F32),
            pltpu.VMEM((4, 4, R, GS), F32),
            pltpu.VMEM((3, XROWS, GS), F32),
            pltpu.VMEM((3, NAX - 1, XROWS, GS), F32),
            pltpu.VMEM((3, NY, YROWS, GS), F32),
            pltpu.VMEM((3, NY - 1, YROWS, GS), F32),
            pltpu.VMEM((3, YROWS, GS), F32),
            pltpu.VMEM((3, NZ - 1, YROWS, GS), F32),
            pltpu.VMEM((NZ, 2 * R, GS), F32),
            pltpu.VMEM((NZ, 2 * R, GS), F32),
            pltpu.VMEM((NY, 2 * R, GS), F32),
            pltpu.VMEM((NY, 2 * R, GS), F32),
            pltpu.VMEM((NY, R, GS), F32),
            dma((2,)),
            dma,
            dma,
            dma((4,)),
            dma((4,)),
            dma((3,)),
            dma((3,)),
            dma((3,)),
            dma((3,)),
            dma((3,)),
            dma((3,)),
            dma((2,)),
            dma((2,)),
            dma((2,)),
            dma((2,)),
        ],
        compiler_params=pltpu.CompilerParams(
            collective_id=0, has_side_effects=True, vmem_limit_bytes=32 << 20
        ),
    )(right_side, mass_term, band_weight, band_shift, coarse_basis, local_solver, coarse_inverse)


def solution(mesh):
    placed = (
        P(None, "axial", "sector"),
        P("axial", "sector"),
        P("axial", "sector"),
        P(),
        P("axial", "sector", None),
        P(("sector", "axial"), None),
        P(None, "axial", "sector"),
    )
    return jax.shard_map(
        on_device,
        mesh=mesh,
        in_specs=placed,
        out_specs=(P(None, "axial", "sector"), P(None, "axial", "sector")),
        check_vma=False,
    )
```

```python
import jax
import jax.numpy as jnp
from jax import lax
from jax.experimental import pallas as pl
from jax.experimental.pallas import tpu as pltpu
from jax.sharding import PartitionSpec as P

EPSILON = 1e-06
MESH = pl.DeviceIdType.MESH
F32 = jnp.float32
BF16 = jnp.bfloat16

R = 16
GA = 4
GS = 128
NV = 16
NEXT = 780
NZ = 8
NY = 8
NSEC = NY * NZ
NAX = 8
XROWS = R + 8


def nt(a, b):
    return lax.dot_general(a, b, (((1,), (1,)), ((), ())), preferred_element_type=F32)


def nn(a, b):
    return lax.dot_general(a, b, (((1,), (0,)), ((), ())), preferred_element_type=F32)


def two_parts(x):
    high = x.astype(BF16)
    low = (x - high.astype(F32)).astype(BF16)
    return jnp.concatenate([high, low], axis=0)


def joined(x):
    half = x.shape[0] // 2
    return x[:half] + x[half:]


def body(
    rhs_ref, mass_ref, bw_ref, shift_ref, basis_ref, solver_hbm, inverse_hbm,
    sol_ref, res_ref,
    solver, inverse_y, h_send, h_recv, x_send, x_recv, z_tiles, y_send, y_recv,
    w_first, w_second, b1_first, b1_second, b2_first, b2_second, f_send, f_recv,
    local_sems, m_ssem, m_rsem, h_ssem, h_rsem, x_ssem, x_rsem, z_ssem, z_rsem,
    y_ssem, y_rsem, w_ssem, w_rsem, b1_ssem, b1_rsem, b2_ssem, b2_rsem, f_ssem, f_rsem,
):
    ws = (w_first, w_second)
    b1s = (b1_first, b1_second)
    b2s = (b2_first, b2_second)
    s = lax.axis_index("sector")
    q = lax.axis_index("axial")
    y = s // NZ
    z = s % NZ

    def x_peer(k):
        return (s, (q + k) % NAX)

    def y_peer(k):
        return (((y + k) % NY) * NZ + z, q)

    def z_peer(k):
        return (y * NZ + (z + k) % NZ, q)

    def s_peer(k):
        return ((s + k) % NSEC, q)

    def wait_for(ref, sem):
        pltpu.make_async_copy(ref, ref, sem).wait()

    def remote(src, dst, ssem, rsem, device):
        pltpu.make_async_remote_copy(
            src_ref=src, dst_ref=dst, send_sem=ssem, recv_sem=rsem,
            device_id=device, device_id_type=MESH,
        ).start()

    barrier = pltpu.get_barrier_semaphore()
    for k in range(1, 8):
        for peer in (y_peer(k), z_peer(k), x_peer(k)):
            pl.semaphore_signal(barrier, inc=1, device_id=peer, device_id_type=MESH)
    for k in (1, NSEC - 1):
        pl.semaphore_signal(barrier, inc=1, device_id=s_peer(k), device_id_type=MESH)

    solver_copy = pltpu.make_async_copy(solver_hbm.at[0], solver, local_sems.at[0])
    solver_copy.start()

    def inverse_for(to):
        return inverse_hbm.at[:, pl.ds(pl.multiple_of(to * NZ * GS, NZ * GS), NZ * GS)]

    own_copy = pltpu.make_async_copy(inverse_for(y), inverse_y.at[y], local_sems.at[1])
    own_copy.start()

    lane = lax.broadcasted_iota(jnp.int32, (R, GS), 1)
    lane8 = lax.broadcasted_iota(jnp.int32, (8, GS), 1)
    rows128 = lax.broadcasted_iota(jnp.int32, (8 * NV, GS), 0) // NV
    rhs = rhs_ref[...]
    r0 = [rhs[:, a, :] for a in range(GA)]
    basis_all = basis_ref[...].astype(F32)
    basis = [basis_all[:, a, :] for a in range(GA)]
    mass = [mass_ref[a : a + 1, :] + 4.0 for a in range(GA)]
    weight = bw_ref[...]
    shift = shift_ref[0]
    shift_z = shift % NZ
    shift_y = (shift // NZ + jnp.where(z < shift_z, 1, 0)) % NY

    def spread(tile, at):
        return jnp.where(rows128 == at, jnp.concatenate([tile] * 8, axis=0), 0.0).astype(BF16)

    basis_q = jnp.concatenate([spread(t, q) for t in basis], axis=1)
    basis_y = jnp.concatenate([spread(t, y) for t in basis], axis=1)

    def coarse_of(field):
        return joined(nt(two_parts(jnp.concatenate(field, axis=1)), basis_q))

    def edges(field):
        tile = jnp.zeros((R, GS), F32)
        for a in range(GA):
            at = 2 * (a + 1)
            moved = pltpu.roll(field[a], at + 1, 1)
            tile = jnp.where((lane == at) | (lane == at + 1), moved, tile)
        return tile

    def send_halo(n, field):
        h_send[n, 0] = edges(field)
        h_send[n, 1] = field[0]
        h_send[n, 2] = field[GA - 1]
        remote(h_send.at[n, 0], h_recv.at[n, 0], h_ssem.at[n], h_rsem.at[n], s_peer(1))
        remote(h_send.at[n, 0], h_recv.at[n, 1], h_ssem.at[n], h_rsem.at[n], s_peer(NSEC - 1))
        remote(h_send.at[n, 2], h_recv.at[n, 2], h_ssem.at[n], h_rsem.at[n], x_peer(1))
        remote(h_send.at[n, 1], h_recv.at[n, 3], h_ssem.at[n], h_rsem.at[n], x_peer(NAX - 1))

    def get_halo(n):
        wait_for(h_recv.at[n], h_rsem.at[n])
        above = jnp.where(q == 0, 0.0, h_recv[n, 2])
        below = jnp.where(q == NAX - 1, 0.0, h_recv[n, 3])
        return h_recv[n, 0], h_recv[n, 1], above, below

    def local_solve(field, halo):
        left, right, above, below = halo
        stack = [above] + field + [below]
        moved = [pltpu.roll(stack[j], 2 * j + 1, 1) for j in range(GA + 2)]
        zero = jnp.zeros((R, GS), F32)
        parts = []
        for t in range(GA + 3):
            here = moved[t] if t < GA + 2 else zero
            before = moved[t - 1] if t > 0 else zero
            tile = jnp.where(lane == 2 * t - 1, right, before)
            tile = jnp.where(lane == 2 * t, left, tile)
            parts.append(jnp.where(lane > 2 * t, here, tile))
        window = jnp.concatenate(parts, axis=1)
        out = joined(nn(two_parts(window)[:, :NEXT], solver[...]))
        return [out[:, a * GS : (a + 1) * GS] for a in range(GA)]

    def apply_operator(field, halo, band):
        left, right, above, below = halo
        stack = [above] + field + [below]
        image = []
        for a in range(GA):
            u = field[a]
            before = jnp.where(lane == 0, pltpu.roll(left, GS - 2 * (a + 1), 1), pltpu.roll(u, 1, 1))
            after = jnp.where(
                lane == GS - 1, pltpu.roll(right, GS - 1 - (2 * a + 3), 1), pltpu.roll(u, GS - 1, 1)
            )
            value = mass[a] * u - ((stack[a + 2] + stack[a]) + before + after)
            if a == 0:
                value = value + weight * (u - band)
            image.append(value)
        return image

    def send_band(n, rows):
        b1s[n][0] = rows
        for k in range(1, NZ):
            remote(b1s[n].at[0], b1s[n].at[k], b1_ssem.at[n], b1_rsem.at[n], z_peer(k))

    def forward_band(n):
        wait_for(b1s[n].at[pl.ds(1, NZ - 1)], b1_rsem.at[n])
        b2s[n][0] = b1s[n][shift_z]
        for k in range(1, NY):
            remote(b2s[n].at[0], b2s[n].at[k], b2_ssem.at[n], b2_rsem.at[n], y_peer(k))

    def get_band(n):
        wait_for(b2s[n].at[pl.ds(1, NY - 1)], b2_rsem.at[n])
        return b2s[n][shift_y]

    def rows_of(n):
        return pl.ds(0, R if n == 0 else XROWS)

    def send_x(n, coarse, inner):
        x_send[n, pl.ds(0, R)] = coarse
        if inner is not None:
            x_send[n, pl.ds(R, 8)] = inner
        for k in range(1, NAX):
            remote(
                x_send.at[n, rows_of(n)], x_recv.at[n, k - 1, rows_of(n)],
                x_ssem.at[n], x_rsem.at[n], x_peer(k),
            )

    def pass_z(n):
        wait_for(x_recv.at[n, :, rows_of(n)], x_rsem.at[n])
        total = x_send[n, rows_of(n)]
        for k in range(NAX - 1):
            total = total + x_recv[n, k, rows_of(n)]
        z_tiles[n, z, rows_of(n)] = total
        for k in range(1, NZ):
            remote(
                z_tiles.at[n, z, rows_of(n)], z_tiles.at[n, z, rows_of(n)],
                z_ssem.at[n], z_rsem.at[n], z_peer(k),
            )

    def pass_y(n):
        wait_for(z_tiles.at[n, pl.ds(0, NZ - 1), rows_of(n)], z_rsem.at[n])
        gathered = jnp.concatenate([z_tiles[n, t, pl.ds(0, R)] for t in range(NZ)], axis=1)
        if n == 0:
            own_copy.wait()
            wait_for(inverse_y.at[pl.ds(0, NY - 1)], m_rsem)
        matrix = jnp.concatenate([inverse_y[t] for t in range(NY)], axis=0)
        y_send[n, pl.ds(0, R)] = joined(nt(two_parts(gathered), matrix))
        if n > 0:
            inner = z_tiles[n, 0, pl.ds(R, 8)]
            for t in range(1, NZ):
                inner = inner + z_tiles[n, t, pl.ds(R, 8)]
            y_send[n, pl.ds(R, 8)] = inner
        for k in range(1, NY):
            remote(
                y_send.at[n, rows_of(n)], y_recv.at[n, k - 1, rows_of(n)],
                y_ssem.at[n], y_rsem.at[n], y_peer(k),
            )

    def get_y(n):
        wait_for(y_recv.at[n, :, rows_of(n)], y_rsem.at[n])
        total = y_send[n, rows_of(n)]
        for k in range(NY - 1):
            total = total + y_recv[n, k, rows_of(n)]
        return total[:R], total[R:]

    def send_coarse(n, tile):
        ws[n][0] = tile
        for k in range(1, NZ):
            remote(ws[n].at[0], ws[n].at[k], w_ssem.at[n], w_rsem.at[n], z_peer(k))

    def get_coarse(n):
        wait_for(ws[n].at[pl.ds(1, NZ - 1)], w_rsem.at[n])
        return ws[n][shift_z]

    def prolong(coarse, rows):
        out = joined(nn(two_parts(coarse), rows))
        return [out[:, i * GS : (i + 1) * GS] for i in range(rows.shape[1] // GS)]

    def inner_products(residual, image):
        cross = residual[0] * image[0]
        square = image[0] * image[0]
        for a in range(1, GA):
            cross = cross + residual[a] * image[a]
            square = square + image[a] * image[a]
        cross = jnp.sum(cross, axis=1, keepdims=True)
        square = jnp.sum(square, axis=1, keepdims=True)
        tile = jnp.zeros((8, GS), F32)
        for i, column in enumerate((cross[:8], square[:8], cross[8:], square[8:])):
            tile = jnp.where(lane8 == i, column, tile)
        return tile

    def step_of(inner):
        cross = jnp.concatenate([inner[:, 0:1], inner[:, 2:3]], axis=0)
        square = jnp.concatenate([inner[:, 1:2], inner[:, 3:4]], axis=0)
        return cross / (square + EPSILON)

    coarse_r0 = coarse_of(r0)

    pl.semaphore_wait(barrier, 7 + 7 + 7 + 2)

    send_x(0, coarse_r0, None)
    send_halo(0, r0)
    for k in range(1, NY):
        remote(inverse_for((y + k) % NY), inverse_y.at[y], m_ssem, m_rsem, y_peer(k))
    pass_z(0)
    halo_r0 = get_halo(0)
    solver_copy.wait()
    local_r0 = local_solve(r0, halo_r0)
    send_band(0, jnp.concatenate([local_r0[0], basis[0]], axis=0))
    pass_y(0)
    forward_band(0)
    coarse, _ = get_y(0)
    send_coarse(0, coarse)
    corr0 = [u + v for u, v in zip(local_r0, prolong(coarse, basis_y))]
    send_halo(1, corr0)
    band_rows = get_band(0)
    band_basis = spread(band_rows[R:], (y + NY - shift_y) % NY)
    band_corr0 = band_rows[:R] + prolong(get_coarse(0), band_basis)[0]
    image0 = apply_operator(corr0, get_halo(1), band_corr0)

    send_x(1, coarse_of(image0), inner_products(r0, image0))
    send_halo(2, image0)
    pass_z(1)
    local_im = local_solve(image0, get_halo(2))
    send_band(1, local_im[0])
    pass_y(1)
    forward_band(1)
    coarse, inner = get_y(1)
    send_coarse(1, coarse)
    diff = [u + v for u, v in zip(local_im, prolong(coarse, basis_y))]
    send_halo(3, diff)
    step0 = step_of(inner)
    corr1 = [u - step0 * v for u, v in zip(corr0, diff)]
    res1 = [u - step0 * v for u, v in zip(r0, image0)]
    band_row = get_band(1)
    band_diff = band_row + prolong(get_coarse(1), band_basis)[0]
    image_diff = apply_operator(diff, get_halo(3), band_diff)
    image1 = [u - step0 * v for u, v in zip(image0, image_diff)]

    inner = inner_products(res1, image1)
    for i, peer in enumerate((x_peer, y_peer, z_peer)):
        f_send[i] = inner
        for k in range(1, 8):
            remote(f_send.at[i], f_recv.at[i, k - 1], f_ssem.at[i], f_rsem.at[i], peer(k))
        wait_for(f_recv.at[i], f_rsem.at[i])
        for k in range(7):
            inner = inner + f_recv[i, k]
    step1 = step_of(inner)
    for a in range(GA):
        sol_ref[:, a, :] = step0 * corr0[a] + step1 * corr1[a]
        res_ref[:, a, :] = res1[a] - step1 * image1[a]

    wait_for(inverse_y.at[pl.ds(0, NY - 1)], m_ssem)
    for n in range(4):
        wait_for(h_recv.at[n], h_ssem.at[n])
    for n in range(2):
        wait_for(x_recv.at[n, :, rows_of(n)], x_ssem.at[n])
        wait_for(z_tiles.at[n, pl.ds(0, NZ - 1), rows_of(n)], z_ssem.at[n])
        wait_for(y_recv.at[n, :, rows_of(n)], y_ssem.at[n])
        wait_for(ws[n].at[pl.ds(1, NZ - 1)], w_ssem.at[n])
        wait_for(b1s[n].at[pl.ds(1, NZ - 1)], b1_ssem.at[n])
        wait_for(b2s[n].at[pl.ds(1, NY - 1)], b2_ssem.at[n])
    for i in range(3):
        wait_for(f_recv.at[i], f_ssem.at[i])


def on_device(
    right_side, mass_term, band_weight, band_shift, local_solver, coarse_inverse, coarse_basis
):
    vmem = pl.BlockSpec(memory_space=pltpu.VMEM)
    smem = pl.BlockSpec(memory_space=pltpu.SMEM)
    hbm = pl.BlockSpec(memory_space=pltpu.HBM)
    dma = pltpu.SemaphoreType.DMA
    out = jax.ShapeDtypeStruct(right_side.shape, F32)

    def tiles(*shape):
        return pltpu.VMEM(shape + (GS,), F32)

    return pl.pallas_call(
        body,
        name="schwarz_steps",
        out_shape=(out, out),
        in_specs=[vmem, vmem, vmem, smem, vmem, hbm, hbm],
        out_specs=(vmem, vmem),
        scratch_shapes=[
            pltpu.VMEM((NEXT, GA * GS), BF16),
            pltpu.VMEM((NY, NV, NZ * GS), BF16),
            tiles(4, 3, R),
            tiles(4, 4, R),
            tiles(2, XROWS),
            tiles(2, NAX - 1, XROWS),
            tiles(2, NZ, XROWS),
            tiles(2, XROWS),
            tiles(2, NY - 1, XROWS),
            tiles(NZ, R),
            tiles(NZ, R),
            tiles(NZ, 2 * R),
            tiles(NZ, R),
            tiles(NY, 2 * R),
            tiles(NY, R),
            tiles(3, 8),
            tiles(3, 7, 8),
            dma((2,)),
            dma,
            dma,
            dma((4,)),
            dma((4,)),
        ]
        + [dma((2,))] * 12
        + [dma((3,))] * 2,
        compiler_params=pltpu.CompilerParams(
            collective_id=0, has_side_effects=True, vmem_limit_bytes=32 << 20
        ),
    )(
        right_side, mass_term, band_weight, band_shift, coarse_basis,
        jnp.swapaxes(local_solver, 1, 2), coarse_inverse,
    )


def solution(mesh):
    placed = (
        P(None, "axial", "sector"),
        P("axial", "sector"),
        P("axial", "sector"),
        P(),
        P("axial", "sector", None),
        P(("sector", "axial"), None),
        P(None, "axial", "sector"),
    )
    return jax.shard_map(
        on_device,
        mesh=mesh,
        in_specs=placed,
        out_specs=(P(None, "axial", "sector"), P(None, "axial", "sector")),
        check_vma=False,
    )
```

```python
import jax
import jax.numpy as jnp
from jax import lax
from jax.experimental import pallas as pl
from jax.experimental.pallas import tpu as pltpu
from jax.sharding import PartitionSpec as P

EPSILON = 1e-06
MESH = pl.DeviceIdType.MESH
F32 = jnp.float32
BF16 = jnp.bfloat16

R = 16
GA = 4
GS = 128
NV = 16
NEXT = 780
NZ = 8
NY = 8
NSEC = NY * NZ
NAX = 8
XROWS = R + 8
FAR_FIRST = (4, 3, 5, 2, 6, 1, 7)


def nt(a, b):
    return lax.dot_general(a, b, (((1,), (1,)), ((), ())), preferred_element_type=F32)


def nn(a, b):
    return lax.dot_general(a, b, (((1,), (0,)), ((), ())), preferred_element_type=F32)


def two_parts(x):
    high = x.astype(BF16)
    low = (x - high.astype(F32)).astype(BF16)
    return jnp.concatenate([high, low], axis=0)


def joined(x):
    half = x.shape[0] // 2
    return x[:half] + x[half:]


def body(
    rhs_hbm, mass_hbm, bw_hbm, shift_ref, basis_hbm, solver_hbm, inverse_hbm,
    sol_ref, res_ref,
    rhs_ref, mass_ref, bw_ref, basis_ref,
    solver, inverse_y, h_send, h_recv, x_send, x_recv, z_tiles, y_send, y_recv,
    w_first, w_second, b1_first, b1_second, b2_first, b2_second, basis_moved, f_send, f_recv,
    local_sems, c_ssem, c_rsem, m_ssem, m_rsem, h_ssem, h_rsem, x_ssem, x_rsem, z_ssem, z_rsem,
    y_ssem, y_rsem, w_ssem, w_rsem, b1_ssem, b1_rsem, b2_ssem, b2_rsem, f_ssem, f_rsem,
):
    ws = (w_first, w_second)
    b1s = (b1_first, b1_second)
    b2s = (b2_first, b2_second)
    s = lax.axis_index("sector")
    q = lax.axis_index("axial")
    y = s // NZ
    z = s % NZ

    def x_peer(k):
        return (s, (q + k) % NAX)

    def y_peer(k):
        return (((y + k) % NY) * NZ + z, q)

    def z_peer(k):
        return (y * NZ + (z + k) % NZ, q)

    def s_peer(k):
        return ((s + k) % NSEC, q)

    def wait_for(ref, sem):
        pltpu.make_async_copy(ref, ref, sem).wait()

    def remote(src, dst, ssem, rsem, device):
        pltpu.make_async_remote_copy(
            src_ref=src, dst_ref=dst, send_sem=ssem, recv_sem=rsem,
            device_id=device, device_id_type=MESH,
        ).start()

    loads = [
        pltpu.make_async_copy(src, dst, local_sems.at[i])
        for i, (src, dst) in enumerate(
            ((rhs_hbm, rhs_ref), (basis_hbm, basis_ref), (mass_hbm, mass_ref), (bw_hbm, bw_ref))
        )
    ]
    for load in loads:
        load.start()

    barrier = pltpu.get_barrier_semaphore()
    for k in FAR_FIRST:
        for peer in (y_peer(k), z_peer(k), x_peer(k)):
            pl.semaphore_signal(barrier, inc=1, device_id=peer, device_id_type=MESH)
    for k in (1, NSEC - 1):
        pl.semaphore_signal(barrier, inc=1, device_id=s_peer(k), device_id_type=MESH)

    solver_copy = pltpu.make_async_copy(solver_hbm.at[0], solver, local_sems.at[4])
    solver_copy.start()

    def inverse_for(to):
        return inverse_hbm.at[:, pl.ds(pl.multiple_of(to * NZ * GS, NZ * GS), NZ * GS)]

    own_copy = pltpu.make_async_copy(inverse_for(y), inverse_y.at[y], local_sems.at[5])
    own_copy.start()

    lane = lax.broadcasted_iota(jnp.int32, (R, GS), 1)
    lane8 = lax.broadcasted_iota(jnp.int32, (8, GS), 1)
    rows128 = lax.broadcasted_iota(jnp.int32, (8 * NV, GS), 0) // NV
    for load in loads:
        load.wait()
    rhs = rhs_ref[...]
    r0 = [rhs[:, a, :] for a in range(GA)]
    basis_all = basis_ref[...].astype(F32)
    basis = [basis_all[:, a, :] for a in range(GA)]
    mass = [mass_ref[a : a + 1, :] + 4.0 for a in range(GA)]
    weight = bw_ref[...]
    shift = shift_ref[0]
    shift_z = shift % NZ
    up = (shift // NZ + jnp.where(z < shift_z, 1, 0)) % NY
    up_there = (shift // NZ + jnp.where(z + shift_z >= NZ, 1, 0)) % NY

    def spread(tile, at):
        return jnp.where(rows128 == at, jnp.concatenate([tile] * 8, axis=0), 0.0).astype(BF16)

    basis_q = jnp.concatenate([spread(t, q) for t in basis], axis=1)
    basis_y = jnp.concatenate([spread(t, y) for t in basis], axis=1)

    def coarse_of(field):
        return joined(nt(two_parts(jnp.concatenate(field, axis=1)), basis_q))

    def edges(field):
        tile = jnp.zeros((R, GS), F32)
        for a in range(GA):
            at = 2 * (a + 1)
            moved = pltpu.roll(field[a], at + 1, 1)
            tile = jnp.where((lane == at) | (lane == at + 1), moved, tile)
        return tile

    def send_halo(n, field):
        h_send[n, 0] = edges(field)
        h_send[n, 1] = field[0]
        h_send[n, 2] = field[GA - 1]
        remote(h_send.at[n, 0], h_recv.at[n, 0], h_ssem.at[n], h_rsem.at[n], s_peer(1))
        remote(h_send.at[n, 0], h_recv.at[n, 1], h_ssem.at[n], h_rsem.at[n], s_peer(NSEC - 1))
        remote(h_send.at[n, 2], h_recv.at[n, 2], h_ssem.at[n], h_rsem.at[n], x_peer(1))
        remote(h_send.at[n, 1], h_recv.at[n, 3], h_ssem.at[n], h_rsem.at[n], x_peer(NAX - 1))

    def get_halo(n):
        wait_for(h_recv.at[n], h_rsem.at[n])
        above = jnp.where(q == 0, 0.0, h_recv[n, 2])
        below = jnp.where(q == NAX - 1, 0.0, h_recv[n, 3])
        return h_recv[n, 0], h_recv[n, 1], above, below

    def local_solve(field, halo):
        left, right, above, below = halo
        stack = [above] + field + [below]
        moved = [pltpu.roll(stack[j], 2 * j + 1, 1) for j in range(GA + 2)]
        zero = jnp.zeros((R, GS), F32)
        parts = []
        for t in range(GA + 3):
            here = moved[t] if t < GA + 2 else zero
            before = moved[t - 1] if t > 0 else zero
            tile = jnp.where(lane == 2 * t - 1, right, before)
            tile = jnp.where(lane == 2 * t, left, tile)
            parts.append(jnp.where(lane > 2 * t, here, tile))
        window = jnp.concatenate(parts, axis=1)
        out = joined(nn(two_parts(window)[:, :NEXT], solver[...]))
        return [out[:, a * GS : (a + 1) * GS] for a in range(GA)]

    def apply_operator(field, halo, band):
        left, right, above, below = halo
        stack = [above] + field + [below]
        image = []
        for a in range(GA):
            u = field[a]
            before = jnp.where(lane == 0, pltpu.roll(left, GS - 2 * (a + 1), 1), pltpu.roll(u, 1, 1))
            after = jnp.where(
                lane == GS - 1, pltpu.roll(right, GS - 1 - (2 * a + 3), 1), pltpu.roll(u, GS - 1, 1)
            )
            value = mass[a] * u - ((stack[a + 2] + stack[a]) + before + after)
            if a == 0:
                value = value + weight * (u - band)
            image.append(value)
        return image

    def send_band(n, rows):
        b1s[n][0] = rows
        for k in FAR_FIRST:
            remote(b1s[n].at[0], b1s[n].at[k], b1_ssem.at[n], b1_rsem.at[n], y_peer(k))

    def forward_band(n):
        wait_for(b1s[n].at[pl.ds(1, NY - 1)], b1_rsem.at[n])
        b2s[n][0, pl.ds(0, R)] = b1s[n][up_there]
        if n == 0:
            wait_for(basis_moved.at[pl.ds(1, NY - 1)], c_rsem)
            b2s[n][0, pl.ds(R, R)] = basis_moved[up_there].astype(F32)
        for k in FAR_FIRST:
            remote(b2s[n].at[0], b2s[n].at[k], b2_ssem.at[n], b2_rsem.at[n], z_peer(k))

    def get_band(n):
        wait_for(b2s[n].at[pl.ds(1, NZ - 1)], b2_rsem.at[n])
        return b2s[n][shift_z]

    def rows_of(n):
        return pl.ds(0, R if n == 0 else XROWS)

    def send_x(n, coarse, inner):
        x_send[n, pl.ds(0, R)] = coarse
        if inner is not None:
            x_send[n, pl.ds(R, 8)] = inner
        for k in FAR_FIRST:
            remote(
                x_send.at[n, rows_of(n)], x_recv.at[n, k - 1, rows_of(n)],
                x_ssem.at[n], x_rsem.at[n], x_peer(k),
            )

    def pass_z(n):
        wait_for(x_recv.at[n, :, rows_of(n)], x_rsem.at[n])
        total = x_send[n, rows_of(n)]
        for k in range(NAX - 1):
            total = total + x_recv[n, k, rows_of(n)]
        z_tiles[n, z, rows_of(n)] = total
        for k in FAR_FIRST:
            remote(
                z_tiles.at[n, z, rows_of(n)], z_tiles.at[n, z, rows_of(n)],
                z_ssem.at[n], z_rsem.at[n], z_peer(k),
            )

    def pass_y(n):
        wait_for(z_tiles.at[n, pl.ds(0, NZ - 1), rows_of(n)], z_rsem.at[n])
        gathered = jnp.concatenate([z_tiles[n, t, pl.ds(0, R)] for t in range(NZ)], axis=1)
        if n == 0:
            own_copy.wait()
            wait_for(inverse_y.at[pl.ds(0, NY - 1)], m_rsem)
        matrix = jnp.concatenate([inverse_y[t] for t in range(NY)], axis=0)
        y_send[n, pl.ds(0, R)] = joined(nt(two_parts(gathered), matrix))
        if n > 0:
            inner = z_tiles[n, 0, pl.ds(R, 8)]
            for t in range(1, NZ):
                inner = inner + z_tiles[n, t, pl.ds(R, 8)]
            y_send[n, pl.ds(R, 8)] = inner
        for k in FAR_FIRST:
            remote(
                y_send.at[n, rows_of(n)], y_recv.at[n, k - 1, rows_of(n)],
                y_ssem.at[n], y_rsem.at[n], y_peer(k),
            )

    def get_y(n):
        wait_for(y_recv.at[n, :, rows_of(n)], y_rsem.at[n])
        total = y_send[n, rows_of(n)]
        for k in range(NY - 1):
            total = total + y_recv[n, k, rows_of(n)]
        return total[:R], total[R:]

    def send_coarse(n, tile):
        ws[n][0] = tile
        for k in FAR_FIRST:
            remote(ws[n].at[0], ws[n].at[k], w_ssem.at[n], w_rsem.at[n], z_peer(k))

    def get_coarse(n):
        wait_for(ws[n].at[pl.ds(1, NZ - 1)], w_rsem.at[n])
        return ws[n][shift_z]

    def prolong(coarse, rows):
        out = joined(nn(two_parts(coarse), rows))
        return [out[:, i * GS : (i + 1) * GS] for i in range(rows.shape[1] // GS)]

    def inner_products(residual, image):
        cross = residual[0] * image[0]
        square = image[0] * image[0]
        for a in range(1, GA):
            cross = cross + residual[a] * image[a]
            square = square + image[a] * image[a]
        cross = jnp.sum(cross, axis=1, keepdims=True)
        square = jnp.sum(square, axis=1, keepdims=True)
        tile = jnp.zeros((8, GS), F32)
        for i, column in enumerate((cross[:8], square[:8], cross[8:], square[8:])):
            tile = jnp.where(lane8 == i, column, tile)
        return tile

    def step_of(inner):
        cross = jnp.concatenate([inner[:, 0:1], inner[:, 2:3]], axis=0)
        square = jnp.concatenate([inner[:, 1:2], inner[:, 3:4]], axis=0)
        return cross / (square + EPSILON)

    coarse_r0 = coarse_of(r0)

    pl.semaphore_wait(barrier, 7 + 7 + 7 + 2)

    send_x(0, coarse_r0, None)
    basis_moved[0] = basis[0].astype(BF16)
    for k in FAR_FIRST:
        remote(basis_moved.at[0], basis_moved.at[k], c_ssem, c_rsem, y_peer(k))
    send_halo(0, r0)
    for k in FAR_FIRST:
        remote(inverse_for((y + k) % NY), inverse_y.at[y], m_ssem, m_rsem, y_peer(k))
    pass_z(0)
    halo_r0 = get_halo(0)
    solver_copy.wait()
    local_r0 = local_solve(r0, halo_r0)
    send_band(0, local_r0[0])
    pass_y(0)
    forward_band(0)
    coarse, _ = get_y(0)
    send_coarse(0, coarse)
    corr0 = [u + v for u, v in zip(local_r0, prolong(coarse, basis_y))]
    send_halo(1, corr0)
    band_rows = get_band(0)
    band_basis = spread(band_rows[R:], (y + NY - up) % NY)
    band_corr0 = band_rows[:R] + prolong(get_coarse(0), band_basis)[0]
    image0 = apply_operator(corr0, get_halo(1), band_corr0)

    send_x(1, coarse_of(image0), inner_products(r0, image0))
    send_halo(2, image0)
    pass_z(1)
    local_im = local_solve(image0, get_halo(2))
    send_band(1, local_im[0])
    pass_y(1)
    forward_band(1)
    coarse, inner = get_y(1)
    send_coarse(1, coarse)
    diff = [u + v for u, v in zip(local_im, prolong(coarse, basis_y))]
    send_halo(3, diff)
    step0 = step_of(inner)
    corr1 = [u - step0 * v for u, v in zip(corr0, diff)]
    res1 = [u - step0 * v for u, v in zip(r0, image0)]
    band_row = get_band(1)
    band_diff = band_row + prolong(get_coarse(1), band_basis)[0]
    image_diff = apply_operator(diff, get_halo(3), band_diff)
    image1 = [u - step0 * v for u, v in zip(image0, image_diff)]

    inner = inner_products(res1, image1)
    for i, peer in enumerate((x_peer, y_peer, z_peer)):
        f_send[i] = inner
        for k in FAR_FIRST:
            remote(f_send.at[i], f_recv.at[i, k - 1], f_ssem.at[i], f_rsem.at[i], peer(k))
        wait_for(f_recv.at[i], f_rsem.at[i])
        for k in range(7):
            inner = inner + f_recv[i, k]
    step1 = step_of(inner)
    for a in range(GA):
        sol_ref[:, a, :] = step0 * corr0[a] + step1 * corr1[a]
        res_ref[:, a, :] = res1[a] - step1 * image1[a]

    wait_for(inverse_y.at[pl.ds(0, NY - 1)], m_ssem)
    wait_for(basis_moved.at[pl.ds(1, NY - 1)], c_ssem)
    for n in range(4):
        wait_for(h_recv.at[n], h_ssem.at[n])
    for n in range(2):
        wait_for(x_recv.at[n, :, rows_of(n)], x_ssem.at[n])
        wait_for(z_tiles.at[n, pl.ds(0, NZ - 1), rows_of(n)], z_ssem.at[n])
        wait_for(y_recv.at[n, :, rows_of(n)], y_ssem.at[n])
        wait_for(ws[n].at[pl.ds(1, NZ - 1)], w_ssem.at[n])
        wait_for(b1s[n].at[pl.ds(1, NY - 1)], b1_ssem.at[n])
        wait_for(b2s[n].at[pl.ds(1, NZ - 1)], b2_ssem.at[n])
    for i in range(3):
        wait_for(f_recv.at[i], f_ssem.at[i])


def on_device(
    right_side, mass_term, band_weight, band_shift, local_solver, coarse_inverse, coarse_basis
):
    vmem = pl.BlockSpec(memory_space=pltpu.VMEM)
    smem = pl.BlockSpec(memory_space=pltpu.SMEM)
    hbm = pl.BlockSpec(memory_space=pltpu.HBM)
    dma = pltpu.SemaphoreType.DMA
    out = jax.ShapeDtypeStruct(right_side.shape, F32)

    def tiles(*shape):
        return pltpu.VMEM(shape + (GS,), F32)

    return pl.pallas_call(
        body,
        name="schwarz_steps",
        out_shape=(out, out),
        in_specs=[hbm, hbm, hbm, smem, hbm, hbm, hbm],
        out_specs=(vmem, vmem),
        scratch_shapes=[
            pltpu.VMEM(right_side.shape, F32),
            pltpu.VMEM(mass_term.shape, F32),
            pltpu.VMEM(band_weight.shape, F32),
            pltpu.VMEM(coarse_basis.shape, BF16),
            pltpu.VMEM((NEXT, GA * GS), BF16),
            pltpu.VMEM((NY, NV, NZ * GS), BF16),
            tiles(4, 3, R),
            tiles(4, 4, R),
            tiles(2, XROWS),
            tiles(2, NAX - 1, XROWS),
            tiles(2, NZ, XROWS),
            tiles(2, XROWS),
            tiles(2, NY - 1, XROWS),
            tiles(NZ, R),
            tiles(NZ, R),
            tiles(NY, R),
            tiles(NY, R),
            tiles(NZ, 2 * R),
            tiles(NZ, R),
            pltpu.VMEM((NY, NV, GS), BF16),
            tiles(3, 8),
            tiles(3, 7, 8),
            dma((6,)),
            dma,
            dma,
            dma,
            dma,
            dma((4,)),
            dma((4,)),
        ]
        + [dma((2,))] * 12
        + [dma((3,))] * 2,
        compiler_params=pltpu.CompilerParams(
            collective_id=0, has_side_effects=True, vmem_limit_bytes=60 << 20
        ),
    )(
        right_side, mass_term, band_weight, band_shift, coarse_basis,
        jnp.swapaxes(local_solver, 1, 2), coarse_inverse,
    )


def solution(mesh):
    placed = (
        P(None, "axial", "sector"),
        P("axial", "sector"),
        P("axial", "sector"),
        P(),
        P("axial", "sector", None),
        P(("sector", "axial"), None),
        P(None, "axial", "sector"),
    )
    return jax.shard_map(
        on_device,
        mesh=mesh,
        in_specs=placed,
        out_specs=(P(None, "axial", "sector"), P(None, "axial", "sector")),
        check_vma=False,
    )
```

```python
import jax
import jax.numpy as jnp
from jax import lax
from jax.experimental import pallas as pl
from jax.experimental.pallas import tpu as pltpu
from jax.sharding import PartitionSpec as P

EPSILON = 1e-06
MESH = pl.DeviceIdType.MESH
F32 = jnp.float32
BF16 = jnp.bfloat16

R = 16
GA = 4
GS = 128
NV = 16
NEXT = 780
NZ = 8
NY = 8
NSEC = NY * NZ
NAX = 8
FAR_FIRST = (4, 3, 5, 2, 6, 1, 7)


def nt(a, b):
    return lax.dot_general(a, b, (((1,), (1,)), ((), ())), preferred_element_type=F32)


def nn(a, b):
    return lax.dot_general(a, b, (((1,), (0,)), ((), ())), preferred_element_type=F32)


def two_parts(x):
    high = x.astype(BF16)
    low = (x - high.astype(F32)).astype(BF16)
    return jnp.concatenate([high, low], axis=0)


def joined(x):
    half = x.shape[0] // 2
    return x[:half] + x[half:]


def body(
    rhs_hbm, mass_hbm, bw_hbm, shift_ref, basis_hbm, solver_hbm, inverse_hbm,
    out_ref,
    rhs_ref, mass_ref, bw_ref, basis_ref,
    solver, inverse_y, h_send, h_recv, x_send, x_recv, z_tiles, y_send, y_recv,
    w_first, w_second, b1_first, b1_second, b2_first, b2_second, basis_moved, f_rows, e_rows,
    local_sems, c_ssem, c_rsem, m_ssem, m_rsem, h_ssem, h_rsem, x_ssem, x_rsem, z_ssem, z_rsem,
    y_ssem, y_rsem, w_ssem, w_rsem, b1_ssem, b1_rsem, b2_ssem, b2_rsem, f_ssem, f_rsem, e_ssem, e_rsem,
):
    ws = (w_first, w_second)
    b1s = (b1_first, b1_second)
    b2s = (b2_first, b2_second)
    s = lax.axis_index("sector")
    q = lax.axis_index("axial")
    y = s // NZ
    z = s % NZ

    def x_peer(k):
        return (s, (q + k) % NAX)

    def y_peer(k):
        return (((y + k) % NY) * NZ + z, q)

    def z_peer(k):
        return (y * NZ + (z + k) % NZ, q)

    def s_peer(k):
        return ((s + k) % NSEC, q)

    def wait_for(ref, sem):
        pltpu.make_async_copy(ref, ref, sem).wait()

    def remote(src, dst, ssem, rsem, device):
        pltpu.make_async_remote_copy(
            src_ref=src, dst_ref=dst, send_sem=ssem, recv_sem=rsem,
            device_id=device, device_id_type=MESH,
        ).start()

    loads = [
        pltpu.make_async_copy(src, dst, local_sems.at[i])
        for i, (src, dst) in enumerate(
            ((rhs_hbm, rhs_ref), (basis_hbm, basis_ref), (mass_hbm, mass_ref), (bw_hbm, bw_ref))
        )
    ]
    for load in loads:
        load.start()

    barrier = pltpu.get_barrier_semaphore()
    for k in FAR_FIRST:
        for peer in (y_peer(k), z_peer(k), x_peer(k)):
            pl.semaphore_signal(barrier, inc=1, device_id=peer, device_id_type=MESH)
    for k in (1, NSEC - 1):
        pl.semaphore_signal(barrier, inc=1, device_id=s_peer(k), device_id_type=MESH)

    solver_copy = pltpu.make_async_copy(solver_hbm.at[0], solver, local_sems.at[4])
    solver_copy.start()

    def inverse_for(to):
        return inverse_hbm.at[:, pl.ds(pl.multiple_of(to * NZ * GS, NZ * GS), NZ * GS)]

    own_copy = pltpu.make_async_copy(inverse_for(y), inverse_y.at[y], local_sems.at[5])
    own_copy.start()

    lane = lax.broadcasted_iota(jnp.int32, (R, GS), 1)
    rotor = lax.broadcasted_iota(jnp.int32, (R, GS), 0)
    rows128 = lax.broadcasted_iota(jnp.int32, (8 * NV, GS), 0) // NV
    for load in loads:
        load.wait()
    rhs = rhs_ref[...]
    r0 = [rhs[:, a, :] for a in range(GA)]
    basis_all = basis_ref[...].astype(F32)
    basis = [basis_all[:, a, :] for a in range(GA)]
    mass = [mass_ref[a : a + 1, :] + 4.0 for a in range(GA)]
    weight = bw_ref[...]
    shift = shift_ref[0]
    shift_z = shift % NZ
    up = (shift // NZ + jnp.where(z < shift_z, 1, 0)) % NY
    up_there = (shift // NZ + jnp.where(z + shift_z >= NZ, 1, 0)) % NY

    def spread(tile, at):
        return jnp.where(rows128 == at, jnp.concatenate([tile] * 8, axis=0), 0.0).astype(BF16)

    basis_q = jnp.concatenate([spread(t, q) for t in basis], axis=1)
    basis_y = jnp.concatenate([spread(t, y) for t in basis], axis=1)

    def coarse_of(field):
        return joined(nt(two_parts(jnp.concatenate(field, axis=1)), basis_q))

    def edges(field):
        tile = jnp.zeros((R, GS), F32)
        for a in range(GA):
            at = 2 * (a + 1)
            moved = pltpu.roll(field[a], at + 1, 1)
            tile = jnp.where((lane == at) | (lane == at + 1), moved, tile)
        return tile

    def send_halo(n, field):
        h_send[n, 0] = edges(field)
        h_send[n, 1] = field[0]
        h_send[n, 2] = field[GA - 1]
        remote(h_send.at[n, 0], h_recv.at[n, 0], h_ssem.at[n], h_rsem.at[n], s_peer(1))
        remote(h_send.at[n, 0], h_recv.at[n, 1], h_ssem.at[n], h_rsem.at[n], s_peer(NSEC - 1))
        remote(h_send.at[n, 2], h_recv.at[n, 2], h_ssem.at[n], h_rsem.at[n], x_peer(1))
        remote(h_send.at[n, 1], h_recv.at[n, 3], h_ssem.at[n], h_rsem.at[n], x_peer(NAX - 1))

    def get_halo(n):
        wait_for(h_recv.at[n], h_rsem.at[n])
        above = jnp.where(q == 0, 0.0, h_recv[n, 2])
        below = jnp.where(q == NAX - 1, 0.0, h_recv[n, 3])
        return h_recv[n, 0], h_recv[n, 1], above, below

    def local_solve(field, halo):
        left, right, above, below = halo
        stack = [above] + field + [below]
        moved = [pltpu.roll(stack[j], 2 * j + 1, 1) for j in range(GA + 2)]
        zero = jnp.zeros((R, GS), F32)
        parts = []
        for t in range(GA + 3):
            here = moved[t] if t < GA + 2 else zero
            before = moved[t - 1] if t > 0 else zero
            tile = jnp.where(lane == 2 * t - 1, right, before)
            tile = jnp.where(lane == 2 * t, left, tile)
            parts.append(jnp.where(lane > 2 * t, here, tile))
        window = jnp.concatenate(parts, axis=1)
        out = joined(nn(two_parts(window)[:, :NEXT], solver[...]))
        return [out[:, a * GS : (a + 1) * GS] for a in range(GA)]

    def apply_operator(field, halo, band):
        left, right, above, below = halo
        stack = [above] + field + [below]
        image = []
        for a in range(GA):
            u = field[a]
            before = jnp.where(lane == 0, pltpu.roll(left, GS - 2 * (a + 1), 1), pltpu.roll(u, 1, 1))
            after = jnp.where(
                lane == GS - 1, pltpu.roll(right, GS - 1 - (2 * a + 3), 1), pltpu.roll(u, GS - 1, 1)
            )
            value = mass[a] * u - ((stack[a + 2] + stack[a]) + before + after)
            if a == 0:
                value = value + weight * (u - band)
            image.append(value)
        return image

    def send_band(n, rows):
        b1s[n][0] = rows
        for k in FAR_FIRST:
            remote(b1s[n].at[0], b1s[n].at[k], b1_ssem.at[n], b1_rsem.at[n], y_peer(k))

    def forward_band(n):
        wait_for(b1s[n].at[pl.ds(1, NY - 1)], b1_rsem.at[n])
        b2s[n][0, pl.ds(0, R)] = b1s[n][up_there]
        if n == 0:
            wait_for(basis_moved.at[pl.ds(1, NY - 1)], c_rsem)
            b2s[n][0, pl.ds(R, R)] = basis_moved[up_there].astype(F32)
        for k in FAR_FIRST:
            remote(b2s[n].at[0], b2s[n].at[k], b2_ssem.at[n], b2_rsem.at[n], z_peer(k))

    def get_band(n):
        wait_for(b2s[n].at[pl.ds(1, NZ - 1)], b2_rsem.at[n])
        return b2s[n][shift_z]

    def send_x(n, coarse):
        x_send[n] = coarse
        for k in FAR_FIRST:
            remote(x_send.at[n], x_recv.at[n, k - 1], x_ssem.at[n], x_rsem.at[n], x_peer(k))

    def pass_z(n):
        wait_for(x_recv.at[n], x_rsem.at[n])
        total = x_send[n]
        for k in range(NAX - 1):
            total = total + x_recv[n, k]
        z_tiles[n, z] = total
        for k in FAR_FIRST:
            remote(z_tiles.at[n, z], z_tiles.at[n, z], z_ssem.at[n], z_rsem.at[n], z_peer(k))

    def pass_y(n):
        wait_for(z_tiles.at[n, pl.ds(0, NZ - 1)], z_rsem.at[n])
        gathered = jnp.concatenate([z_tiles[n, t] for t in range(NZ)], axis=1)
        if n == 0:
            own_copy.wait()
            wait_for(inverse_y.at[pl.ds(0, NY - 1)], m_rsem)
        matrix = jnp.concatenate([inverse_y[t] for t in range(NY)], axis=0)
        y_send[n] = joined(nt(two_parts(gathered), matrix))
        for k in FAR_FIRST:
            remote(y_send.at[n], y_recv.at[n, k - 1], y_ssem.at[n], y_rsem.at[n], y_peer(k))

    def get_y(n):
        wait_for(y_recv.at[n], y_rsem.at[n])
        total = y_send[n]
        for k in range(NY - 1):
            total = total + y_recv[n, k]
        return total

    def send_coarse(n, tile):
        ws[n][0] = tile
        for k in FAR_FIRST:
            remote(ws[n].at[0], ws[n].at[k], w_ssem.at[n], w_rsem.at[n], z_peer(k))

    def get_coarse(n):
        wait_for(ws[n].at[pl.ds(1, NZ - 1)], w_rsem.at[n])
        return ws[n][shift_z]

    def prolong(coarse, rows):
        out = joined(nn(two_parts(coarse), rows))
        return [out[:, i * GS : (i + 1) * GS] for i in range(rows.shape[1] // GS)]

    def inner_products(residual, image):
        cross = residual[0] * image[0]
        square = image[0] * image[0]
        for a in range(1, GA):
            cross = cross + residual[a] * image[a]
            square = square + image[a] * image[a]
        cross = jnp.sum(cross, axis=1, keepdims=True)
        square = jnp.sum(square, axis=1, keepdims=True)
        spread_out = jnp.where(lane == rotor, cross, jnp.where(lane == rotor + R, square, 0.0))
        return jnp.sum(spread_out, axis=0, keepdims=True)

    def send_inner(n, row):
        f_rows[n, pl.ds(NAX - 1, 1)] = row
        for k in FAR_FIRST:
            remote(
                f_rows.at[n, pl.ds(NAX - 1, 1)], f_rows.at[n, pl.ds(k - 1, 1)],
                f_ssem.at[n], f_rsem.at[n], x_peer(k),
            )

    def pass_inner(n):
        wait_for(f_rows.at[n, pl.ds(0, NAX - 1)], f_rsem.at[n])
        e_rows[n, pl.ds(NSEC - 1, 1)] = jnp.sum(f_rows[n], axis=0, keepdims=True)

        def give(j, carry):
            k = (j * 27) % NSEC
            remote(
                e_rows.at[n, pl.ds(NSEC - 1, 1)], e_rows.at[n, pl.ds(k - 1, 1)],
                e_ssem.at[n], e_rsem.at[n], s_peer(k),
            )
            return carry

        lax.fori_loop(1, NSEC, give, 0)

    def get_step(n):
        wait_for(e_rows.at[n, pl.ds(0, NSEC - 1)], e_rsem.at[n])
        row = jnp.sum(e_rows[n], axis=0, keepdims=True)
        cross = jnp.sum(jnp.where(lane == rotor, row, 0.0), axis=1, keepdims=True)
        square = jnp.sum(jnp.where(lane == rotor + R, row, 0.0), axis=1, keepdims=True)
        return cross / (square + EPSILON)

    coarse_r0 = coarse_of(r0)

    pl.semaphore_wait(barrier, 7 + 7 + 7 + 2)

    send_x(0, coarse_r0)
    for k in FAR_FIRST:
        remote(inverse_for((y + k) % NY), inverse_y.at[y], m_ssem, m_rsem, y_peer(k))
    send_halo(0, r0)
    basis_moved[0] = basis[0].astype(BF16)
    for k in FAR_FIRST:
        remote(basis_moved.at[0], basis_moved.at[k], c_ssem, c_rsem, y_peer(k))
    pass_z(0)
    halo_r0 = get_halo(0)
    solver_copy.wait()
    local_r0 = local_solve(r0, halo_r0)
    send_band(0, local_r0[0])
    pass_y(0)
    forward_band(0)
    coarse = get_y(0)
    send_coarse(0, coarse)
    corr0 = [u + v for u, v in zip(local_r0, prolong(coarse, basis_y))]
    send_halo(1, corr0)
    band_rows = get_band(0)
    band_basis = spread(band_rows[R:], (y + NY - up) % NY)
    band_corr0 = band_rows[:R] + prolong(get_coarse(0), band_basis)[0]
    image0 = apply_operator(corr0, get_halo(1), band_corr0)

    send_x(1, coarse_of(image0))
    send_halo(2, image0)
    send_inner(0, inner_products(r0, image0))
    pass_z(1)
    local_im = local_solve(image0, get_halo(2))
    send_band(1, local_im[0])
    pass_inner(0)
    pass_y(1)
    forward_band(1)
    coarse = get_y(1)
    send_coarse(1, coarse)
    diff = [u + v for u, v in zip(local_im, prolong(coarse, basis_y))]
    send_halo(3, diff)
    step0 = get_step(0)
    corr1 = [u - step0 * v for u, v in zip(corr0, diff)]
    res1 = [u - step0 * v for u, v in zip(r0, image0)]
    band_row = get_band(1)
    band_diff = band_row + prolong(get_coarse(1), band_basis)[0]
    image_diff = apply_operator(diff, get_halo(3), band_diff)
    image1 = [u - step0 * v for u, v in zip(image0, image_diff)]

    send_inner(1, inner_products(res1, image1))
    pass_inner(1)
    step1 = get_step(1)
    for a in range(GA):
        out_ref[0, :, a, :] = step0 * corr0[a] + step1 * corr1[a]
        out_ref[1, :, a, :] = res1[a] - step1 * image1[a]

    wait_for(inverse_y.at[pl.ds(0, NY - 1)], m_ssem)
    wait_for(basis_moved.at[pl.ds(1, NY - 1)], c_ssem)
    for n in range(4):
        wait_for(h_recv.at[n], h_ssem.at[n])
    for n in range(2):
        wait_for(x_recv.at[n], x_ssem.at[n])
        wait_for(z_tiles.at[n, pl.ds(0, NZ - 1)], z_ssem.at[n])
        wait_for(y_recv.at[n], y_ssem.at[n])
        wait_for(ws[n].at[pl.ds(1, NZ - 1)], w_ssem.at[n])
        wait_for(b1s[n].at[pl.ds(1, NY - 1)], b1_ssem.at[n])
        wait_for(b2s[n].at[pl.ds(1, NZ - 1)], b2_ssem.at[n])
        wait_for(f_rows.at[n, pl.ds(0, NAX - 1)], f_ssem.at[n])
        wait_for(e_rows.at[n, pl.ds(0, NSEC - 1)], e_ssem.at[n])


def on_device(
    right_side, mass_term, band_weight, band_shift, local_solver, coarse_inverse, coarse_basis
):
    hbm = pl.BlockSpec(memory_space=pltpu.HBM)
    dma = pltpu.SemaphoreType.DMA

    def tiles(*shape):
        return pltpu.VMEM(shape + (GS,), F32)

    both = pl.pallas_call(
        body,
        name="schwarz_steps",
        out_shape=pltpu.VMEM((2,) + right_side.shape, F32),
        in_specs=[hbm, hbm, hbm, pl.BlockSpec(memory_space=pltpu.SMEM), hbm, hbm, hbm],
        out_specs=pl.BlockSpec(memory_space=pltpu.VMEM),
        scratch_shapes=[
            pltpu.VMEM(right_side.shape, F32),
            pltpu.VMEM(mass_term.shape, F32),
            pltpu.VMEM(band_weight.shape, F32),
            pltpu.VMEM(coarse_basis.shape, BF16),
            pltpu.VMEM((NEXT, GA * GS), BF16),
            pltpu.VMEM((NY, NV, NZ * GS), BF16),
            tiles(4, 3, R),
            tiles(4, 4, R),
            tiles(2, R),
            tiles(2, NAX - 1, R),
            tiles(2, NZ, R),
            tiles(2, R),
            tiles(2, NY - 1, R),
            tiles(NZ, R),
            tiles(NZ, R),
            tiles(NY, R),
            tiles(NY, R),
            tiles(NZ, 2 * R),
            tiles(NZ, R),
            pltpu.VMEM((NY, NV, GS), BF16),
            tiles(2, NAX),
            tiles(2, NSEC),
            dma((6,)),
            dma,
            dma,
            dma,
            dma,
            dma((4,)),
            dma((4,)),
        ]
        + [dma((2,))] * 16,
        compiler_params=pltpu.CompilerParams(
            collective_id=0, has_side_effects=True, vmem_limit_bytes=60 << 20
        ),
    )(
        right_side, mass_term, band_weight, band_shift, coarse_basis,
        jnp.swapaxes(local_solver, 1, 2), coarse_inverse,
    )
    return both[0], both[1]


def solution(mesh):
    placed = (
        P(None, "axial", "sector"),
        P("axial", "sector"),
        P("axial", "sector"),
        P(),
        P("axial", "sector", None),
        P(("sector", "axial"), None),
        P(None, "axial", "sector"),
    )
    return jax.shard_map(
        on_device,
        mesh=mesh,
        in_specs=placed,
        out_specs=(P(None, "axial", "sector"), P(None, "axial", "sector")),
        check_vma=False,
    )
```

```python
import jax
import jax.numpy as jnp
from jax import lax
from jax.experimental import pallas as pl
from jax.experimental.pallas import tpu as pltpu
from jax.sharding import PartitionSpec as P

EPSILON = 1e-06
MESH = pl.DeviceIdType.MESH
F32 = jnp.float32
BF16 = jnp.bfloat16

R = 16
GA = 4
GS = 128
NV = 16
NEXT = 780
NZ = 8
NY = 8
NSEC = NY * NZ
NAX = 8
FAR_FIRST = (4, 3, 5, 2, 6, 1, 7)


def nt(a, b):
    return lax.dot_general(a, b, (((1,), (1,)), ((), ())), preferred_element_type=F32)


def nn(a, b):
    return lax.dot_general(a, b, (((1,), (0,)), ((), ())), preferred_element_type=F32)


def two_parts(x):
    high = x.astype(BF16)
    low = (x - high.astype(F32)).astype(BF16)
    return jnp.concatenate([high, low], axis=0)


def joined(x):
    half = x.shape[0] // 2
    return x[:half] + x[half:]


def body(
    rhs_hbm, mass_hbm, bw_hbm, shift_ref, basis_hbm, solver_hbm, inverse_hbm,
    out_ref,
    rhs_ref, mass_ref, bw_ref, basis_ref,
    solver, inverse_y, h_send, h_recv, x_send, x_recv, z_tiles, y_send, y_recv,
    w_first, w_second, b1_first, b1_second, b2_first, b2_second, c1, c2, f_rows, e_rows,
    local_sems, c1_ssem, c1_rsem, c2_ssem, c2_rsem, m_ssem, m_rsem, h_ssem, h_rsem, x_ssem, x_rsem, z_ssem, z_rsem,
    y_ssem, y_rsem, w_ssem, w_rsem, b1_ssem, b1_rsem, b2_ssem, b2_rsem, f_ssem, f_rsem, e_ssem, e_rsem,
):
    ws = (w_first, w_second)
    b1s = (b1_first, b1_second)
    b2s = (b2_first, b2_second)
    s = lax.axis_index("sector")
    q = lax.axis_index("axial")
    y = s // NZ
    z = s % NZ

    def x_peer(k):
        return (s, (q + k) % NAX)

    def y_peer(k):
        return (((y + k) % NY) * NZ + z, q)

    def z_peer(k):
        return (y * NZ + (z + k) % NZ, q)

    def s_peer(k):
        return ((s + k) % NSEC, q)

    def wait_for(ref, sem):
        pltpu.make_async_copy(ref, ref, sem).wait()

    def remote(src, dst, ssem, rsem, device):
        pltpu.make_async_remote_copy(
            src_ref=src, dst_ref=dst, send_sem=ssem, recv_sem=rsem,
            device_id=device, device_id_type=MESH,
        ).start()

    loads = [
        pltpu.make_async_copy(src, dst, local_sems.at[i])
        for i, (src, dst) in enumerate(
            ((rhs_hbm, rhs_ref), (basis_hbm, basis_ref), (mass_hbm, mass_ref), (bw_hbm, bw_ref))
        )
    ]
    for load in loads:
        load.start()

    barrier = pltpu.get_barrier_semaphore()
    for k in FAR_FIRST:
        for peer in (y_peer(k), z_peer(k), x_peer(k)):
            pl.semaphore_signal(barrier, inc=1, device_id=peer, device_id_type=MESH)
    for k in (1, NSEC - 1):
        pl.semaphore_signal(barrier, inc=1, device_id=s_peer(k), device_id_type=MESH)

    solver_copy = pltpu.make_async_copy(solver_hbm.at[0], solver, local_sems.at[4])
    solver_copy.start()

    def inverse_for(to):
        return inverse_hbm.at[:, pl.ds(pl.multiple_of(to * NZ * GS, NZ * GS), NZ * GS)]

    own_copy = pltpu.make_async_copy(inverse_for(y), inverse_y.at[y], local_sems.at[5])
    own_copy.start()

    lane = lax.broadcasted_iota(jnp.int32, (R, GS), 1)
    rotor = lax.broadcasted_iota(jnp.int32, (R, GS), 0)
    rows128 = lax.broadcasted_iota(jnp.int32, (8 * NV, GS), 0) // NV
    for load in loads:
        load.wait()
    rhs = rhs_ref[...]
    r0 = [rhs[:, a, :] for a in range(GA)]
    basis_all = basis_ref[...].astype(F32)
    basis = [basis_all[:, a, :] for a in range(GA)]
    mass = [mass_ref[a : a + 1, :] + 4.0 for a in range(GA)]
    weight = bw_ref[...]
    shift = shift_ref[0]
    shift_z = shift % NZ
    up = (shift // NZ + jnp.where(z < shift_z, 1, 0)) % NY
    up_there = (shift // NZ + jnp.where(z + shift_z >= NZ, 1, 0)) % NY

    def spread(tile, at):
        return jnp.where(rows128 == at, jnp.concatenate([tile] * 8, axis=0), 0.0).astype(BF16)

    basis_q = jnp.concatenate([spread(t, q) for t in basis], axis=1)
    basis_y = jnp.concatenate([spread(t, y) for t in basis], axis=1)

    def coarse_of(field):
        return joined(nt(two_parts(jnp.concatenate(field, axis=1)), basis_q))

    def edges(field):
        tile = jnp.zeros((R, GS), F32)
        for a in range(GA):
            at = 2 * (a + 1)
            moved = pltpu.roll(field[a], at + 1, 1)
            tile = jnp.where((lane == at) | (lane == at + 1), moved, tile)
        return tile

    def send_halo(n, field):
        h_send[n, 0] = edges(field)
        h_send[n, 1] = field[0]
        h_send[n, 2] = field[GA - 1]
        remote(h_send.at[n, 0], h_recv.at[n, 0], h_ssem.at[n], h_rsem.at[n], s_peer(1))
        remote(h_send.at[n, 0], h_recv.at[n, 1], h_ssem.at[n], h_rsem.at[n], s_peer(NSEC - 1))
        remote(h_send.at[n, 2], h_recv.at[n, 2], h_ssem.at[n], h_rsem.at[n], x_peer(1))
        remote(h_send.at[n, 1], h_recv.at[n, 3], h_ssem.at[n], h_rsem.at[n], x_peer(NAX - 1))

    def get_halo(n):
        wait_for(h_recv.at[n], h_rsem.at[n])
        above = jnp.where(q == 0, 0.0, h_recv[n, 2])
        below = jnp.where(q == NAX - 1, 0.0, h_recv[n, 3])
        return h_recv[n, 0], h_recv[n, 1], above, below

    def local_solve(field, halo):
        left, right, above, below = halo
        stack = [above] + field + [below]
        moved = [pltpu.roll(stack[j], 2 * j + 1, 1) for j in range(GA + 2)]
        zero = jnp.zeros((R, GS), F32)
        parts = []
        for t in range(GA + 3):
            here = moved[t] if t < GA + 2 else zero
            before = moved[t - 1] if t > 0 else zero
            tile = jnp.where(lane == 2 * t - 1, right, before)
            tile = jnp.where(lane == 2 * t, left, tile)
            parts.append(jnp.where(lane > 2 * t, here, tile))
        window = jnp.concatenate(parts, axis=1)
        out = joined(nn(two_parts(window)[:, :NEXT], solver[...]))
        return [out[:, a * GS : (a + 1) * GS] for a in range(GA)]

    def apply_operator(field, halo, band):
        left, right, above, below = halo
        stack = [above] + field + [below]
        image = []
        for a in range(GA):
            u = field[a]
            before = jnp.where(lane == 0, pltpu.roll(left, GS - 2 * (a + 1), 1), pltpu.roll(u, 1, 1))
            after = jnp.where(
                lane == GS - 1, pltpu.roll(right, GS - 1 - (2 * a + 3), 1), pltpu.roll(u, GS - 1, 1)
            )
            value = mass[a] * u - ((stack[a + 2] + stack[a]) + before + after)
            if a == 0:
                value = value + weight * (u - band)
            image.append(value)
        return image

    def send_rows(slots, first, ssem, rsem, peer):
        slots[0] = first
        for k in FAR_FIRST:
            remote(slots.at[0], slots.at[k], ssem, rsem, peer(k))

    def get_rows(slots, sem, at):
        wait_for(slots.at[pl.ds(1, 7)], sem)
        return slots[at]

    def send_band(n, rows):
        send_rows(b1s[n], rows, b1_ssem.at[n], b1_rsem.at[n], z_peer if n == 0 else y_peer)

    def forward_band(n):
        row = get_rows(b1s[n], b1_rsem.at[n], shift_z if n == 0 else up_there)
        send_rows(b2s[n], row, b2_ssem.at[n], b2_rsem.at[n], y_peer if n == 0 else z_peer)

    def get_band(n):
        return get_rows(b2s[n], b2_rsem.at[n], up if n == 0 else shift_z)

    def send_x(n, coarse):
        x_send[n] = coarse
        for k in FAR_FIRST:
            remote(x_send.at[n], x_recv.at[n, k - 1], x_ssem.at[n], x_rsem.at[n], x_peer(k))

    def pass_z(n):
        wait_for(x_recv.at[n], x_rsem.at[n])
        total = x_send[n]
        for k in range(NAX - 1):
            total = total + x_recv[n, k]
        z_tiles[n, z] = total
        for k in FAR_FIRST:
            remote(z_tiles.at[n, z], z_tiles.at[n, z], z_ssem.at[n], z_rsem.at[n], z_peer(k))

    def pass_y(n):
        wait_for(z_tiles.at[n, pl.ds(0, NZ - 1)], z_rsem.at[n])
        gathered = jnp.concatenate([z_tiles[n, t] for t in range(NZ)], axis=1)
        if n == 0:
            own_copy.wait()
            wait_for(inverse_y.at[pl.ds(0, NY - 1)], m_rsem)
        matrix = jnp.concatenate([inverse_y[t] for t in range(NY)], axis=0)
        y_send[n] = joined(nt(two_parts(gathered), matrix))
        for k in FAR_FIRST:
            remote(y_send.at[n], y_recv.at[n, k - 1], y_ssem.at[n], y_rsem.at[n], y_peer(k))

    def get_y(n):
        wait_for(y_recv.at[n], y_rsem.at[n])
        total = y_send[n]
        for k in range(NY - 1):
            total = total + y_recv[n, k]
        return total

    def send_coarse(n, tile):
        ws[n][0] = tile
        for k in FAR_FIRST:
            remote(ws[n].at[0], ws[n].at[k], w_ssem.at[n], w_rsem.at[n], z_peer(k))

    def get_coarse(n):
        wait_for(ws[n].at[pl.ds(1, NZ - 1)], w_rsem.at[n])
        return ws[n][shift_z]

    def prolong(coarse, rows):
        out = joined(nn(two_parts(coarse), rows))
        return [out[:, i * GS : (i + 1) * GS] for i in range(rows.shape[1] // GS)]

    def inner_products(residual, image):
        cross = residual[0] * image[0]
        square = image[0] * image[0]
        for a in range(1, GA):
            cross = cross + residual[a] * image[a]
            square = square + image[a] * image[a]
        cross = jnp.sum(cross, axis=1, keepdims=True)
        square = jnp.sum(square, axis=1, keepdims=True)
        spread_out = jnp.where(lane == rotor, cross, jnp.where(lane == rotor + R, square, 0.0))
        return jnp.sum(spread_out, axis=0, keepdims=True)

    def send_inner(n, row):
        f_rows[n, pl.ds(NAX - 1, 1)] = row
        for k in FAR_FIRST:
            remote(
                f_rows.at[n, pl.ds(NAX - 1, 1)], f_rows.at[n, pl.ds(k - 1, 1)],
                f_ssem.at[n], f_rsem.at[n], x_peer(k),
            )

    def pass_inner(n):
        wait_for(f_rows.at[n, pl.ds(0, NAX - 1)], f_rsem.at[n])
        e_rows[n, pl.ds(NSEC - 1, 1)] = jnp.sum(f_rows[n], axis=0, keepdims=True)

        for i in FAR_FIRST + (0,):
            for j in FAR_FIRST + (0,):
                if i or j:
                    remote(
                        e_rows.at[n, pl.ds(NSEC - 1, 1)], e_rows.at[n, pl.ds(i * NZ + j - 1, 1)],
                        e_ssem.at[n], e_rsem.at[n], ((y + i) % NY * NZ + (z + j) % NZ, q),
                    )

    def get_step(n):
        wait_for(e_rows.at[n, pl.ds(0, NSEC - 1)], e_rsem.at[n])
        row = jnp.sum(e_rows[n], axis=0, keepdims=True)
        cross = jnp.sum(jnp.where(lane == rotor, row, 0.0), axis=1, keepdims=True)
        square = jnp.sum(jnp.where(lane == rotor + R, row, 0.0), axis=1, keepdims=True)
        return cross / (square + EPSILON)

    coarse_r0 = coarse_of(r0)

    pl.semaphore_wait(barrier, 7 + 7 + 7 + 2)

    send_x(0, coarse_r0)
    send_halo(0, r0)
    for k in FAR_FIRST:
        remote(inverse_for((y + k) % NY), inverse_y.at[y], m_ssem, m_rsem, y_peer(k))
    send_rows(c1, basis[0].astype(BF16), c1_ssem, c1_rsem, z_peer)
    pass_z(0)
    halo_r0 = get_halo(0)
    solver_copy.wait()
    local_r0 = local_solve(r0, halo_r0)
    send_band(0, local_r0[0])
    pass_y(0)
    forward_band(0)
    send_rows(c2, get_rows(c1, c1_rsem, shift_z), c2_ssem, c2_rsem, y_peer)
    coarse = get_y(0)
    send_coarse(0, coarse)
    corr0 = [u + v for u, v in zip(local_r0, prolong(coarse, basis_y))]
    send_halo(1, corr0)
    band_row = get_band(0)
    band_basis = spread(get_rows(c2, c2_rsem, up).astype(F32), (y + NY - up) % NY)
    band_corr0 = band_row + prolong(get_coarse(0), band_basis)[0]
    image0 = apply_operator(corr0, get_halo(1), band_corr0)

    send_x(1, coarse_of(image0))
    send_halo(2, image0)
    send_inner(0, inner_products(r0, image0))
    pass_z(1)
    local_im = local_solve(image0, get_halo(2))
    send_band(1, local_im[0])
    pass_inner(0)
    pass_y(1)
    forward_band(1)
    coarse = get_y(1)
    send_coarse(1, coarse)
    diff = [u + v for u, v in zip(local_im, prolong(coarse, basis_y))]
    send_halo(3, diff)
    step0 = get_step(0)
    corr1 = [u - step0 * v for u, v in zip(corr0, diff)]
    res1 = [u - step0 * v for u, v in zip(r0, image0)]
    band_row = get_band(1)
    band_diff = band_row + prolong(get_coarse(1), band_basis)[0]
    image_diff = apply_operator(diff, get_halo(3), band_diff)
    image1 = [u - step0 * v for u, v in zip(image0, image_diff)]

    send_inner(1, inner_products(res1, image1))
    pass_inner(1)
    step1 = get_step(1)
    for a in range(GA):
        out_ref[0, :, a, :] = step0 * corr0[a] + step1 * corr1[a]
        out_ref[1, :, a, :] = res1[a] - step1 * image1[a]

    wait_for(inverse_y.at[pl.ds(0, NY - 1)], m_ssem)
    wait_for(c1.at[pl.ds(1, 7)], c1_ssem)
    wait_for(c2.at[pl.ds(1, 7)], c2_ssem)
    for n in range(4):
        wait_for(h_recv.at[n], h_ssem.at[n])
    for n in range(2):
        wait_for(x_recv.at[n], x_ssem.at[n])
        wait_for(z_tiles.at[n, pl.ds(0, NZ - 1)], z_ssem.at[n])
        wait_for(y_recv.at[n], y_ssem.at[n])
        wait_for(ws[n].at[pl.ds(1, NZ - 1)], w_ssem.at[n])
        wait_for(b1s[n].at[pl.ds(1, NY - 1)], b1_ssem.at[n])
        wait_for(b2s[n].at[pl.ds(1, NZ - 1)], b2_ssem.at[n])
        wait_for(f_rows.at[n, pl.ds(0, NAX - 1)], f_ssem.at[n])
        wait_for(e_rows.at[n, pl.ds(0, NSEC - 1)], e_ssem.at[n])


def on_device(
    right_side, mass_term, band_weight, band_shift, local_solver, coarse_inverse, coarse_basis
):
    hbm = pl.BlockSpec(memory_space=pltpu.HBM)
    dma = pltpu.SemaphoreType.DMA

    def tiles(*shape):
        return pltpu.VMEM(shape + (GS,), F32)

    both = pl.pallas_call(
        body,
        name="schwarz_steps",
        out_shape=pltpu.VMEM((2,) + right_side.shape, F32),
        in_specs=[hbm, hbm, hbm, pl.BlockSpec(memory_space=pltpu.SMEM), hbm, hbm, hbm],
        out_specs=pl.BlockSpec(memory_space=pltpu.VMEM),
        scratch_shapes=[
            pltpu.VMEM(right_side.shape, F32),
            pltpu.VMEM(mass_term.shape, F32),
            pltpu.VMEM(band_weight.shape, F32),
            pltpu.VMEM(coarse_basis.shape, BF16),
            pltpu.VMEM((NEXT, GA * GS), BF16),
            pltpu.VMEM((NY, NV, NZ * GS), BF16),
            tiles(4, 3, R),
            tiles(4, 4, R),
            tiles(2, R),
            tiles(2, NAX - 1, R),
            tiles(2, NZ, R),
            tiles(2, R),
            tiles(2, NY - 1, R),
            tiles(NZ, R),
            tiles(NZ, R),
            tiles(NY, R),
            tiles(NY, R),
            tiles(NY, R),
            tiles(NZ, R),
            pltpu.VMEM((NZ, NV, GS), BF16),
            pltpu.VMEM((NY, NV, GS), BF16),
            tiles(2, NAX),
            tiles(2, NSEC),
            dma((6,)),
            dma,
            dma,
            dma,
            dma,
            dma,
            dma,
            dma((4,)),
            dma((4,)),
        ]
        + [dma((2,))] * 16,
        compiler_params=pltpu.CompilerParams(
            collective_id=0, has_side_effects=True, vmem_limit_bytes=60 << 20
        ),
    )(
        right_side, mass_term, band_weight, band_shift, coarse_basis,
        jnp.swapaxes(local_solver, 1, 2), coarse_inverse,
    )
    return both[0], both[1]


def solution(mesh):
    placed = (
        P(None, "axial", "sector"),
        P("axial", "sector"),
        P("axial", "sector"),
        P(),
        P("axial", "sector", None),
        P(("sector", "axial"), None),
        P(None, "axial", "sector"),
    )
    return jax.shard_map(
        on_device,
        mesh=mesh,
        in_specs=placed,
        out_specs=(P(None, "axial", "sector"), P(None, "axial", "sector")),
        check_vma=False,
    )
```

```python
import jax
import jax.numpy as jnp
from jax import lax
from jax.experimental import pallas as pl
from jax.experimental.pallas import tpu as pltpu
from jax.sharding import PartitionSpec as P

EPSILON = 1e-06
MESH = pl.DeviceIdType.MESH
F32 = jnp.float32
BF16 = jnp.bfloat16

R = 16
GA = 4
GS = 128
NV = 16
NEXT = 780
NZ = 8
NY = 8
NSEC = NY * NZ
NAX = 8
FAR_FIRST = (4, 3, 5, 2, 6, 1, 7)


def nt(a, b):
    return lax.dot_general(a, b, (((1,), (1,)), ((), ())), preferred_element_type=F32)


def nn(a, b):
    return lax.dot_general(a, b, (((1,), (0,)), ((), ())), preferred_element_type=F32)


def two_parts(x):
    high = x.astype(BF16)
    low = (x - high.astype(F32)).astype(BF16)
    return jnp.concatenate([high, low], axis=0)


def joined(x):
    half = x.shape[0] // 2
    return x[:half] + x[half:]


def body(
    rhs_hbm, mass_hbm, bw_hbm, shift_ref, basis_hbm, solver_hbm, inverse_hbm,
    out_ref,
    rhs_ref, mass_ref, bw_ref, basis_ref,
    solver, inverse_y, h_send, h_recv, x_send, x_recv, z_tiles, plane, y_send, y_recv,
    w_first, w_second, b1_first, b1_second, b2_first, b2_second, c1, c2, f_rows, e_rows,
    local_sems, c1_ssem, c1_rsem, c2_ssem, c2_rsem, m_ssem, m_rsem, h_ssem, h_rsem, x_ssem, x_rsem, z_ssem, z_rsem, p_ssem, p_rsem,
    y_ssem, y_rsem, w_ssem, w_rsem, b1_ssem, b1_rsem, b2_ssem, b2_rsem, f_ssem, f_rsem, e_ssem, e_rsem,
):
    ws = (w_first, w_second)
    b1s = (b1_first, b1_second)
    b2s = (b2_first, b2_second)
    s = lax.axis_index("sector")
    q = lax.axis_index("axial")
    y = s // NZ
    z = s % NZ

    def x_peer(k):
        return (s, (q + k) % NAX)

    def y_peer(k):
        return (((y + k) % NY) * NZ + z, q)

    def z_peer(k):
        return (y * NZ + (z + k) % NZ, q)

    def s_peer(k):
        return ((s + k) % NSEC, q)

    def wait_for(ref, sem):
        pltpu.make_async_copy(ref, ref, sem).wait()

    def remote(src, dst, ssem, rsem, device):
        pltpu.make_async_remote_copy(
            src_ref=src, dst_ref=dst, send_sem=ssem, recv_sem=rsem,
            device_id=device, device_id_type=MESH,
        ).start()

    loads = [
        pltpu.make_async_copy(src, dst, local_sems.at[i])
        for i, (src, dst) in enumerate(
            ((rhs_hbm, rhs_ref), (basis_hbm, basis_ref), (mass_hbm, mass_ref), (bw_hbm, bw_ref))
        )
    ]
    for load in loads:
        load.start()

    barrier = pltpu.get_barrier_semaphore()
    for k in FAR_FIRST:
        for peer in (y_peer(k), z_peer(k), x_peer(k)):
            pl.semaphore_signal(barrier, inc=1, device_id=peer, device_id_type=MESH)
    for k in (1, NSEC - 1):
        pl.semaphore_signal(barrier, inc=1, device_id=s_peer(k), device_id_type=MESH)

    solver_copy = pltpu.make_async_copy(solver_hbm.at[0], solver, local_sems.at[4])
    solver_copy.start()

    def inverse_for(to):
        return inverse_hbm.at[:, pl.ds(pl.multiple_of(to * NZ * GS, NZ * GS), NZ * GS)]

    own_copy = pltpu.make_async_copy(inverse_for(y), inverse_y.at[y], local_sems.at[5])
    own_copy.start()

    lane = lax.broadcasted_iota(jnp.int32, (R, GS), 1)
    rotor = lax.broadcasted_iota(jnp.int32, (R, GS), 0)
    lane8 = lax.broadcasted_iota(jnp.int32, (8, GS), 1)
    row8 = lax.broadcasted_iota(jnp.int32, (8, GS), 0)
    rows128 = lax.broadcasted_iota(jnp.int32, (8 * NV, GS), 0) // NV
    for load in loads:
        load.wait()
    rhs = rhs_ref[...]
    r0 = [rhs[:, a, :] for a in range(GA)]
    basis_all = basis_ref[...].astype(F32)
    basis = [basis_all[:, a, :] for a in range(GA)]
    mass = [mass_ref[a : a + 1, :] + 4.0 for a in range(GA)]
    weight = bw_ref[...]
    shift = shift_ref[0]
    shift_z = shift % NZ
    up = (shift // NZ + jnp.where(z < shift_z, 1, 0)) % NY
    up_there = (shift // NZ + jnp.where(z + shift_z >= NZ, 1, 0)) % NY

    def spread(tile, at):
        return jnp.where(rows128 == at, jnp.concatenate([tile] * 8, axis=0), 0.0).astype(BF16)

    basis_q = jnp.concatenate([spread(t, q) for t in basis], axis=1)
    basis_each = jnp.concatenate([jnp.concatenate([t] * 8, axis=0).astype(BF16) for t in basis], axis=1)
    basis_y = jnp.concatenate([spread(t, y) for t in basis], axis=1)

    def coarse_of(field):
        return joined(nt(two_parts(jnp.concatenate(field, axis=1)), basis_q))

    def packed(tile):
        kept = jnp.where(lane // NV == rotor % 8, tile, 0.0)
        return [jnp.sum(kept[8 * h : 8 * h + 8], axis=0, keepdims=True) for h in range(2)]

    def block_transposed(x):
        for d in (4, 2, 1):
            from_above = pltpu.roll(pltpu.roll(x, d, 0), GS - NV * d, 1)
            from_below = pltpu.roll(pltpu.roll(x, 8 - d, 0), NV * d, 1)
            row_bit = (row8 // d) % 2
            block_bit = (lane8 // (NV * d)) % 2
            x = jnp.where(row_bit == block_bit, x, jnp.where(row_bit == 1, from_above, from_below))
        return x

    def edges(field):
        tile = jnp.zeros((R, GS), F32)
        for a in range(GA):
            at = 2 * (a + 1)
            moved = pltpu.roll(field[a], at + 1, 1)
            tile = jnp.where((lane == at) | (lane == at + 1), moved, tile)
        return tile

    def send_halo(n, field):
        h_send[n, 0] = edges(field)
        h_send[n, 1] = field[0]
        h_send[n, 2] = field[GA - 1]
        remote(h_send.at[n, 0], h_recv.at[n, 0], h_ssem.at[n], h_rsem.at[n], s_peer(1))
        remote(h_send.at[n, 0], h_recv.at[n, 1], h_ssem.at[n], h_rsem.at[n], s_peer(NSEC - 1))
        remote(h_send.at[n, 2], h_recv.at[n, 2], h_ssem.at[n], h_rsem.at[n], x_peer(1))
        remote(h_send.at[n, 1], h_recv.at[n, 3], h_ssem.at[n], h_rsem.at[n], x_peer(NAX - 1))

    def get_halo(n):
        wait_for(h_recv.at[n], h_rsem.at[n])
        above = jnp.where(q == 0, 0.0, h_recv[n, 2])
        below = jnp.where(q == NAX - 1, 0.0, h_recv[n, 3])
        return h_recv[n, 0], h_recv[n, 1], above, below

    def local_solve(field, halo):
        left, right, above, below = halo
        stack = [above] + field + [below]
        moved = [pltpu.roll(stack[j], 2 * j + 1, 1) for j in range(GA + 2)]
        zero = jnp.zeros((R, GS), F32)
        parts = []
        for t in range(GA + 3):
            here = moved[t] if t < GA + 2 else zero
            before = moved[t - 1] if t > 0 else zero
            tile = jnp.where(lane == 2 * t - 1, right, before)
            tile = jnp.where(lane == 2 * t, left, tile)
            parts.append(jnp.where(lane > 2 * t, here, tile))
        window = jnp.concatenate(parts, axis=1)
        out = joined(nn(two_parts(window)[:, :NEXT], solver[...]))
        return [out[:, a * GS : (a + 1) * GS] for a in range(GA)]

    def apply_operator(field, halo, band):
        left, right, above, below = halo
        stack = [above] + field + [below]
        image = []
        for a in range(GA):
            u = field[a]
            before = jnp.where(lane == 0, pltpu.roll(left, GS - 2 * (a + 1), 1), pltpu.roll(u, 1, 1))
            after = jnp.where(
                lane == GS - 1, pltpu.roll(right, GS - 1 - (2 * a + 3), 1), pltpu.roll(u, GS - 1, 1)
            )
            value = mass[a] * u - ((stack[a + 2] + stack[a]) + before + after)
            if a == 0:
                value = value + weight * (u - band)
            image.append(value)
        return image

    def send_rows(slots, first, ssem, rsem, peer):
        slots[0] = first
        for k in FAR_FIRST:
            remote(slots.at[0], slots.at[k], ssem, rsem, peer(k))

    def get_rows(slots, sem, at):
        wait_for(slots.at[pl.ds(1, 7)], sem)
        return slots[at]

    def send_band(n, rows):
        send_rows(b1s[n], rows, b1_ssem.at[n], b1_rsem.at[n], z_peer if n == 0 else y_peer)

    def forward_band(n):
        row = get_rows(b1s[n], b1_rsem.at[n], shift_z if n == 0 else up_there)
        send_rows(b2s[n], row, b2_ssem.at[n], b2_rsem.at[n], y_peer if n == 0 else z_peer)

    def get_band(n):
        return get_rows(b2s[n], b2_rsem.at[n], up if n == 0 else shift_z)

    def send_x(coarse):
        x_send[...] = coarse
        for k in FAR_FIRST:
            remote(x_send, x_recv.at[k - 1], x_ssem, x_rsem, x_peer(k))

    def pass_z():
        wait_for(x_recv, x_rsem)
        total = x_send[...]
        for k in range(NAX - 1):
            total = total + x_recv[k]
        z_tiles[z] = total
        for k in FAR_FIRST:
            remote(z_tiles.at[z], z_tiles.at[z], z_ssem, z_rsem, z_peer(k))

    def get_z():
        wait_for(z_tiles.at[pl.ds(0, NZ - 1)], z_rsem)
        own_copy.wait()
        wait_for(inverse_y.at[pl.ds(0, NY - 1)], m_rsem)
        return jnp.concatenate([z_tiles[t] for t in range(NZ)], axis=1)

    def send_plane(field):
        out = joined(nt(two_parts(jnp.concatenate(field, axis=1)), basis_each))
        at = z * NAX + q
        for h, row in enumerate(packed(out)):
            plane[h, pl.ds(at, 1)] = row
        for j in FAR_FIRST + (0,):
            for i in FAR_FIRST + (0,):
                if i or j:
                    remote(
                        plane.at[:, pl.ds(at, 1)], plane.at[:, pl.ds(at, 1)],
                        p_ssem, p_rsem, (y * NZ + (z + j) % NZ, (q + i) % NAX),
                    )

    def get_plane():
        wait_for(plane.at[:, pl.ds(0, NZ * NAX - 1)], p_rsem)
        halves = [
            jnp.concatenate([block_transposed(plane[h, pl.ds(8 * t, 8)]) for t in range(NZ)], axis=1)
            for h in range(2)
        ]
        return jnp.concatenate(halves, axis=0)

    def pass_y(n, gathered):
        matrix = jnp.concatenate([inverse_y[t] for t in range(NY)], axis=0)
        y_send[n] = joined(nt(two_parts(gathered), matrix))
        for k in FAR_FIRST:
            remote(y_send.at[n], y_recv.at[n, k - 1], y_ssem.at[n], y_rsem.at[n], y_peer(k))

    def get_y(n):
        wait_for(y_recv.at[n], y_rsem.at[n])
        total = y_send[n]
        for k in range(NY - 1):
            total = total + y_recv[n, k]
        return total

    def send_coarse(n, tile):
        ws[n][0] = tile
        for k in FAR_FIRST:
            remote(ws[n].at[0], ws[n].at[k], w_ssem.at[n], w_rsem.at[n], z_peer(k))

    def get_coarse(n):
        wait_for(ws[n].at[pl.ds(1, NZ - 1)], w_rsem.at[n])
        return ws[n][shift_z]

    def prolong(coarse, rows):
        out = joined(nn(two_parts(coarse), rows))
        return [out[:, i * GS : (i + 1) * GS] for i in range(rows.shape[1] // GS)]

    def inner_products(residual, image):
        cross = residual[0] * image[0]
        square = image[0] * image[0]
        for a in range(1, GA):
            cross = cross + residual[a] * image[a]
            square = square + image[a] * image[a]
        cross = jnp.sum(cross, axis=1, keepdims=True)
        square = jnp.sum(square, axis=1, keepdims=True)
        spread_out = jnp.where(lane == rotor, cross, jnp.where(lane == rotor + R, square, 0.0))
        return jnp.sum(spread_out, axis=0, keepdims=True)

    def send_inner(n, row):
        f_rows[n, pl.ds(NAX - 1, 1)] = row
        for k in FAR_FIRST:
            remote(
                f_rows.at[n, pl.ds(NAX - 1, 1)], f_rows.at[n, pl.ds(k - 1, 1)],
                f_ssem.at[n], f_rsem.at[n], x_peer(k),
            )

    def pass_inner(n):
        wait_for(f_rows.at[n, pl.ds(0, NAX - 1)], f_rsem.at[n])
        e_rows[n, pl.ds(NSEC - 1, 1)] = jnp.sum(f_rows[n], axis=0, keepdims=True)

        for i in FAR_FIRST + (0,):
            for j in FAR_FIRST + (0,):
                if i or j:
                    remote(
                        e_rows.at[n, pl.ds(NSEC - 1, 1)], e_rows.at[n, pl.ds(i * NZ + j - 1, 1)],
                        e_ssem.at[n], e_rsem.at[n], ((y + i) % NY * NZ + (z + j) % NZ, q),
                    )

    def get_step(n):
        wait_for(e_rows.at[n, pl.ds(0, NSEC - 1)], e_rsem.at[n])
        row = jnp.sum(e_rows[n], axis=0, keepdims=True)
        cross = jnp.sum(jnp.where(lane == rotor, row, 0.0), axis=1, keepdims=True)
        square = jnp.sum(jnp.where(lane == rotor + R, row, 0.0), axis=1, keepdims=True)
        return cross / (square + EPSILON)

    coarse_r0 = coarse_of(r0)

    pl.semaphore_wait(barrier, 7 + 7 + 7 + 2)

    send_x(coarse_r0)
    send_halo(0, r0)
    for k in FAR_FIRST:
        remote(inverse_for((y + k) % NY), inverse_y.at[y], m_ssem, m_rsem, y_peer(k))
    send_rows(c1, basis[0].astype(BF16), c1_ssem, c1_rsem, z_peer)
    pass_z()
    halo_r0 = get_halo(0)
    solver_copy.wait()
    local_r0 = local_solve(r0, halo_r0)
    send_band(0, local_r0[0])
    pass_y(0, get_z())
    forward_band(0)
    send_rows(c2, get_rows(c1, c1_rsem, shift_z), c2_ssem, c2_rsem, y_peer)
    coarse = get_y(0)
    send_coarse(0, coarse)
    corr0 = [u + v for u, v in zip(local_r0, prolong(coarse, basis_y))]
    send_halo(1, corr0)
    band_row = get_band(0)
    band_basis = spread(get_rows(c2, c2_rsem, up).astype(F32), (y + NY - up) % NY)
    band_corr0 = band_row + prolong(get_coarse(0), band_basis)[0]
    image0 = apply_operator(corr0, get_halo(1), band_corr0)

    send_plane(image0)
    send_halo(2, image0)
    send_inner(0, inner_products(r0, image0))
    local_im = local_solve(image0, get_halo(2))
    send_band(1, local_im[0])
    pass_inner(0)
    pass_y(1, get_plane())
    forward_band(1)
    coarse = get_y(1)
    send_coarse(1, coarse)
    diff = [u + v for u, v in zip(local_im, prolong(coarse, basis_y))]
    send_halo(3, diff)
    step0 = get_step(0)
    corr1 = [u - step0 * v for u, v in zip(corr0, diff)]
    res1 = [u - step0 * v for u, v in zip(r0, image0)]
    band_row = get_band(1)
    band_diff = band_row + prolong(get_coarse(1), band_basis)[0]
    image_diff = apply_operator(diff, get_halo(3), band_diff)
    image1 = [u - step0 * v for u, v in zip(image0, image_diff)]

    send_inner(1, inner_products(res1, image1))
    pass_inner(1)
    step1 = get_step(1)
    for a in range(GA):
        out_ref[0, :, a, :] = step0 * corr0[a] + step1 * corr1[a]
        out_ref[1, :, a, :] = res1[a] - step1 * image1[a]

    wait_for(inverse_y.at[pl.ds(0, NY - 1)], m_ssem)
    wait_for(c1.at[pl.ds(1, 7)], c1_ssem)
    wait_for(c2.at[pl.ds(1, 7)], c2_ssem)
    wait_for(x_recv, x_ssem)
    wait_for(z_tiles.at[pl.ds(0, NZ - 1)], z_ssem)
    wait_for(plane.at[:, pl.ds(0, NZ * NAX - 1)], p_ssem)
    for n in range(4):
        wait_for(h_recv.at[n], h_ssem.at[n])
    for n in range(2):
        wait_for(y_recv.at[n], y_ssem.at[n])
        wait_for(ws[n].at[pl.ds(1, NZ - 1)], w_ssem.at[n])
        wait_for(b1s[n].at[pl.ds(1, NY - 1)], b1_ssem.at[n])
        wait_for(b2s[n].at[pl.ds(1, NZ - 1)], b2_ssem.at[n])
        wait_for(f_rows.at[n, pl.ds(0, NAX - 1)], f_ssem.at[n])
        wait_for(e_rows.at[n, pl.ds(0, NSEC - 1)], e_ssem.at[n])


def on_device(
    right_side, mass_term, band_weight, band_shift, local_solver, coarse_inverse, coarse_basis
):
    hbm = pl.BlockSpec(memory_space=pltpu.HBM)
    dma = pltpu.SemaphoreType.DMA

    def tiles(*shape):
        return pltpu.VMEM(shape + (GS,), F32)

    both = pl.pallas_call(
        body,
        name="schwarz_steps",
        out_shape=pltpu.VMEM((2,) + right_side.shape, F32),
        in_specs=[hbm, hbm, hbm, pl.BlockSpec(memory_space=pltpu.SMEM), hbm, hbm, hbm],
        out_specs=pl.BlockSpec(memory_space=pltpu.VMEM),
        scratch_shapes=[
            pltpu.VMEM(right_side.shape, F32),
            pltpu.VMEM(mass_term.shape, F32),
            pltpu.VMEM(band_weight.shape, F32),
            pltpu.VMEM(coarse_basis.shape, BF16),
            pltpu.VMEM((NEXT, GA * GS), BF16),
            pltpu.VMEM((NY, NV, NZ * GS), BF16),
            tiles(4, 3, R),
            tiles(4, 4, R),
            tiles(R),
            tiles(NAX - 1, R),
            tiles(NZ, R),
            tiles(2, NZ * NAX),
            tiles(2, R),
            tiles(2, NY - 1, R),
            tiles(NZ, R),
            tiles(NZ, R),
            tiles(NY, R),
            tiles(NY, R),
            tiles(NY, R),
            tiles(NZ, R),
            pltpu.VMEM((NZ, NV, GS), BF16),
            pltpu.VMEM((NY, NV, GS), BF16),
            tiles(2, NAX),
            tiles(2, NSEC),
            dma((6,)),
            dma,
            dma,
            dma,
            dma,
            dma,
            dma,
            dma((4,)),
            dma((4,)),
        ]
        + [dma] * 6
        + [dma((2,))] * 12,
        compiler_params=pltpu.CompilerParams(
            collective_id=0, has_side_effects=True, vmem_limit_bytes=60 << 20
        ),
    )(
        right_side, mass_term, band_weight, band_shift, coarse_basis,
        jnp.swapaxes(local_solver, 1, 2), coarse_inverse,
    )
    return both[0], both[1]


def solution(mesh):
    placed = (
        P(None, "axial", "sector"),
        P("axial", "sector"),
        P("axial", "sector"),
        P(),
        P("axial", "sector", None),
        P(("sector", "axial"), None),
        P(None, "axial", "sector"),
    )
    return jax.shard_map(
        on_device,
        mesh=mesh,
        in_specs=placed,
        out_specs=(P(None, "axial", "sector"), P(None, "axial", "sector")),
        check_vma=False,
    )
```

```python
import jax
import jax.numpy as jnp
from jax import lax
from jax.experimental import pallas as pl
from jax.experimental.pallas import tpu as pltpu
from jax.sharding import PartitionSpec as P

EPSILON = 1e-06
MESH = pl.DeviceIdType.MESH
F32 = jnp.float32
BF16 = jnp.bfloat16

R = 16
GA = 4
GS = 128
NV = 16
NEXT = 780
NZ = 8
NY = 8
NSEC = NY * NZ
NAX = 8
FAR_FIRST = (4, 3, 5, 2, 6, 1, 7)


def nt(a, b):
    return lax.dot_general(a, b, (((1,), (1,)), ((), ())), preferred_element_type=F32)


def nn(a, b):
    return lax.dot_general(a, b, (((1,), (0,)), ((), ())), preferred_element_type=F32)


def two_parts(x):
    high = x.astype(BF16)
    low = (x - high.astype(F32)).astype(BF16)
    return jnp.concatenate([high, low], axis=0)


def joined(x):
    half = x.shape[0] // 2
    return x[:half] + x[half:]


def body(
    rhs_hbm, mass_hbm, bw_hbm, shift_ref, basis_hbm, solver_hbm, inverse_hbm,
    out_ref,
    rhs_ref, mass_ref, bw_ref, basis_ref,
    solver, inverse_y, h_send, h_recv, x_send, x_recv, z_tiles, plane, shares, beside,
    got_first, got_second, b1_first, b1_second, b2_first, b2_second, c1, c2, f_rows, e_rows,
    local_sems, c1_ssem, c1_rsem, c2_ssem, c2_rsem, m_ssem, m_rsem, h_ssem, h_rsem, x_ssem, x_rsem, z_ssem, z_rsem, p_ssem, p_rsem,
    s_ssem, s_rsem, r_ssem, r_rsem, a_ssem, a_rsem, b1_ssem, b1_rsem, b2_ssem, b2_rsem, f_ssem, f_rsem, e_ssem, e_rsem,
):
    got = (got_first, got_second)
    b1s = (b1_first, b1_second)
    b2s = (b2_first, b2_second)
    s = lax.axis_index("sector")
    q = lax.axis_index("axial")
    y = s // NZ
    z = s % NZ

    def x_peer(k):
        return (s, (q + k) % NAX)

    def y_peer(k):
        return (((y + k) % NY) * NZ + z, q)

    def z_peer(k):
        return (y * NZ + (z + k) % NZ, q)

    def s_peer(k):
        return ((s + k) % NSEC, q)

    def wait_for(ref, sem):
        pltpu.make_async_copy(ref, ref, sem).wait()

    def remote(src, dst, ssem, rsem, device):
        pltpu.make_async_remote_copy(
            src_ref=src, dst_ref=dst, send_sem=ssem, recv_sem=rsem,
            device_id=device, device_id_type=MESH,
        ).start()

    loads = [
        pltpu.make_async_copy(src, dst, local_sems.at[i])
        for i, (src, dst) in enumerate(
            ((rhs_hbm, rhs_ref), (basis_hbm, basis_ref), (mass_hbm, mass_ref), (bw_hbm, bw_ref))
        )
    ]
    for load in loads:
        load.start()

    barrier = pltpu.get_barrier_semaphore()
    for k in FAR_FIRST:
        for peer in (y_peer(k), z_peer(k), x_peer(k)):
            pl.semaphore_signal(barrier, inc=1, device_id=peer, device_id_type=MESH)
    for k in (1, NSEC - 1):
        pl.semaphore_signal(barrier, inc=1, device_id=s_peer(k), device_id_type=MESH)

    solver_copy = pltpu.make_async_copy(solver_hbm.at[0], solver, local_sems.at[4])
    solver_copy.start()

    def inverse_for(to):
        return inverse_hbm.at[:, pl.ds(pl.multiple_of(to * NZ * GS, NZ * GS), NZ * GS)]

    own_copy = pltpu.make_async_copy(inverse_for(y), inverse_y.at[y], local_sems.at[5])
    own_copy.start()

    lane = lax.broadcasted_iota(jnp.int32, (R, GS), 1)
    rotor = lax.broadcasted_iota(jnp.int32, (R, GS), 0)
    lane8 = lax.broadcasted_iota(jnp.int32, (8, GS), 1)
    row8 = lax.broadcasted_iota(jnp.int32, (8, GS), 0)
    rows128 = lax.broadcasted_iota(jnp.int32, (8 * NV, GS), 0) // NV
    for load in loads:
        load.wait()
    rhs = rhs_ref[...]
    r0 = [rhs[:, a, :] for a in range(GA)]
    basis_all = basis_ref[...].astype(F32)
    basis = [basis_all[:, a, :] for a in range(GA)]
    mass = [mass_ref[a : a + 1, :] + 4.0 for a in range(GA)]
    weight = bw_ref[...]
    shift = shift_ref[0]
    shift_z = shift % NZ
    up = (shift // NZ + jnp.where(z < shift_z, 1, 0)) % NY
    up_there = (shift // NZ + jnp.where(z + shift_z >= NZ, 1, 0)) % NY

    def spread(tile, at):
        return jnp.where(rows128 == at, jnp.concatenate([tile] * 8, axis=0), 0.0).astype(BF16)

    def each(tile):
        return jnp.concatenate([tile.astype(F32)] * 8, axis=0).astype(BF16)

    basis_q = jnp.concatenate([spread(t, q) for t in basis], axis=1)
    basis_each = jnp.concatenate([each(t) for t in basis], axis=1)

    def coarse_of(field):
        return joined(nt(two_parts(jnp.concatenate(field, axis=1)), basis_q))

    def packed(tile):
        kept = jnp.where(lane // NV == rotor % 8, tile, 0.0)
        return [jnp.sum(kept[8 * h : 8 * h + 8], axis=0, keepdims=True) for h in range(2)]

    def block_transposed(x):
        for d in (4, 2, 1):
            from_above = pltpu.roll(pltpu.roll(x, d, 0), GS - NV * d, 1)
            from_below = pltpu.roll(pltpu.roll(x, 8 - d, 0), NV * d, 1)
            row_bit = (row8 // d) % 2
            block_bit = (lane8 // (NV * d)) % 2
            x = jnp.where(row_bit == block_bit, x, jnp.where(row_bit == 1, from_above, from_below))
        return x

    def edges(field):
        tile = jnp.zeros((R, GS), F32)
        for a in range(GA):
            at = 2 * (a + 1)
            moved = pltpu.roll(field[a], at + 1, 1)
            tile = jnp.where((lane == at) | (lane == at + 1), moved, tile)
        return tile

    def send_halo(n, field):
        h_send[n, 0] = edges(field)
        h_send[n, 1] = field[0]
        h_send[n, 2] = field[GA - 1]
        remote(h_send.at[n, 0], h_recv.at[n, 0], h_ssem.at[n], h_rsem.at[n], s_peer(1))
        remote(h_send.at[n, 0], h_recv.at[n, 1], h_ssem.at[n], h_rsem.at[n], s_peer(NSEC - 1))
        remote(h_send.at[n, 2], h_recv.at[n, 2], h_ssem.at[n], h_rsem.at[n], x_peer(1))
        remote(h_send.at[n, 1], h_recv.at[n, 3], h_ssem.at[n], h_rsem.at[n], x_peer(NAX - 1))

    def get_halo(n):
        wait_for(h_recv.at[n], h_rsem.at[n])
        above = jnp.where(q == 0, 0.0, h_recv[n, 2])
        below = jnp.where(q == NAX - 1, 0.0, h_recv[n, 3])
        return h_recv[n, 0], h_recv[n, 1], above, below

    def local_solve(field, halo):
        left, right, above, below = halo
        stack = [above] + field + [below]
        moved = [pltpu.roll(stack[j], 2 * j + 1, 1) for j in range(GA + 2)]
        zero = jnp.zeros((R, GS), F32)
        parts = []
        for t in range(GA + 3):
            here = moved[t] if t < GA + 2 else zero
            before = moved[t - 1] if t > 0 else zero
            tile = jnp.where(lane == 2 * t - 1, right, before)
            tile = jnp.where(lane == 2 * t, left, tile)
            parts.append(jnp.where(lane > 2 * t, here, tile))
        window = jnp.concatenate(parts, axis=1)
        out = joined(nn(two_parts(window)[:, :NEXT], solver[...]))
        return [out[:, a * GS : (a + 1) * GS] for a in range(GA)]

    def apply_operator(field, halo, band):
        left, right, above, below = halo
        stack = [above] + field + [below]
        image = []
        for a in range(GA):
            u = field[a]
            before = jnp.where(lane == 0, pltpu.roll(left, GS - 2 * (a + 1), 1), pltpu.roll(u, 1, 1))
            after = jnp.where(
                lane == GS - 1, pltpu.roll(right, GS - 1 - (2 * a + 3), 1), pltpu.roll(u, GS - 1, 1)
            )
            value = mass[a] * u - ((stack[a + 2] + stack[a]) + before + after)
            if a == 0:
                value = value + weight * (u - band)
            image.append(value)
        return image

    def send_rows(slots, first, ssem, rsem, peer):
        slots[0] = first
        for k in FAR_FIRST:
            remote(slots.at[0], slots.at[k], ssem, rsem, peer(k))

    def get_rows(slots, sem, at):
        wait_for(slots.at[pl.ds(1, 7)], sem)
        return slots[at]

    def send_band(n, rows):
        send_rows(b1s[n], rows, b1_ssem.at[n], b1_rsem.at[n], z_peer if n == 0 else y_peer)

    def forward_band(n):
        row = get_rows(b1s[n], b1_rsem.at[n], shift_z if n == 0 else up_there)
        send_rows(b2s[n], row, b2_ssem.at[n], b2_rsem.at[n], y_peer if n == 0 else z_peer)

    def get_band(n):
        return get_rows(b2s[n], b2_rsem.at[n], up if n == 0 else shift_z)

    def send_x(coarse):
        x_send[...] = coarse
        for k in FAR_FIRST:
            remote(x_send, x_recv.at[k - 1], x_ssem, x_rsem, x_peer(k))

    def pass_z():
        wait_for(x_recv, x_rsem)
        total = x_send[...]
        for k in range(NAX - 1):
            total = total + x_recv[k]
        z_tiles[z] = total
        for k in FAR_FIRST:
            remote(z_tiles.at[z], z_tiles.at[z], z_ssem, z_rsem, z_peer(k))

    def get_z():
        wait_for(z_tiles.at[pl.ds(0, NZ - 1)], z_rsem)
        own_copy.wait()
        wait_for(inverse_y.at[pl.ds(0, NY - 1)], m_rsem)
        return jnp.concatenate([z_tiles[t] for t in range(NZ)], axis=1)

    def send_plane(field):
        out = joined(nt(two_parts(jnp.concatenate(field, axis=1)), basis_each))
        at = z * NAX + q
        for h, row in enumerate(packed(out)):
            plane[h, pl.ds(at, 1)] = row
        for j in FAR_FIRST + (0,):
            for i in FAR_FIRST + (0,):
                if i or j:
                    remote(
                        plane.at[:, pl.ds(at, 1)], plane.at[:, pl.ds(at, 1)],
                        p_ssem, p_rsem, (y * NZ + (z + j) % NZ, (q + i) % NAX),
                    )

    def get_plane():
        wait_for(plane.at[:, pl.ds(0, NZ * NAX - 1)], p_rsem)
        halves = [
            jnp.concatenate([block_transposed(plane[h, pl.ds(8 * t, 8)]) for t in range(NZ)], axis=1)
            for h in range(2)
        ]
        return jnp.concatenate(halves, axis=0)

    def send_shares(n, gathered):
        matrix = jnp.concatenate([inverse_y[t] for t in range(NY)], axis=0)
        out = joined(nt(two_parts(gathered), matrix))
        for h in range(2):
            share = block_transposed(out[8 * h : 8 * h + 8])
            band = pltpu.roll(share, up_there, 0)
            ahead = jnp.where(z == NZ - 1, pltpu.roll(share, 1, 0), share)
            behind = jnp.where(z == 0, pltpu.roll(share, NY - 1, 0), share)
            for i, own in enumerate((share, ahead, behind)):
                shares[n, i, h] = own
                shares[n, i, 2 + h] = band
        for h in range(4):
            got[n][h, z, pl.ds(y, 1)] = shares[n, 0, h, pl.ds(y, 1)]
        for i in FAR_FIRST + (0,):
            to = (y + i) % NY
            for j in FAR_FIRST + (0,):
                if i or j:
                    remote(
                        shares.at[n, {1: 1, NZ - 1: 2}.get(j, 0), :, pl.ds(to, 1)], got[n].at[:, z, pl.ds(y, 1)],
                        (s_ssem if j else r_ssem).at[n], (s_rsem if j else r_rsem).at[n],
                        (to * NZ + (z + j) % NZ, q),
                    )
            for side, k in enumerate((1, NAX - 1)):
                remote(
                    shares.at[n, 0, pl.ds(0, 2), pl.ds(to, 1)], beside.at[n, side, :, pl.ds(y, 1)],
                    a_ssem.at[n], a_rsem.at[n], (to * NZ + z, (q + k) % NAX),
                )

    def wait_shares(n, s_sem, r_sem, a_sem):
        wait_for(got[n].at[:, pl.ds(0, NZ - 1)], s_sem.at[n])
        wait_for(got[n].at[:, 0, pl.ds(0, NY - 1)], r_sem.at[n])
        wait_for(beside.at[n], a_sem.at[n])

    def unpacked(first, second):
        rows = [jnp.sum(x, axis=0, keepdims=True) for x in (first, second)]
        tile = jnp.concatenate([jnp.broadcast_to(x, (8, GS)) for x in rows], axis=0)
        return jnp.where(lane // NV == rotor % 8, tile, 0.0)

    def get_shares(n):
        wait_shares(n, s_rsem, r_rsem, a_rsem)

        def along_z(at, h=0):
            return unpacked(got[n][h, at], got[n][h + 1, at])

        sides = (
            along_z((z + NZ - 1) % NZ), along_z((z + 1) % NZ),
            unpacked(beside[n, 0, 0], beside[n, 0, 1]), unpacked(beside[n, 1, 0], beside[n, 1, 1]),
        )
        return along_z(z), sides, along_z((z + NZ - shift_z) % NZ, 2)

    def prolong(coarse, rows):
        out = joined(nn(two_parts(coarse), rows))
        return [out[:, i * GS : (i + 1) * GS] for i in range(rows.shape[1] // GS)]

    def inner_products(residual, image):
        cross = residual[0] * image[0]
        square = image[0] * image[0]
        for a in range(1, GA):
            cross = cross + residual[a] * image[a]
            square = square + image[a] * image[a]
        cross = jnp.sum(cross, axis=1, keepdims=True)
        square = jnp.sum(square, axis=1, keepdims=True)
        spread_out = jnp.where(lane == rotor, cross, jnp.where(lane == rotor + R, square, 0.0))
        return jnp.sum(spread_out, axis=0, keepdims=True)

    def send_inner(n, row):
        f_rows[n, pl.ds(NAX - 1, 1)] = row
        for k in FAR_FIRST:
            remote(
                f_rows.at[n, pl.ds(NAX - 1, 1)], f_rows.at[n, pl.ds(k - 1, 1)],
                f_ssem.at[n], f_rsem.at[n], x_peer(k),
            )

    def pass_inner(n):
        wait_for(f_rows.at[n, pl.ds(0, NAX - 1)], f_rsem.at[n])
        e_rows[n, pl.ds(NSEC - 1, 1)] = jnp.sum(f_rows[n], axis=0, keepdims=True)

        for i in FAR_FIRST + (0,):
            for j in FAR_FIRST + (0,):
                if i or j:
                    remote(
                        e_rows.at[n, pl.ds(NSEC - 1, 1)], e_rows.at[n, pl.ds(i * NZ + j - 1, 1)],
                        e_ssem.at[n], e_rsem.at[n], ((y + i) % NY * NZ + (z + j) % NZ, q),
                    )

    def get_step(n):
        wait_for(e_rows.at[n, pl.ds(0, NSEC - 1)], e_rsem.at[n])
        row = jnp.sum(e_rows[n], axis=0, keepdims=True)
        cross = jnp.sum(jnp.where(lane == rotor, row, 0.0), axis=1, keepdims=True)
        square = jnp.sum(jnp.where(lane == rotor + R, row, 0.0), axis=1, keepdims=True)
        return cross / (square + EPSILON)

    coarse_r0 = coarse_of(r0)

    pl.semaphore_wait(barrier, 7 + 7 + 7 + 2)

    send_x(coarse_r0)
    send_halo(0, r0)
    send_halo(4, basis)
    for k in FAR_FIRST:
        remote(inverse_for((y + k) % NY), inverse_y.at[y], m_ssem, m_rsem, y_peer(k))
    send_rows(c1, basis[0].astype(BF16), c1_ssem, c1_rsem, z_peer)
    pass_z()
    halo_r0 = get_halo(0)
    solver_copy.wait()
    local_r0 = local_solve(r0, halo_r0)
    send_band(0, local_r0[0])
    send_halo(1, local_r0)
    send_shares(0, get_z())
    forward_band(0)
    send_rows(c2, get_rows(c1, c1_rsem, shift_z), c2_ssem, c2_rsem, y_peer)
    basis_sides = [each(t) for t in get_halo(4)]
    halo = get_halo(1)
    band_row = get_band(0)
    band_basis = each(get_rows(c2, c2_rsem, up))

    def with_coarse(field, halo, band_row, n):
        coarse, sides, band = get_shares(n)
        own = [u + v for u, v in zip(field, prolong(coarse, basis_each))]
        around = [u + prolong(v, w)[0] for u, v, w in zip(halo, sides, basis_sides)]
        return own, around, band_row + prolong(band, band_basis)[0]

    corr0, halo, band_row = with_coarse(local_r0, halo, band_row, 0)
    image0 = apply_operator(corr0, halo, band_row)

    send_plane(image0)
    send_halo(2, image0)
    send_inner(0, inner_products(r0, image0))
    local_im = local_solve(image0, get_halo(2))
    send_band(1, local_im[0])
    send_halo(3, local_im)
    pass_inner(0)
    send_shares(1, get_plane())
    forward_band(1)
    step0 = get_step(0)
    res1 = [u - step0 * v for u, v in zip(r0, image0)]
    halo = get_halo(3)
    band_row = get_band(1)
    diff, halo, band_row = with_coarse(local_im, halo, band_row, 1)
    image_diff = apply_operator(diff, halo, band_row)
    corr1 = [u - step0 * v for u, v in zip(corr0, diff)]
    image1 = [u - step0 * v for u, v in zip(image0, image_diff)]

    send_inner(1, inner_products(res1, image1))
    pass_inner(1)
    step1 = get_step(1)
    for a in range(GA):
        out_ref[0, :, a, :] = step0 * corr0[a] + step1 * corr1[a]
        out_ref[1, :, a, :] = res1[a] - step1 * image1[a]

    wait_for(inverse_y.at[pl.ds(0, NY - 1)], m_ssem)
    wait_for(c1.at[pl.ds(1, 7)], c1_ssem)
    wait_for(c2.at[pl.ds(1, 7)], c2_ssem)
    wait_for(x_recv, x_ssem)
    wait_for(z_tiles.at[pl.ds(0, NZ - 1)], z_ssem)
    wait_for(plane.at[:, pl.ds(0, NZ * NAX - 1)], p_ssem)
    for n in range(5):
        wait_for(h_recv.at[n], h_ssem.at[n])
    for n in range(2):
        wait_shares(n, s_ssem, r_ssem, a_ssem)
        wait_for(b1s[n].at[pl.ds(1, NY - 1)], b1_ssem.at[n])
        wait_for(b2s[n].at[pl.ds(1, NZ - 1)], b2_ssem.at[n])
        wait_for(f_rows.at[n, pl.ds(0, NAX - 1)], f_ssem.at[n])
        wait_for(e_rows.at[n, pl.ds(0, NSEC - 1)], e_ssem.at[n])


def on_device(
    right_side, mass_term, band_weight, band_shift, local_solver, coarse_inverse, coarse_basis
):
    hbm = pl.BlockSpec(memory_space=pltpu.HBM)
    dma = pltpu.SemaphoreType.DMA

    def tiles(*shape):
        return pltpu.VMEM(shape + (GS,), F32)

    both = pl.pallas_call(
        body,
        name="schwarz_steps",
        out_shape=pltpu.VMEM((2,) + right_side.shape, F32),
        in_specs=[hbm, hbm, hbm, pl.BlockSpec(memory_space=pltpu.SMEM), hbm, hbm, hbm],
        out_specs=pl.BlockSpec(memory_space=pltpu.VMEM),
        scratch_shapes=[
            pltpu.VMEM(right_side.shape, F32),
            pltpu.VMEM(mass_term.shape, F32),
            pltpu.VMEM(band_weight.shape, F32),
            pltpu.VMEM(coarse_basis.shape, BF16),
            pltpu.VMEM((NEXT, GA * GS), BF16),
            pltpu.VMEM((NY, NV, NZ * GS), BF16),
            tiles(5, 3, R),
            tiles(5, 4, R),
            tiles(R),
            tiles(NAX - 1, R),
            tiles(NZ, R),
            tiles(2, NZ * NAX),
            tiles(2, 3, 4, NY),
            tiles(2, 2, 2, NY),
            tiles(4, NZ, NY),
            tiles(4, NZ, NY),
            tiles(NY, R),
            tiles(NY, R),
            tiles(NY, R),
            tiles(NZ, R),
            pltpu.VMEM((NZ, NV, GS), BF16),
            pltpu.VMEM((NY, NV, GS), BF16),
            tiles(2, NAX),
            tiles(2, NSEC),
            dma((6,)),
            dma,
            dma,
            dma,
            dma,
            dma,
            dma,
            dma((5,)),
            dma((5,)),
        ]
        + [dma] * 6
        + [dma((2,))] * 14,
        compiler_params=pltpu.CompilerParams(
            collective_id=0, has_side_effects=True, vmem_limit_bytes=60 << 20
        ),
    )(
        right_side, mass_term, band_weight, band_shift, coarse_basis,
        jnp.swapaxes(local_solver, 1, 2), coarse_inverse,
    )
    return both[0], both[1]


def solution(mesh):
    placed = (
        P(None, "axial", "sector"),
        P("axial", "sector"),
        P("axial", "sector"),
        P(),
        P("axial", "sector", None),
        P(("sector", "axial"), None),
        P(None, "axial", "sector"),
    )
    return jax.shard_map(
        on_device,
        mesh=mesh,
        in_specs=placed,
        out_specs=(P(None, "axial", "sector"), P(None, "axial", "sector")),
        check_vma=False,
    )
```

```python
import jax
import jax.numpy as jnp
from jax import lax
from jax.experimental import pallas as pl
from jax.experimental.pallas import tpu as pltpu
from jax.sharding import PartitionSpec as P

EPSILON = 1e-06
MESH = pl.DeviceIdType.MESH
F32 = jnp.float32
BF16 = jnp.bfloat16

R = 16
GA = 4
GS = 128
NV = 16
NEXT = 780
NZ = 8
NY = 8
NSEC = NY * NZ
NAX = 8
FAR_FIRST = (4, 3, 5, 2, 6, 1, 7)


def nt(a, b):
    return lax.dot_general(a, b, (((1,), (1,)), ((), ())), preferred_element_type=F32)


def nn(a, b):
    return lax.dot_general(a, b, (((1,), (0,)), ((), ())), preferred_element_type=F32)


def two_parts(x):
    high = x.astype(BF16)
    low = (x - high.astype(F32)).astype(BF16)
    return jnp.concatenate([high, low], axis=0)


def joined(x):
    half = x.shape[0] // 2
    return x[:half] + x[half:]


def body(
    rhs_hbm, mass_hbm, bw_hbm, shift_ref, basis_hbm, solver_hbm, inverse_hbm,
    out_ref,
    rhs_ref, mass_ref, bw_ref, basis_ref,
    solver, inverse_y, h_send, h_recv, x_send, x_recv, z_tiles, plane, shares, beside,
    got_first, got_second, b1_first, b1_second, b2_first, b2_second, c1, c2, f_rows, e_rows,
    local_sems, c1_ssem, c1_rsem, c2_ssem, c2_rsem, m_ssem, m_rsem, h_ssem, h_rsem, x_ssem, x_rsem, z_ssem, z_rsem, p_ssem, p_rsem,
    s_ssem, s_rsem, o_ssem, o_rsem, r_ssem, r_rsem, a_ssem, a_rsem, b1_ssem, b1_rsem, b2_ssem, b2_rsem, f_ssem, f_rsem, e_ssem, e_rsem,
):
    got = (got_first, got_second)
    b1s = (b1_first, b1_second)
    b2s = (b2_first, b2_second)
    s = lax.axis_index("sector")
    q = lax.axis_index("axial")
    y = s // NZ
    z = s % NZ

    def x_peer(k):
        return (s, (q + k) % NAX)

    def y_peer(k):
        return (((y + k) % NY) * NZ + z, q)

    def z_peer(k):
        return (y * NZ + (z + k) % NZ, q)

    def s_peer(k):
        return ((s + k) % NSEC, q)

    def wait_for(ref, sem):
        pltpu.make_async_copy(ref, ref, sem).wait()

    def remote(src, dst, ssem, rsem, device):
        pltpu.make_async_remote_copy(
            src_ref=src, dst_ref=dst, send_sem=ssem, recv_sem=rsem,
            device_id=device, device_id_type=MESH,
        ).start()

    loads = [
        pltpu.make_async_copy(src, dst, local_sems.at[i])
        for i, (src, dst) in enumerate(
            ((rhs_hbm, rhs_ref), (basis_hbm, basis_ref), (mass_hbm, mass_ref), (bw_hbm, bw_ref))
        )
    ]
    for load in loads:
        load.start()

    barrier = pltpu.get_barrier_semaphore()
    for k in FAR_FIRST:
        for peer in (y_peer(k), z_peer(k), x_peer(k)):
            pl.semaphore_signal(barrier, inc=1, device_id=peer, device_id_type=MESH)
    for k in (1, NSEC - 1):
        pl.semaphore_signal(barrier, inc=1, device_id=s_peer(k), device_id_type=MESH)

    solver_copy = pltpu.make_async_copy(solver_hbm.at[0], solver, local_sems.at[4])
    solver_copy.start()

    def inverse_for(to):
        return inverse_hbm.at[:, pl.ds(pl.multiple_of(to * NZ * GS, NZ * GS), NZ * GS)]

    own_copy = pltpu.make_async_copy(inverse_for(y), inverse_y.at[y], local_sems.at[5])
    own_copy.start()

    lane = lax.broadcasted_iota(jnp.int32, (R, GS), 1)
    rotor = lax.broadcasted_iota(jnp.int32, (R, GS), 0)
    lane8 = lax.broadcasted_iota(jnp.int32, (8, GS), 1)
    row8 = lax.broadcasted_iota(jnp.int32, (8, GS), 0)
    rows128 = lax.broadcasted_iota(jnp.int32, (8 * NV, GS), 0) // NV
    for load in loads:
        load.wait()
    rhs = rhs_ref[...]
    r0 = [rhs[:, a, :] for a in range(GA)]
    basis_all = basis_ref[...].astype(F32)
    basis = [basis_all[:, a, :] for a in range(GA)]
    mass = [mass_ref[a : a + 1, :] + 4.0 for a in range(GA)]
    weight = bw_ref[...]
    shift = shift_ref[0]
    shift_z = shift % NZ
    up = (shift // NZ + jnp.where(z < shift_z, 1, 0)) % NY
    up_there = (shift // NZ + jnp.where(z + shift_z >= NZ, 1, 0)) % NY

    def spread(tile, at):
        return jnp.where(rows128 == at, jnp.concatenate([tile] * 8, axis=0), 0.0).astype(BF16)

    def each(tile):
        return jnp.concatenate([tile.astype(F32)] * 8, axis=0).astype(BF16)

    basis_q = jnp.concatenate([spread(t, q) for t in basis], axis=1)
    basis_each = jnp.concatenate([each(t) for t in basis], axis=1)

    def coarse_of(field):
        return joined(nt(two_parts(jnp.concatenate(field, axis=1)), basis_q))

    def packed(tile):
        kept = jnp.where(lane // NV == rotor % 8, tile, 0.0)
        return [jnp.sum(kept[8 * h : 8 * h + 8], axis=0, keepdims=True) for h in range(2)]

    def block_transposed(x):
        for d in (4, 2, 1):
            from_above = pltpu.roll(pltpu.roll(x, d, 0), GS - NV * d, 1)
            from_below = pltpu.roll(pltpu.roll(x, 8 - d, 0), NV * d, 1)
            row_bit = (row8 // d) % 2
            block_bit = (lane8 // (NV * d)) % 2
            x = jnp.where(row_bit == block_bit, x, jnp.where(row_bit == 1, from_above, from_below))
        return x

    def edges(field):
        tile = jnp.zeros((R, GS), F32)
        for a in range(GA):
            at = 2 * (a + 1)
            moved = pltpu.roll(field[a], at + 1, 1)
            tile = jnp.where((lane == at) | (lane == at + 1), moved, tile)
        return tile

    def send_halo(n, field):
        h_send[n, 0] = edges(field)
        h_send[n, 1] = field[0]
        h_send[n, 2] = field[GA - 1]
        remote(h_send.at[n, 0], h_recv.at[n, 0], h_ssem.at[n], h_rsem.at[n], s_peer(1))
        remote(h_send.at[n, 0], h_recv.at[n, 1], h_ssem.at[n], h_rsem.at[n], s_peer(NSEC - 1))
        remote(h_send.at[n, 2], h_recv.at[n, 2], h_ssem.at[n], h_rsem.at[n], x_peer(1))
        remote(h_send.at[n, 1], h_recv.at[n, 3], h_ssem.at[n], h_rsem.at[n], x_peer(NAX - 1))

    def get_halo(n):
        wait_for(h_recv.at[n], h_rsem.at[n])
        above = jnp.where(q == 0, 0.0, h_recv[n, 2])
        below = jnp.where(q == NAX - 1, 0.0, h_recv[n, 3])
        return h_recv[n, 0], h_recv[n, 1], above, below

    def local_solve(field, halo):
        left, right, above, below = halo
        stack = [above] + field + [below]
        moved = [pltpu.roll(stack[j], 2 * j + 1, 1) for j in range(GA + 2)]
        zero = jnp.zeros((R, GS), F32)
        parts = []
        for t in range(GA + 3):
            here = moved[t] if t < GA + 2 else zero
            before = moved[t - 1] if t > 0 else zero
            tile = jnp.where(lane == 2 * t - 1, right, before)
            tile = jnp.where(lane == 2 * t, left, tile)
            parts.append(jnp.where(lane > 2 * t, here, tile))
        window = jnp.concatenate(parts, axis=1)
        out = joined(nn(two_parts(window)[:, :NEXT], solver[...]))
        return [out[:, a * GS : (a + 1) * GS] for a in range(GA)]

    def apply_operator(field, halo, band):
        left, right, above, below = halo
        stack = [above] + field + [below]
        image = []
        for a in range(GA):
            u = field[a]
            before = jnp.where(lane == 0, pltpu.roll(left, GS - 2 * (a + 1), 1), pltpu.roll(u, 1, 1))
            after = jnp.where(
                lane == GS - 1, pltpu.roll(right, GS - 1 - (2 * a + 3), 1), pltpu.roll(u, GS - 1, 1)
            )
            value = mass[a] * u - ((stack[a + 2] + stack[a]) + before + after)
            if a == 0:
                value = value + weight * (u - band)
            image.append(value)
        return image

    def send_rows(slots, first, ssem, rsem, peer):
        slots[0] = first
        for k in FAR_FIRST:
            remote(slots.at[0], slots.at[k], ssem, rsem, peer(k))

    def get_rows(slots, sem, at):
        wait_for(slots.at[pl.ds(1, 7)], sem)
        return slots[at]

    def send_band(n, rows):
        send_rows(b1s[n], rows, b1_ssem.at[n], b1_rsem.at[n], z_peer if n == 0 else y_peer)

    def forward_band(n):
        row = get_rows(b1s[n], b1_rsem.at[n], shift_z if n == 0 else up_there)
        send_rows(b2s[n], row, b2_ssem.at[n], b2_rsem.at[n], y_peer if n == 0 else z_peer)

    def get_band(n):
        return get_rows(b2s[n], b2_rsem.at[n], up if n == 0 else shift_z)

    def send_x(coarse):
        x_send[...] = coarse
        for k in FAR_FIRST:
            remote(x_send, x_recv.at[k - 1], x_ssem, x_rsem, x_peer(k))

    def pass_z():
        wait_for(x_recv, x_rsem)
        total = x_send[...]
        for k in range(NAX - 1):
            total = total + x_recv[k]
        z_tiles[z] = total
        for k in FAR_FIRST:
            remote(z_tiles.at[z], z_tiles.at[z], z_ssem, z_rsem, z_peer(k))

    def get_z():
        wait_for(z_tiles.at[pl.ds(0, NZ - 1)], z_rsem)
        own_copy.wait()
        wait_for(inverse_y.at[pl.ds(0, NY - 1)], m_rsem)
        return jnp.concatenate([z_tiles[t] for t in range(NZ)], axis=1)

    def send_plane(field):
        out = joined(nt(two_parts(jnp.concatenate(field, axis=1)), basis_each))
        at = z * NAX + q
        for h, row in enumerate(packed(out)):
            plane[h, pl.ds(at, 1)] = row
        for j in FAR_FIRST + (0,):
            for i in FAR_FIRST + (0,):
                if i or j:
                    remote(
                        plane.at[:, pl.ds(at, 1)], plane.at[:, pl.ds(at, 1)],
                        p_ssem, p_rsem, (y * NZ + (z + j) % NZ, (q + i) % NAX),
                    )

    def get_plane():
        wait_for(plane.at[:, pl.ds(0, NZ * NAX - 1)], p_rsem)
        halves = [
            jnp.concatenate([block_transposed(plane[h, pl.ds(8 * t, 8)]) for t in range(NZ)], axis=1)
            for h in range(2)
        ]
        return jnp.concatenate(halves, axis=0)

    def send_shares(n, gathered):
        matrix = jnp.concatenate([inverse_y[t] for t in range(NY)], axis=0)
        out = joined(nt(two_parts(gathered), matrix))
        for h in range(2):
            share = block_transposed(out[8 * h : 8 * h + 8])
            band = pltpu.roll(share, up_there, 0)
            ahead = jnp.where(z == NZ - 1, pltpu.roll(share, 1, 0), share)
            behind = jnp.where(z == 0, pltpu.roll(share, NY - 1, 0), share)
            for i, own in enumerate((share, ahead, behind)):
                shares[n, i, h] = own
                shares[n, i, 2 + h] = band
        for h in range(4):
            got[n][h, z, pl.ds(y, 1)] = shares[n, 0, h, pl.ds(y, 1)]
        for i in FAR_FIRST + (0,):
            to = (y + i) % NY
            for j in FAR_FIRST + (0,):
                sector = (to * NZ + (z + j) % NZ, q)
                if j in (1, NZ - 1):
                    remote(
                        shares.at[n, 1 if j == 1 else 2, :, pl.ds(to, 1)], got[n].at[:, z, pl.ds(y, 1)],
                        s_ssem.at[n], s_rsem.at[n], sector,
                    )
                elif j:
                    remote(
                        shares.at[n, 0, pl.ds(2, 2), pl.ds(to, 1)], got[n].at[pl.ds(2, 2), z, pl.ds(y, 1)],
                        o_ssem.at[n], o_rsem.at[n], sector,
                    )
                elif i:
                    remote(
                        shares.at[n, 0, :, pl.ds(to, 1)], got[n].at[:, z, pl.ds(y, 1)],
                        r_ssem.at[n], r_rsem.at[n], sector,
                    )
            for side, k in enumerate((1, NAX - 1)):
                remote(
                    shares.at[n, 0, pl.ds(0, 2), pl.ds(to, 1)], beside.at[n, side, :, pl.ds(y, 1)],
                    a_ssem.at[n], a_rsem.at[n], (to * NZ + z, (q + k) % NAX),
                )

    def wait_shares(n, s_sem, o_sem, r_sem, a_sem):
        wait_for(got[n].at[:, pl.ds(0, 2)], s_sem.at[n])
        wait_for(got[n].at[pl.ds(0, 2), pl.ds(0, NZ - 3)], o_sem.at[n])
        wait_for(got[n].at[:, 0, pl.ds(0, NY - 1)], r_sem.at[n])
        wait_for(beside.at[n], a_sem.at[n])

    def unpacked(first, second):
        rows = [jnp.sum(x, axis=0, keepdims=True) for x in (first, second)]
        tile = jnp.concatenate([jnp.broadcast_to(x, (8, GS)) for x in rows], axis=0)
        return jnp.where(lane // NV == rotor % 8, tile, 0.0)

    def get_shares(n):
        wait_shares(n, s_rsem, o_rsem, r_rsem, a_rsem)

        def along_z(at, h=0):
            return unpacked(got[n][h, at], got[n][h + 1, at])

        sides = (
            along_z((z + NZ - 1) % NZ), along_z((z + 1) % NZ),
            unpacked(beside[n, 0, 0], beside[n, 0, 1]), unpacked(beside[n, 1, 0], beside[n, 1, 1]),
        )
        return along_z(z), sides, along_z((z + NZ - shift_z) % NZ, 2)

    def prolong(coarse, rows):
        out = joined(nn(two_parts(coarse), rows))
        return [out[:, i * GS : (i + 1) * GS] for i in range(rows.shape[1] // GS)]

    def inner_products(residual, image):
        cross = residual[0] * image[0]
        square = image[0] * image[0]
        for a in range(1, GA):
            cross = cross + residual[a] * image[a]
            square = square + image[a] * image[a]
        cross = jnp.sum(cross, axis=1, keepdims=True)
        square = jnp.sum(square, axis=1, keepdims=True)
        spread_out = jnp.where(lane == rotor, cross, jnp.where(lane == rotor + R, square, 0.0))
        return jnp.sum(spread_out, axis=0, keepdims=True)

    def send_inner(n, row):
        f_rows[n, pl.ds(NAX - 1, 1)] = row
        for k in FAR_FIRST:
            remote(
                f_rows.at[n, pl.ds(NAX - 1, 1)], f_rows.at[n, pl.ds(k - 1, 1)],
                f_ssem.at[n], f_rsem.at[n], x_peer(k),
            )

    def pass_inner(n):
        wait_for(f_rows.at[n, pl.ds(0, NAX - 1)], f_rsem.at[n])
        e_rows[n, pl.ds(NSEC - 1, 1)] = jnp.sum(f_rows[n], axis=0, keepdims=True)

        for i in FAR_FIRST + (0,):
            for j in FAR_FIRST + (0,):
                if i or j:
                    remote(
                        e_rows.at[n, pl.ds(NSEC - 1, 1)], e_rows.at[n, pl.ds(i * NZ + j - 1, 1)],
                        e_ssem.at[n], e_rsem.at[n], ((y + i) % NY * NZ + (z + j) % NZ, q),
                    )

    def get_step(n):
        wait_for(e_rows.at[n, pl.ds(0, NSEC - 1)], e_rsem.at[n])
        row = jnp.sum(e_rows[n], axis=0, keepdims=True)
        cross = jnp.sum(jnp.where(lane == rotor, row, 0.0), axis=1, keepdims=True)
        square = jnp.sum(jnp.where(lane == rotor + R, row, 0.0), axis=1, keepdims=True)
        return cross / (square + EPSILON)

    coarse_r0 = coarse_of(r0)

    pl.semaphore_wait(barrier, 7 + 7 + 7 + 2)

    send_x(coarse_r0)
    send_halo(0, r0)
    send_halo(4, basis)
    for k in FAR_FIRST:
        remote(inverse_for((y + k) % NY), inverse_y.at[y], m_ssem, m_rsem, y_peer(k))
    send_rows(c1, basis[0].astype(BF16), c1_ssem, c1_rsem, z_peer)
    pass_z()
    halo_r0 = get_halo(0)
    solver_copy.wait()
    local_r0 = local_solve(r0, halo_r0)
    send_band(0, local_r0[0])
    send_halo(1, local_r0)
    send_rows(c2, get_rows(c1, c1_rsem, shift_z), c2_ssem, c2_rsem, y_peer)
    send_shares(0, get_z())
    forward_band(0)
    basis_sides = [each(t) for t in get_halo(4)]
    halo = get_halo(1)
    band_row = get_band(0)
    band_basis = each(get_rows(c2, c2_rsem, up))

    def with_coarse(field, halo, band_row, n):
        coarse, sides, band = get_shares(n)
        own = [u + v for u, v in zip(field, prolong(coarse, basis_each))]
        around = [u + prolong(v, w)[0] for u, v, w in zip(halo, sides, basis_sides)]
        return own, around, band_row + prolong(band, band_basis)[0]

    corr0, halo, band_row = with_coarse(local_r0, halo, band_row, 0)
    image0 = apply_operator(corr0, halo, band_row)

    send_halo(2, image0)
    send_plane(image0)
    send_inner(0, inner_products(r0, image0))
    local_im = local_solve(image0, get_halo(2))
    send_band(1, local_im[0])
    send_halo(3, local_im)
    pass_inner(0)
    send_shares(1, get_plane())
    forward_band(1)
    step0 = get_step(0)
    res1 = [u - step0 * v for u, v in zip(r0, image0)]
    halo = get_halo(3)
    band_row = get_band(1)
    diff, halo, band_row = with_coarse(local_im, halo, band_row, 1)
    image_diff = apply_operator(diff, halo, band_row)
    corr1 = [u - step0 * v for u, v in zip(corr0, diff)]
    image1 = [u - step0 * v for u, v in zip(image0, image_diff)]

    send_inner(1, inner_products(res1, image1))
    pass_inner(1)
    step1 = get_step(1)
    for a in range(GA):
        out_ref[0, :, a, :] = step0 * corr0[a] + step1 * corr1[a]
        out_ref[1, :, a, :] = res1[a] - step1 * image1[a]

    wait_for(inverse_y.at[pl.ds(0, NY - 1)], m_ssem)
    wait_for(c1.at[pl.ds(1, 7)], c1_ssem)
    wait_for(c2.at[pl.ds(1, 7)], c2_ssem)
    wait_for(x_recv, x_ssem)
    wait_for(z_tiles.at[pl.ds(0, NZ - 1)], z_ssem)
    wait_for(plane.at[:, pl.ds(0, NZ * NAX - 1)], p_ssem)
    for n in range(5):
        wait_for(h_recv.at[n], h_ssem.at[n])
    for n in range(2):
        wait_shares(n, s_ssem, o_ssem, r_ssem, a_ssem)
        wait_for(b1s[n].at[pl.ds(1, NY - 1)], b1_ssem.at[n])
        wait_for(b2s[n].at[pl.ds(1, NZ - 1)], b2_ssem.at[n])
        wait_for(f_rows.at[n, pl.ds(0, NAX - 1)], f_ssem.at[n])
        wait_for(e_rows.at[n, pl.ds(0, NSEC - 1)], e_ssem.at[n])


def on_device(
    right_side, mass_term, band_weight, band_shift, local_solver, coarse_inverse, coarse_basis
):
    hbm = pl.BlockSpec(memory_space=pltpu.HBM)
    dma = pltpu.SemaphoreType.DMA

    def tiles(*shape):
        return pltpu.VMEM(shape + (GS,), F32)

    both = pl.pallas_call(
        body,
        name="schwarz_steps",
        out_shape=pltpu.VMEM((2,) + right_side.shape, F32),
        in_specs=[hbm, hbm, hbm, pl.BlockSpec(memory_space=pltpu.SMEM), hbm, hbm, hbm],
        out_specs=pl.BlockSpec(memory_space=pltpu.VMEM),
        scratch_shapes=[
            pltpu.VMEM(right_side.shape, F32),
            pltpu.VMEM(mass_term.shape, F32),
            pltpu.VMEM(band_weight.shape, F32),
            pltpu.VMEM(coarse_basis.shape, BF16),
            pltpu.VMEM((NEXT, GA * GS), BF16),
            pltpu.VMEM((NY, NV, NZ * GS), BF16),
            tiles(5, 3, R),
            tiles(5, 4, R),
            tiles(R),
            tiles(NAX - 1, R),
            tiles(NZ, R),
            tiles(2, NZ * NAX),
            tiles(2, 3, 4, NY),
            tiles(2, 2, 2, NY),
            tiles(4, NZ, NY),
            tiles(4, NZ, NY),
            tiles(NY, R),
            tiles(NY, R),
            tiles(NY, R),
            tiles(NZ, R),
            pltpu.VMEM((NZ, NV, GS), BF16),
            pltpu.VMEM((NY, NV, GS), BF16),
            tiles(2, NAX),
            tiles(2, NSEC),
            dma((6,)),
            dma,
            dma,
            dma,
            dma,
            dma,
            dma,
            dma((5,)),
            dma((5,)),
        ]
        + [dma] * 6
        + [dma((2,))] * 16,
        compiler_params=pltpu.CompilerParams(
            collective_id=0, has_side_effects=True, vmem_limit_bytes=60 << 20
        ),
    )(
        right_side, mass_term, band_weight, band_shift, coarse_basis,
        jnp.swapaxes(local_solver, 1, 2), coarse_inverse,
    )
    return both[0], both[1]


def solution(mesh):
    placed = (
        P(None, "axial", "sector"),
        P("axial", "sector"),
        P("axial", "sector"),
        P(),
        P("axial", "sector", None),
        P(("sector", "axial"), None),
        P(None, "axial", "sector"),
    )
    return jax.shard_map(
        on_device,
        mesh=mesh,
        in_specs=placed,
        out_specs=(P(None, "axial", "sector"), P(None, "axial", "sector")),
        check_vma=False,
    )
```

```python
import jax
import jax.numpy as jnp
from jax import lax
from jax.experimental import pallas as pl
from jax.experimental.pallas import tpu as pltpu
from jax.sharding import PartitionSpec as P

EPSILON = 1e-06
MESH = pl.DeviceIdType.MESH
F32 = jnp.float32
BF16 = jnp.bfloat16

R = 16
GA = 4
GS = 128
NV = 16
NEXT = 780
NZ = 8
NY = 8
NSEC = NY * NZ
NAX = 8
FAR_FIRST = (4, 3, 5, 2, 6, 1, 7)


def nt(a, b):
    return lax.dot_general(a, b, (((1,), (1,)), ((), ())), preferred_element_type=F32)


def nn(a, b):
    return lax.dot_general(a, b, (((1,), (0,)), ((), ())), preferred_element_type=F32)


def two_parts(x):
    high = x.astype(BF16)
    low = (x - high.astype(F32)).astype(BF16)
    return jnp.concatenate([high, low], axis=0)


def joined(x):
    half = x.shape[0] // 2
    return x[:half] + x[half:]


def body(
    rhs_hbm, mass_hbm, bw_hbm, shift_ref, basis_hbm, solver_hbm, inverse_hbm,
    out_ref,
    rhs_ref, mass_ref, bw_ref, basis_ref,
    solver, inverse_y, h_send, h_recv, x_send, x_recv, z_tiles, plane, shares, beside,
    got_first, got_second, b1_first, b1_second, b2_first, b2_second, c1, c2, f_rows, e_rows,
    local_sems, c1_ssem, c1_rsem, c2_ssem, c2_rsem, m_ssem, m_rsem, h_ssem, h_rsem, x_ssem, x_rsem, z_ssem, z_rsem, p_ssem, p_rsem,
    s_ssem, s_rsem, o_ssem, o_rsem, r_ssem, r_rsem, a_ssem, a_rsem, b1_ssem, b1_rsem, b2_ssem, b2_rsem, f_ssem, f_rsem, e_ssem, e_rsem,
):
    got = (got_first, got_second)
    b1s = (b1_first, b1_second)
    b2s = (b2_first, b2_second)
    s = lax.axis_index("sector")
    q = lax.axis_index("axial")
    y = s // NZ
    z = s % NZ

    def x_peer(k):
        return (s, (q + k) % NAX)

    def y_peer(k):
        return (((y + k) % NY) * NZ + z, q)

    def z_peer(k):
        return (y * NZ + (z + k) % NZ, q)

    def s_peer(k):
        return ((s + k) % NSEC, q)

    def wait_for(ref, sem):
        pltpu.make_async_copy(ref, ref, sem).wait()

    def remote(src, dst, ssem, rsem, device):
        pltpu.make_async_remote_copy(
            src_ref=src, dst_ref=dst, send_sem=ssem, recv_sem=rsem,
            device_id=device, device_id_type=MESH,
        ).start()

    barrier = pltpu.get_barrier_semaphore()
    for k in FAR_FIRST:
        for peer in (y_peer(k), z_peer(k), x_peer(k)):
            pl.semaphore_signal(barrier, inc=1, device_id=peer, device_id_type=MESH)
    for k in (1, NSEC - 1):
        pl.semaphore_signal(barrier, inc=1, device_id=s_peer(k), device_id_type=MESH)

    loads = [
        pltpu.make_async_copy(src, dst, local_sems.at[i])
        for i, (src, dst) in enumerate(
            ((rhs_hbm, rhs_ref), (basis_hbm, basis_ref), (mass_hbm, mass_ref), (bw_hbm, bw_ref))
        )
    ]
    for load in loads:
        load.start()
    solver_copy = pltpu.make_async_copy(solver_hbm.at[0], solver, local_sems.at[4])
    solver_copy.start()

    def inverse_for(to):
        return inverse_hbm.at[:, pl.ds(pl.multiple_of(to * NZ * GS, NZ * GS), NZ * GS)]

    own_copy = pltpu.make_async_copy(inverse_for(y), inverse_y.at[y], local_sems.at[5])
    own_copy.start()

    lane = lax.broadcasted_iota(jnp.int32, (R, GS), 1)
    rotor = lax.broadcasted_iota(jnp.int32, (R, GS), 0)
    lane8 = lax.broadcasted_iota(jnp.int32, (8, GS), 1)
    row8 = lax.broadcasted_iota(jnp.int32, (8, GS), 0)
    rows128 = lax.broadcasted_iota(jnp.int32, (8 * NV, GS), 0) // NV
    for load in loads:
        load.wait()
    rhs = rhs_ref[...]
    r0 = [rhs[:, a, :] for a in range(GA)]
    basis_all = basis_ref[...].astype(F32)
    basis = [basis_all[:, a, :] for a in range(GA)]
    mass = [mass_ref[a : a + 1, :] + 4.0 for a in range(GA)]
    weight = bw_ref[...]
    shift = shift_ref[0]
    shift_z = shift % NZ
    up = (shift // NZ + jnp.where(z < shift_z, 1, 0)) % NY
    up_there = (shift // NZ + jnp.where(z + shift_z >= NZ, 1, 0)) % NY

    def spread(tile, at):
        return jnp.where(rows128 == at, jnp.concatenate([tile] * 8, axis=0), 0.0).astype(BF16)

    def each(tile):
        return jnp.concatenate([tile.astype(F32)] * 8, axis=0).astype(BF16)

    basis_q = jnp.concatenate([spread(t, q) for t in basis], axis=1)

    def coarse_of(field):
        return joined(nt(two_parts(jnp.concatenate(field, axis=1)), basis_q))

    def packed(tile):
        kept = jnp.where(lane // NV == rotor % 8, tile, 0.0)
        return [jnp.sum(kept[8 * h : 8 * h + 8], axis=0, keepdims=True) for h in range(2)]

    def block_transposed(x):
        for d in (4, 2, 1):
            from_above = pltpu.roll(pltpu.roll(x, d, 0), GS - NV * d, 1)
            from_below = pltpu.roll(pltpu.roll(x, 8 - d, 0), NV * d, 1)
            row_bit = (row8 // d) % 2
            block_bit = (lane8 // (NV * d)) % 2
            x = jnp.where(row_bit == block_bit, x, jnp.where(row_bit == 1, from_above, from_below))
        return x

    def edges(field):
        tile = jnp.zeros((R, GS), F32)
        for a in range(GA):
            at = 2 * (a + 1)
            moved = pltpu.roll(field[a], at + 1, 1)
            tile = jnp.where((lane == at) | (lane == at + 1), moved, tile)
        return tile

    def send_halo(n, field):
        h_send[n, 0] = edges(field)
        h_send[n, 1] = field[0]
        h_send[n, 2] = field[GA - 1]
        remote(h_send.at[n, 0], h_recv.at[n, 0], h_ssem.at[n], h_rsem.at[n], s_peer(1))
        remote(h_send.at[n, 0], h_recv.at[n, 1], h_ssem.at[n], h_rsem.at[n], s_peer(NSEC - 1))
        remote(h_send.at[n, 2], h_recv.at[n, 2], h_ssem.at[n], h_rsem.at[n], x_peer(1))
        remote(h_send.at[n, 1], h_recv.at[n, 3], h_ssem.at[n], h_rsem.at[n], x_peer(NAX - 1))

    def get_halo(n):
        wait_for(h_recv.at[n], h_rsem.at[n])
        above = jnp.where(q == 0, 0.0, h_recv[n, 2])
        below = jnp.where(q == NAX - 1, 0.0, h_recv[n, 3])
        return h_recv[n, 0], h_recv[n, 1], above, below

    def local_solve(field, halo):
        left, right, above, below = halo
        stack = [above] + field + [below]
        moved = [pltpu.roll(stack[j], 2 * j + 1, 1) for j in range(GA + 2)]
        zero = jnp.zeros((R, GS), F32)
        parts = []
        for t in range(GA + 3):
            here = moved[t] if t < GA + 2 else zero
            before = moved[t - 1] if t > 0 else zero
            tile = jnp.where(lane == 2 * t - 1, right, before)
            tile = jnp.where(lane == 2 * t, left, tile)
            parts.append(jnp.where(lane > 2 * t, here, tile))
        window = jnp.concatenate(parts, axis=1)
        out = joined(nn(two_parts(window)[:, :NEXT], solver[...]))
        return [out[:, a * GS : (a + 1) * GS] for a in range(GA)]

    def apply_operator(field, halo, band):
        left, right, above, below = halo
        stack = [above] + field + [below]
        image = []
        for a in range(GA):
            u = field[a]
            before = jnp.where(lane == 0, pltpu.roll(left, GS - 2 * (a + 1), 1), pltpu.roll(u, 1, 1))
            after = jnp.where(
                lane == GS - 1, pltpu.roll(right, GS - 1 - (2 * a + 3), 1), pltpu.roll(u, GS - 1, 1)
            )
            value = mass[a] * u - ((stack[a + 2] + stack[a]) + before + after)
            if a == 0:
                value = value + weight * (u - band)
            image.append(value)
        return image

    def send_rows(slots, first, ssem, rsem, peer):
        slots[0] = first
        for k in FAR_FIRST:
            remote(slots.at[0], slots.at[k], ssem, rsem, peer(k))

    def get_rows(slots, sem, at):
        wait_for(slots.at[pl.ds(1, 7)], sem)
        return slots[at]

    def send_band(n, rows):
        send_rows(b1s[n], rows, b1_ssem.at[n], b1_rsem.at[n], z_peer if n == 0 else y_peer)

    def forward_band(n):
        row = get_rows(b1s[n], b1_rsem.at[n], shift_z if n == 0 else up_there)
        send_rows(b2s[n], row, b2_ssem.at[n], b2_rsem.at[n], y_peer if n == 0 else z_peer)

    def get_band(n):
        return get_rows(b2s[n], b2_rsem.at[n], up if n == 0 else shift_z)

    def send_x(coarse):
        x_send[...] = coarse
        for k in FAR_FIRST:
            remote(x_send, x_recv.at[k - 1], x_ssem, x_rsem, x_peer(k))

    def pass_z():
        wait_for(x_recv, x_rsem)
        total = x_send[...]
        for k in range(NAX - 1):
            total = total + x_recv[k]
        z_tiles[z] = total
        for k in FAR_FIRST:
            remote(z_tiles.at[z], z_tiles.at[z], z_ssem, z_rsem, z_peer(k))

    def get_z():
        wait_for(z_tiles.at[pl.ds(0, NZ - 1)], z_rsem)
        own_copy.wait()
        wait_for(inverse_y.at[pl.ds(0, NY - 1)], m_rsem)
        return jnp.concatenate([z_tiles[t] for t in range(NZ)], axis=1)

    def send_plane(field):
        out = joined(nt(two_parts(jnp.concatenate(field, axis=1)), basis_each))
        at = z * NAX + q
        for h, row in enumerate(packed(out)):
            plane[h, pl.ds(at, 1)] = row
        for j in FAR_FIRST + (0,):
            for i in FAR_FIRST + (0,):
                if i or j:
                    remote(
                        plane.at[:, pl.ds(at, 1)], plane.at[:, pl.ds(at, 1)],
                        p_ssem, p_rsem, (y * NZ + (z + j) % NZ, (q + i) % NAX),
                    )

    def get_plane():
        wait_for(plane.at[:, pl.ds(0, NZ * NAX - 1)], p_rsem)
        halves = [
            jnp.concatenate([block_transposed(plane[h, pl.ds(8 * t, 8)]) for t in range(NZ)], axis=1)
            for h in range(2)
        ]
        return jnp.concatenate(halves, axis=0)

    def send_shares(n, gathered):
        matrix = jnp.concatenate([inverse_y[t] for t in range(NY)], axis=0)
        out = joined(nt(two_parts(gathered), matrix))
        for h in range(2):
            share = block_transposed(out[8 * h : 8 * h + 8])
            band = pltpu.roll(share, up_there, 0)
            ahead = jnp.where(z == NZ - 1, pltpu.roll(share, 1, 0), share)
            behind = jnp.where(z == 0, pltpu.roll(share, NY - 1, 0), share)
            for i, own in enumerate((share, ahead, behind)):
                shares[n, i, h] = own
                shares[n, i, 2 + h] = band
        for h in range(4):
            got[n][h, z, pl.ds(y, 1)] = shares[n, 0, h, pl.ds(y, 1)]
        for i in FAR_FIRST + (0,):
            to = (y + i) % NY
            for j in FAR_FIRST + (0,):
                sector = (to * NZ + (z + j) % NZ, q)
                if j in (1, NZ - 1):
                    remote(
                        shares.at[n, 1 if j == 1 else 2, :, pl.ds(to, 1)], got[n].at[:, z, pl.ds(y, 1)],
                        s_ssem.at[n], s_rsem.at[n], sector,
                    )
                elif j:
                    remote(
                        shares.at[n, 0, pl.ds(2, 2), pl.ds(to, 1)], got[n].at[pl.ds(2, 2), z, pl.ds(y, 1)],
                        o_ssem.at[n], o_rsem.at[n], sector,
                    )
                elif i:
                    remote(
                        shares.at[n, 0, :, pl.ds(to, 1)], got[n].at[:, z, pl.ds(y, 1)],
                        r_ssem.at[n], r_rsem.at[n], sector,
                    )
            for side, k in enumerate((1, NAX - 1)):
                remote(
                    shares.at[n, 0, pl.ds(0, 2), pl.ds(to, 1)], beside.at[n, side, :, pl.ds(y, 1)],
                    a_ssem.at[n], a_rsem.at[n], (to * NZ + z, (q + k) % NAX),
                )

    def wait_shares(n, s_sem, o_sem, r_sem, a_sem):
        wait_for(got[n].at[:, pl.ds(0, 2)], s_sem.at[n])
        wait_for(got[n].at[pl.ds(0, 2), pl.ds(0, NZ - 3)], o_sem.at[n])
        wait_for(got[n].at[:, 0, pl.ds(0, NY - 1)], r_sem.at[n])
        wait_for(beside.at[n], a_sem.at[n])

    def unpacked(first, second):
        rows = [jnp.sum(x, axis=0, keepdims=True) for x in (first, second)]
        tile = jnp.concatenate([jnp.broadcast_to(x, (8, GS)) for x in rows], axis=0)
        return jnp.where(lane // NV == rotor % 8, tile, 0.0)

    def get_shares(n):
        wait_shares(n, s_rsem, o_rsem, r_rsem, a_rsem)

        def along_z(at, h=0):
            return unpacked(got[n][h, at], got[n][h + 1, at])

        sides = (
            along_z((z + NZ - 1) % NZ), along_z((z + 1) % NZ),
            unpacked(beside[n, 0, 0], beside[n, 0, 1]), unpacked(beside[n, 1, 0], beside[n, 1, 1]),
        )
        return along_z(z), sides, along_z((z + NZ - shift_z) % NZ, 2)

    def prolong(coarse, rows):
        out = joined(nn(two_parts(coarse), rows))
        return [out[:, i * GS : (i + 1) * GS] for i in range(rows.shape[1] // GS)]

    def inner_products(residual, image):
        cross = residual[0] * image[0]
        square = image[0] * image[0]
        for a in range(1, GA):
            cross = cross + residual[a] * image[a]
            square = square + image[a] * image[a]
        cross = jnp.sum(cross, axis=1, keepdims=True)
        square = jnp.sum(square, axis=1, keepdims=True)
        spread_out = jnp.where(lane == rotor, cross, jnp.where(lane == rotor + R, square, 0.0))
        return jnp.sum(spread_out, axis=0, keepdims=True)

    def send_inner(n, row):
        f_rows[n, pl.ds(NAX - 1, 1)] = row
        for k in FAR_FIRST:
            remote(
                f_rows.at[n, pl.ds(NAX - 1, 1)], f_rows.at[n, pl.ds(k - 1, 1)],
                f_ssem.at[n], f_rsem.at[n], x_peer(k),
            )

    def pass_inner(n):
        wait_for(f_rows.at[n, pl.ds(0, NAX - 1)], f_rsem.at[n])
        e_rows[n, pl.ds(NSEC - 1, 1)] = jnp.sum(f_rows[n], axis=0, keepdims=True)

        for i in FAR_FIRST + (0,):
            for j in FAR_FIRST + (0,):
                if i or j:
                    remote(
                        e_rows.at[n, pl.ds(NSEC - 1, 1)], e_rows.at[n, pl.ds(i * NZ + j - 1, 1)],
                        e_ssem.at[n], e_rsem.at[n], ((y + i) % NY * NZ + (z + j) % NZ, q),
                    )

    def get_step(n):
        wait_for(e_rows.at[n, pl.ds(0, NSEC - 1)], e_rsem.at[n])
        row = jnp.sum(e_rows[n], axis=0, keepdims=True)
        cross = jnp.sum(jnp.where(lane == rotor, row, 0.0), axis=1, keepdims=True)
        square = jnp.sum(jnp.where(lane == rotor + R, row, 0.0), axis=1, keepdims=True)
        return cross / (square + EPSILON)

    coarse_r0 = coarse_of(r0)

    pl.semaphore_wait(barrier, 7 + 7 + 7 + 2)

    send_x(coarse_r0)
    send_halo(0, r0)
    for k in FAR_FIRST:
        remote(inverse_for((y + k) % NY), inverse_y.at[y], m_ssem, m_rsem, y_peer(k))
    send_rows(c1, basis[0].astype(BF16), c1_ssem, c1_rsem, z_peer)
    send_halo(4, basis)
    pass_z()
    basis_each = jnp.concatenate([each(t) for t in basis], axis=1)
    halo_r0 = get_halo(0)
    solver_copy.wait()
    local_r0 = local_solve(r0, halo_r0)
    send_band(0, local_r0[0])
    send_halo(1, local_r0)
    send_rows(c2, get_rows(c1, c1_rsem, shift_z), c2_ssem, c2_rsem, y_peer)
    send_shares(0, get_z())
    forward_band(0)
    basis_sides = [each(t) for t in get_halo(4)]
    halo = get_halo(1)
    band_row = get_band(0)
    band_basis = each(get_rows(c2, c2_rsem, up))

    def with_coarse(field, halo, band_row, n):
        coarse, sides, band = get_shares(n)
        own = [u + v for u, v in zip(field, prolong(coarse, basis_each))]
        around = [u + prolong(v, w)[0] for u, v, w in zip(halo, sides, basis_sides)]
        return own, around, band_row + prolong(band, band_basis)[0]

    corr0, halo, band_row = with_coarse(local_r0, halo, band_row, 0)
    image0 = apply_operator(corr0, halo, band_row)

    send_halo(2, image0)
    send_plane(image0)
    send_inner(0, inner_products(r0, image0))
    local_im = local_solve(image0, get_halo(2))
    send_band(1, local_im[0])
    send_halo(3, local_im)
    pass_inner(0)
    send_shares(1, get_plane())
    forward_band(1)
    step0 = get_step(0)
    res1 = [u - step0 * v for u, v in zip(r0, image0)]
    halo = get_halo(3)
    band_row = get_band(1)
    diff, halo, band_row = with_coarse(local_im, halo, band_row, 1)
    image_diff = apply_operator(diff, halo, band_row)
    corr1 = [u - step0 * v for u, v in zip(corr0, diff)]
    image1 = [u - step0 * v for u, v in zip(image0, image_diff)]

    send_inner(1, inner_products(res1, image1))
    pass_inner(1)
    step1 = get_step(1)
    for a in range(GA):
        out_ref[0, :, a, :] = step0 * corr0[a] + step1 * corr1[a]
        out_ref[1, :, a, :] = res1[a] - step1 * image1[a]

    wait_for(inverse_y.at[pl.ds(0, NY - 1)], m_ssem)
    wait_for(c1.at[pl.ds(1, 7)], c1_ssem)
    wait_for(c2.at[pl.ds(1, 7)], c2_ssem)
    wait_for(x_recv, x_ssem)
    wait_for(z_tiles.at[pl.ds(0, NZ - 1)], z_ssem)
    wait_for(plane.at[:, pl.ds(0, NZ * NAX - 1)], p_ssem)
    for n in range(5):
        wait_for(h_recv.at[n], h_ssem.at[n])
    for n in range(2):
        wait_shares(n, s_ssem, o_ssem, r_ssem, a_ssem)
        wait_for(b1s[n].at[pl.ds(1, NY - 1)], b1_ssem.at[n])
        wait_for(b2s[n].at[pl.ds(1, NZ - 1)], b2_ssem.at[n])
        wait_for(f_rows.at[n, pl.ds(0, NAX - 1)], f_ssem.at[n])
        wait_for(e_rows.at[n, pl.ds(0, NSEC - 1)], e_ssem.at[n])


def on_device(
    right_side, mass_term, band_weight, band_shift, local_solver, coarse_inverse, coarse_basis
):
    hbm = pl.BlockSpec(memory_space=pltpu.HBM)
    dma = pltpu.SemaphoreType.DMA

    def tiles(*shape):
        return pltpu.VMEM(shape + (GS,), F32)

    both = pl.pallas_call(
        body,
        name="schwarz_steps",
        out_shape=pltpu.VMEM((2,) + right_side.shape, F32),
        in_specs=[hbm, hbm, hbm, pl.BlockSpec(memory_space=pltpu.SMEM), hbm, hbm, hbm],
        out_specs=pl.BlockSpec(memory_space=pltpu.VMEM),
        scratch_shapes=[
            pltpu.VMEM(right_side.shape, F32),
            pltpu.VMEM(mass_term.shape, F32),
            pltpu.VMEM(band_weight.shape, F32),
            pltpu.VMEM(coarse_basis.shape, BF16),
            pltpu.VMEM((NEXT, GA * GS), BF16),
            pltpu.VMEM((NY, NV, NZ * GS), BF16),
            tiles(5, 3, R),
            tiles(5, 4, R),
            tiles(R),
            tiles(NAX - 1, R),
            tiles(NZ, R),
            tiles(2, NZ * NAX),
            tiles(2, 3, 4, NY),
            tiles(2, 2, 2, NY),
            tiles(4, NZ, NY),
            tiles(4, NZ, NY),
            tiles(NY, R),
            tiles(NY, R),
            tiles(NY, R),
            tiles(NZ, R),
            pltpu.VMEM((NZ, NV, GS), BF16),
            pltpu.VMEM((NY, NV, GS), BF16),
            tiles(2, NAX),
            tiles(2, NSEC),
            dma((6,)),
            dma,
            dma,
            dma,
            dma,
            dma,
            dma,
            dma((5,)),
            dma((5,)),
        ]
        + [dma] * 6
        + [dma((2,))] * 16,
        compiler_params=pltpu.CompilerParams(
            collective_id=0, has_side_effects=True, vmem_limit_bytes=60 << 20
        ),
    )(
        right_side, mass_term, band_weight, band_shift, coarse_basis,
        jnp.swapaxes(local_solver, 1, 2), coarse_inverse,
    )
    return both[0], both[1]


def solution(mesh):
    placed = (
        P(None, "axial", "sector"),
        P("axial", "sector"),
        P("axial", "sector"),
        P(),
        P("axial", "sector", None),
        P(("sector", "axial"), None),
        P(None, "axial", "sector"),
    )
    return jax.shard_map(
        on_device,
        mesh=mesh,
        in_specs=placed,
        out_specs=(P(None, "axial", "sector"), P(None, "axial", "sector")),
        check_vma=False,
    )
```

```python
import jax
import jax.numpy as jnp
from jax import lax
from jax.experimental import pallas as pl
from jax.experimental.pallas import tpu as pltpu
from jax.sharding import PartitionSpec as P

EPSILON = 1e-06
MESH = pl.DeviceIdType.MESH
F32 = jnp.float32
BF16 = jnp.bfloat16

R = 16
GA = 4
GS = 128
NV = 16
NEXT = 780
NZ = 8
NY = 8
NSEC = NY * NZ
NAX = 8
FAR_FIRST = (4, 3, 5, 2, 6, 1, 7)


def nt(a, b):
    return lax.dot_general(a, b, (((1,), (1,)), ((), ())), preferred_element_type=F32)


def nn(a, b):
    return lax.dot_general(a, b, (((1,), (0,)), ((), ())), preferred_element_type=F32)


def two_parts(x):
    high = x.astype(BF16)
    low = (x - high.astype(F32)).astype(BF16)
    return jnp.concatenate([high, low], axis=0)


def joined(x):
    half = x.shape[0] // 2
    return x[:half] + x[half:]


def body(
    rhs_hbm, mass_hbm, bw_hbm, shift_ref, basis_hbm, solver_hbm, inverse_hbm,
    out_ref,
    rhs_ref, mass_ref, bw_ref, basis_ref,
    solver, inverse_y, h_send, h_recv, x_send, x_recv, z_tiles, plane, shares, beside,
    got_first, got_second, b1_first, b1_second, b2_first, b2_second, c1, c2, f_rows, e_rows,
    local_sems, c1_ssem, c1_rsem, c2_ssem, c2_rsem, m_ssem, m_rsem, h_ssem, h_rsem, x_ssem, x_rsem, z_ssem, z_rsem, p_ssem, p_rsem,
    s_ssem, s_rsem, o_ssem, o_rsem, r_ssem, r_rsem, a_ssem, a_rsem, b1_ssem, b1_rsem, b2_ssem, b2_rsem, f_ssem, f_rsem, e_ssem, e_rsem,
):
    got = (got_first, got_second)
    b1s = (b1_first, b1_second)
    b2s = (b2_first, b2_second)
    s = lax.axis_index("sector")
    q = lax.axis_index("axial")
    y = s // NZ
    z = s % NZ

    def x_peer(k):
        return (s, (q + k) % NAX)

    def y_peer(k):
        return (((y + k) % NY) * NZ + z, q)

    def z_peer(k):
        return (y * NZ + (z + k) % NZ, q)

    def s_peer(k):
        return ((s + k) % NSEC, q)

    def wait_for(ref, sem):
        pltpu.make_async_copy(ref, ref, sem).wait()

    def remote(src, dst, ssem, rsem, device):
        pltpu.make_async_remote_copy(
            src_ref=src, dst_ref=dst, send_sem=ssem, recv_sem=rsem,
            device_id=device, device_id_type=MESH,
        ).start()

    barrier = pltpu.get_barrier_semaphore()
    for k in FAR_FIRST:
        for peer in (y_peer(k), z_peer(k), x_peer(k)):
            pl.semaphore_signal(barrier, inc=1, device_id=peer, device_id_type=MESH)
    for k in (1, NSEC - 1):
        pl.semaphore_signal(barrier, inc=1, device_id=s_peer(k), device_id_type=MESH)

    loads = [
        pltpu.make_async_copy(src, dst, local_sems.at[i])
        for i, (src, dst) in enumerate(
            ((rhs_hbm, rhs_ref), (basis_hbm, basis_ref), (mass_hbm, mass_ref), (bw_hbm, bw_ref))
        )
    ]
    for load in loads:
        load.start()
    solver_copy = pltpu.make_async_copy(solver_hbm.at[0], solver, local_sems.at[4])
    solver_copy.start()

    def inverse_for(to):
        return inverse_hbm.at[:, pl.ds(pl.multiple_of(to * NZ * GS, NZ * GS), NZ * GS)]

    own_copy = pltpu.make_async_copy(inverse_for(y), inverse_y.at[y], local_sems.at[5])
    own_copy.start()

    lane = lax.broadcasted_iota(jnp.int32, (R, GS), 1)
    rotor = lax.broadcasted_iota(jnp.int32, (R, GS), 0)
    lane8 = lax.broadcasted_iota(jnp.int32, (8, GS), 1)
    row8 = lax.broadcasted_iota(jnp.int32, (8, GS), 0)
    rows128 = lax.broadcasted_iota(jnp.int32, (8 * NV, GS), 0) // NV
    for load in loads:
        load.wait()
    rhs = rhs_ref[...]
    r0 = [rhs[:, a, :] for a in range(GA)]
    basis_all = basis_ref[...].astype(F32)
    basis = [basis_all[:, a, :] for a in range(GA)]
    mass = [mass_ref[a : a + 1, :] + 4.0 for a in range(GA)]
    weight = bw_ref[...]
    shift = shift_ref[0]
    shift_z = shift % NZ
    up = (shift // NZ + jnp.where(z < shift_z, 1, 0)) % NY
    up_there = (shift // NZ + jnp.where(z + shift_z >= NZ, 1, 0)) % NY

    def spread(tile, at):
        return jnp.where(rows128 == at, jnp.concatenate([tile] * 8, axis=0), 0.0).astype(BF16)

    def each(tile):
        return jnp.concatenate([tile.astype(F32)] * 8, axis=0).astype(BF16)

    basis_q = jnp.concatenate([spread(t, q) for t in basis], axis=1)

    def coarse_of(field):
        return joined(nt(two_parts(jnp.concatenate(field, axis=1)), basis_q))

    def packed(tile):
        kept = jnp.where(lane // NV == rotor % 8, tile, 0.0)
        return [jnp.sum(kept[8 * h : 8 * h + 8], axis=0, keepdims=True) for h in range(2)]

    def block_transposed(x):
        for d in (4, 2, 1):
            from_above = pltpu.roll(pltpu.roll(x, d, 0), GS - NV * d, 1)
            from_below = pltpu.roll(pltpu.roll(x, 8 - d, 0), NV * d, 1)
            row_bit = (row8 // d) % 2
            block_bit = (lane8 // (NV * d)) % 2
            x = jnp.where(row_bit == block_bit, x, jnp.where(row_bit == 1, from_above, from_below))
        return x

    def edges(field):
        tile = jnp.zeros((R, GS), F32)
        for a in range(GA):
            at = 2 * (a + 1)
            moved = pltpu.roll(field[a], at + 1, 1)
            tile = jnp.where((lane == at) | (lane == at + 1), moved, tile)
        return tile

    def send_halo(n, field):
        h_send[n, 0] = edges(field)
        h_send[n, 1] = field[0]
        h_send[n, 2] = field[GA - 1]
        remote(h_send.at[n, 0], h_recv.at[n, 0], h_ssem.at[n], h_rsem.at[n], s_peer(1))
        remote(h_send.at[n, 0], h_recv.at[n, 1], h_ssem.at[n], h_rsem.at[n], s_peer(NSEC - 1))
        remote(h_send.at[n, 2], h_recv.at[n, 2], h_ssem.at[n], h_rsem.at[n], x_peer(1))
        remote(h_send.at[n, 1], h_recv.at[n, 3], h_ssem.at[n], h_rsem.at[n], x_peer(NAX - 1))

    def get_halo(n):
        wait_for(h_recv.at[n], h_rsem.at[n])
        above = jnp.where(q == 0, 0.0, h_recv[n, 2])
        below = jnp.where(q == NAX - 1, 0.0, h_recv[n, 3])
        return h_recv[n, 0], h_recv[n, 1], above, below

    def local_solve(field, halo):
        left, right, above, below = halo
        stack = [above] + field + [below]
        moved = [pltpu.roll(stack[j], 2 * j + 1, 1) for j in range(GA + 2)]
        zero = jnp.zeros((R, GS), F32)
        parts = []
        for t in range(GA + 3):
            here = moved[t] if t < GA + 2 else zero
            before = moved[t - 1] if t > 0 else zero
            tile = jnp.where(lane == 2 * t - 1, right, before)
            tile = jnp.where(lane == 2 * t, left, tile)
            parts.append(jnp.where(lane > 2 * t, here, tile))
        window = jnp.concatenate(parts, axis=1)
        out = joined(nn(two_parts(window)[:, :NEXT], solver[...]))
        return [out[:, a * GS : (a + 1) * GS] for a in range(GA)]

    def apply_operator(field, halo, band):
        left, right, above, below = halo
        stack = [above] + field + [below]
        image = []
        for a in range(GA):
            u = field[a]
            before = jnp.where(lane == 0, pltpu.roll(left, GS - 2 * (a + 1), 1), pltpu.roll(u, 1, 1))
            after = jnp.where(
                lane == GS - 1, pltpu.roll(right, GS - 1 - (2 * a + 3), 1), pltpu.roll(u, GS - 1, 1)
            )
            value = mass[a] * u - ((stack[a + 2] + stack[a]) + before + after)
            if a == 0:
                value = value + weight * (u - band)
            image.append(value)
        return image

    def send_rows(slots, first, ssem, rsem, peer):
        slots[0] = first
        for k in FAR_FIRST:
            remote(slots.at[0], slots.at[k], ssem, rsem, peer(k))

    def get_rows(slots, sem, at):
        wait_for(slots.at[pl.ds(1, 7)], sem)
        return slots[at]

    def send_band(n, rows):
        send_rows(b1s[n], rows, b1_ssem.at[n], b1_rsem.at[n], z_peer if n == 0 else y_peer)

    def forward_band(n):
        row = get_rows(b1s[n], b1_rsem.at[n], shift_z if n == 0 else up_there)
        send_rows(b2s[n], row, b2_ssem.at[n], b2_rsem.at[n], y_peer if n == 0 else z_peer)

    def get_band(n):
        return get_rows(b2s[n], b2_rsem.at[n], up if n == 0 else shift_z)

    def send_x(coarse):
        x_send[...] = coarse
        for k in FAR_FIRST:
            remote(x_send, x_recv.at[k - 1], x_ssem, x_rsem, x_peer(k))

    def pass_z():
        wait_for(x_recv, x_rsem)
        total = x_send[...]
        for k in range(NAX - 1):
            total = total + x_recv[k]
        z_tiles[z] = total
        for k in FAR_FIRST:
            remote(z_tiles.at[z], z_tiles.at[z], z_ssem, z_rsem, z_peer(k))

    def get_z():
        wait_for(z_tiles.at[pl.ds(0, NZ - 1)], z_rsem)
        own_copy.wait()
        wait_for(inverse_y.at[pl.ds(0, NY - 1)], m_rsem)
        return jnp.concatenate([z_tiles[t] for t in range(NZ)], axis=1)

    def send_plane(field):
        out = joined(nt(two_parts(jnp.concatenate(field, axis=1)), basis_each))
        at = z * NAX + q
        for h, row in enumerate(packed(out)):
            plane[h, pl.ds(at, 1)] = row
        for j in FAR_FIRST + (0,):
            for i in FAR_FIRST + (0,):
                if i or j:
                    remote(
                        plane.at[:, pl.ds(at, 1)], plane.at[:, pl.ds(at, 1)],
                        p_ssem, p_rsem, (y * NZ + (z + j) % NZ, (q + i) % NAX),
                    )

    def get_plane():
        wait_for(plane.at[:, pl.ds(0, NZ * NAX - 1)], p_rsem)
        halves = [
            jnp.concatenate([block_transposed(plane[h, pl.ds(8 * t, 8)]) for t in range(NZ)], axis=1)
            for h in range(2)
        ]
        return jnp.concatenate(halves, axis=0)

    def send_shares(n, gathered):
        matrix = jnp.concatenate([inverse_y[t] for t in range(NY)], axis=0)
        out = joined(nt(two_parts(gathered), matrix))
        for h in range(2):
            share = block_transposed(out[8 * h : 8 * h + 8])
            band = pltpu.roll(share, up_there, 0)
            ahead = jnp.where(z == NZ - 1, pltpu.roll(share, 1, 0), share)
            behind = jnp.where(z == 0, pltpu.roll(share, NY - 1, 0), share)
            for i, own in enumerate((share, ahead, behind)):
                shares[n, i, h] = own
                shares[n, i, 2 + h] = band
        for h in range(4):
            got[n][h, z, pl.ds(y, 1)] = shares[n, 0, h, pl.ds(y, 1)]
        for i in FAR_FIRST + (0,):
            to = (y + i) % NY
            for j in FAR_FIRST + (0,):
                sector = (to * NZ + (z + j) % NZ, q)
                if j in (1, NZ - 1):
                    remote(
                        shares.at[n, 1 if j == 1 else 2, :, pl.ds(to, 1)], got[n].at[:, z, pl.ds(y, 1)],
                        s_ssem.at[n], s_rsem.at[n], sector,
                    )
                elif j:
                    remote(
                        shares.at[n, 0, pl.ds(2, 2), pl.ds(to, 1)], got[n].at[pl.ds(2, 2), z, pl.ds(y, 1)],
                        o_ssem.at[n], o_rsem.at[n], sector,
                    )
                elif i:
                    remote(
                        shares.at[n, 0, :, pl.ds(to, 1)], got[n].at[:, z, pl.ds(y, 1)],
                        r_ssem.at[n], r_rsem.at[n], sector,
                    )
            for side, k in enumerate((1, NAX - 1)):
                remote(
                    shares.at[n, 0, pl.ds(0, 2), pl.ds(to, 1)], beside.at[n, side, :, pl.ds(y, 1)],
                    a_ssem.at[n], a_rsem.at[n], (to * NZ + z, (q + k) % NAX),
                )

    def wait_shares(n, s_sem, o_sem, r_sem, a_sem):
        wait_for(got[n].at[:, pl.ds(0, 2)], s_sem.at[n])
        wait_for(got[n].at[pl.ds(0, 2), pl.ds(0, NZ - 3)], o_sem.at[n])
        wait_for(got[n].at[:, 0, pl.ds(0, NY - 1)], r_sem.at[n])
        wait_for(beside.at[n], a_sem.at[n])

    def unpacked(first, second):
        rows = [jnp.sum(x, axis=0, keepdims=True) for x in (first, second)]
        tile = jnp.concatenate([jnp.broadcast_to(x, (8, GS)) for x in rows], axis=0)
        return jnp.where(lane // NV == rotor % 8, tile, 0.0)

    def get_shares(n):
        wait_shares(n, s_rsem, o_rsem, r_rsem, a_rsem)

        def along_z(at, h=0):
            return unpacked(got[n][h, at], got[n][h + 1, at])

        sides = (
            along_z((z + NZ - 1) % NZ), along_z((z + 1) % NZ),
            unpacked(beside[n, 0, 0], beside[n, 0, 1]), unpacked(beside[n, 1, 0], beside[n, 1, 1]),
        )
        return along_z(z), sides, along_z((z + NZ - shift_z) % NZ, 2)

    def prolong(coarse, rows):
        out = joined(nn(two_parts(coarse), rows))
        return [out[:, i * GS : (i + 1) * GS] for i in range(rows.shape[1] // GS)]

    def inner_products(residual, image):
        cross = residual[0] * image[0]
        square = image[0] * image[0]
        for a in range(1, GA):
            cross = cross + residual[a] * image[a]
            square = square + image[a] * image[a]
        cross = jnp.sum(cross, axis=1, keepdims=True)
        square = jnp.sum(square, axis=1, keepdims=True)
        spread_out = jnp.where(lane == rotor, cross, jnp.where(lane == rotor + R, square, 0.0))
        return jnp.sum(spread_out, axis=0, keepdims=True)

    def send_inner(n, row):
        f_rows[n, pl.ds(NAX - 1, 1)] = row
        for k in FAR_FIRST:
            remote(
                f_rows.at[n, pl.ds(NAX - 1, 1)], f_rows.at[n, pl.ds(k - 1, 1)],
                f_ssem.at[n], f_rsem.at[n], x_peer(k),
            )

    def pass_inner(n):
        wait_for(f_rows.at[n, pl.ds(0, NAX - 1)], f_rsem.at[n])
        e_rows[n, pl.ds(NSEC - 1, 1)] = jnp.sum(f_rows[n], axis=0, keepdims=True)

        for i in FAR_FIRST + (0,):
            for j in FAR_FIRST + (0,):
                if i or j:
                    remote(
                        e_rows.at[n, pl.ds(NSEC - 1, 1)], e_rows.at[n, pl.ds(i * NZ + j - 1, 1)],
                        e_ssem.at[n], e_rsem.at[n], ((y + i) % NY * NZ + (z + j) % NZ, q),
                    )

    def get_step(n):
        wait_for(e_rows.at[n, pl.ds(0, NSEC - 1)], e_rsem.at[n])
        row = jnp.sum(e_rows[n], axis=0, keepdims=True)
        cross = jnp.sum(jnp.where(lane == rotor, row, 0.0), axis=1, keepdims=True)
        square = jnp.sum(jnp.where(lane == rotor + R, row, 0.0), axis=1, keepdims=True)
        return cross / (square + EPSILON)

    coarse_r0 = coarse_of(r0)

    pl.semaphore_wait(barrier, 7 + 7 + 7 + 2)

    send_x(coarse_r0)
    send_halo(0, r0)
    for k in FAR_FIRST:
        remote(inverse_for((y + k) % NY), inverse_y.at[y], m_ssem, m_rsem, y_peer(k))
    send_rows(c1, basis[0].astype(BF16), c1_ssem, c1_rsem, z_peer)
    send_halo(4, basis)
    pass_z()
    basis_each = jnp.concatenate([each(t) for t in basis], axis=1)
    halo_r0 = get_halo(0)
    solver_copy.wait()
    local_r0 = local_solve(r0, halo_r0)
    send_band(0, local_r0[0])
    send_halo(1, local_r0)
    send_rows(c2, get_rows(c1, c1_rsem, shift_z), c2_ssem, c2_rsem, y_peer)
    send_shares(0, get_z())
    forward_band(0)
    basis_sides = [each(t) for t in get_halo(4)]
    halo = get_halo(1)
    band_row = get_band(0)
    band_basis = each(get_rows(c2, c2_rsem, up))

    def with_coarse(field, halo, band_row, n):
        coarse, sides, band = get_shares(n)
        own = [u + v for u, v in zip(field, prolong(coarse, basis_each))]
        around = [u + prolong(v, w)[0] for u, v, w in zip(halo, sides, basis_sides)]
        return own, around, band_row + prolong(band, band_basis)[0]

    corr0, halo, band_row = with_coarse(local_r0, halo, band_row, 0)
    image0 = apply_operator(corr0, halo, band_row)

    send_halo(2, image0)
    send_plane(image0)
    send_inner(0, inner_products(r0, image0))
    local_im = local_solve(image0, get_halo(2))
    send_band(1, local_im[0])
    send_halo(3, local_im)
    pass_inner(0)
    send_shares(1, get_plane())
    forward_band(1)
    step0 = get_step(0)
    res1 = [u - step0 * v for u, v in zip(r0, image0)]
    halo = get_halo(3)
    band_row = get_band(1)
    diff, halo, band_row = with_coarse(local_im, halo, band_row, 1)
    image_diff = apply_operator(diff, halo, band_row)
    image1 = [u - step0 * v for u, v in zip(image0, image_diff)]

    send_inner(1, inner_products(res1, image1))
    pass_inner(1)
    corr1 = [u - step0 * v for u, v in zip(corr0, diff)]
    sol0 = [step0 * u for u in corr0]

    wait_for(inverse_y.at[pl.ds(0, NY - 1)], m_ssem)
    wait_for(c1.at[pl.ds(1, 7)], c1_ssem)
    wait_for(c2.at[pl.ds(1, 7)], c2_ssem)
    wait_for(x_recv, x_ssem)
    wait_for(z_tiles.at[pl.ds(0, NZ - 1)], z_ssem)
    wait_for(plane.at[:, pl.ds(0, NZ * NAX - 1)], p_ssem)
    for n in range(5):
        wait_for(h_recv.at[n], h_ssem.at[n])
    for n in range(2):
        wait_shares(n, s_ssem, o_ssem, r_ssem, a_ssem)
        wait_for(b1s[n].at[pl.ds(1, NY - 1)], b1_ssem.at[n])
        wait_for(b2s[n].at[pl.ds(1, NZ - 1)], b2_ssem.at[n])
        wait_for(f_rows.at[n, pl.ds(0, NAX - 1)], f_ssem.at[n])
        wait_for(e_rows.at[n, pl.ds(0, NSEC - 1)], e_ssem.at[n])

    step1 = get_step(1)
    for a in range(GA):
        out_ref[0, :, a, :] = sol0[a] + step1 * corr1[a]
        out_ref[1, :, a, :] = res1[a] - step1 * image1[a]


def on_device(
    right_side, mass_term, band_weight, band_shift, local_solver, coarse_inverse, coarse_basis
):
    hbm = pl.BlockSpec(memory_space=pltpu.HBM)
    dma = pltpu.SemaphoreType.DMA

    def tiles(*shape):
        return pltpu.VMEM(shape + (GS,), F32)

    both = pl.pallas_call(
        body,
        name="schwarz_steps",
        out_shape=pltpu.VMEM((2,) + right_side.shape, F32),
        in_specs=[hbm, hbm, hbm, pl.BlockSpec(memory_space=pltpu.SMEM), hbm, hbm, hbm],
        out_specs=pl.BlockSpec(memory_space=pltpu.VMEM),
        scratch_shapes=[
            pltpu.VMEM(right_side.shape, F32),
            pltpu.VMEM(mass_term.shape, F32),
            pltpu.VMEM(band_weight.shape, F32),
            pltpu.VMEM(coarse_basis.shape, BF16),
            pltpu.VMEM((NEXT, GA * GS), BF16),
            pltpu.VMEM((NY, NV, NZ * GS), BF16),
            tiles(5, 3, R),
            tiles(5, 4, R),
            tiles(R),
            tiles(NAX - 1, R),
            tiles(NZ, R),
            tiles(2, NZ * NAX),
            tiles(2, 3, 4, NY),
            tiles(2, 2, 2, NY),
            tiles(4, NZ, NY),
            tiles(4, NZ, NY),
            tiles(NY, R),
            tiles(NY, R),
            tiles(NY, R),
            tiles(NZ, R),
            pltpu.VMEM((NZ, NV, GS), BF16),
            pltpu.VMEM((NY, NV, GS), BF16),
            tiles(2, NAX),
            tiles(2, NSEC),
            dma((6,)),
            dma,
            dma,
            dma,
            dma,
            dma,
            dma,
            dma((5,)),
            dma((5,)),
        ]
        + [dma] * 6
        + [dma((2,))] * 16,
        compiler_params=pltpu.CompilerParams(
            collective_id=0, has_side_effects=True, vmem_limit_bytes=60 << 20
        ),
    )(
        right_side, mass_term, band_weight, band_shift, coarse_basis,
        jnp.swapaxes(local_solver, 1, 2), coarse_inverse,
    )
    return both[0], both[1]


def solution(mesh):
    placed = (
        P(None, "axial", "sector"),
        P("axial", "sector"),
        P("axial", "sector"),
        P(),
        P("axial", "sector", None),
        P(("sector", "axial"), None),
        P(None, "axial", "sector"),
    )
    return jax.shard_map(
        on_device,
        mesh=mesh,
        in_specs=placed,
        out_specs=(P(None, "axial", "sector"), P(None, "axial", "sector")),
        check_vma=False,
    )
```

```python
import jax
import jax.numpy as jnp
from jax import lax
from jax.experimental import pallas as pl
from jax.experimental.pallas import tpu as pltpu
from jax.sharding import PartitionSpec as P

EPSILON = 1e-06
MESH = pl.DeviceIdType.MESH
F32 = jnp.float32
BF16 = jnp.bfloat16

R = 16
GA = 4
GS = 128
NV = 16
NEXT = 780
NZ = 8
NY = 8
NSEC = NY * NZ
NAX = 8
FAR_FIRST = (4, 3, 5, 2, 6, 1, 7)


def nt(a, b):
    return lax.dot_general(a, b, (((1,), (1,)), ((), ())), preferred_element_type=F32)


def nn(a, b):
    return lax.dot_general(a, b, (((1,), (0,)), ((), ())), preferred_element_type=F32)


def two_parts(x):
    high = x.astype(BF16)
    low = (x - high.astype(F32)).astype(BF16)
    return jnp.concatenate([high, low], axis=0)


def joined(x):
    half = x.shape[0] // 2
    return x[:half] + x[half:]


def body(
    rhs_hbm, mass_hbm, bw_hbm, shift_ref, basis_hbm, solver_hbm, inverse_hbm,
    out_ref,
    rhs_ref, mass_ref, bw_ref, basis_ref,
    solver, inverse_y, h_send, h_recv, x_send, x_recv, z_tiles, plane, shares, beside,
    got_first, got_second, b1_first, b1_second, b2_first, b2_second, c1, c2, f_rows, e_rows,
    local_sems, c1_ssem, c1_rsem, c2_ssem, c2_rsem, m_ssem, m_rsem, h_ssem, h_rsem, x_ssem, x_rsem, z_ssem, z_rsem, p_ssem, p_rsem,
    s_ssem, s_rsem, o_ssem, o_rsem, r_ssem, r_rsem, a_ssem, a_rsem, b1_ssem, b1_rsem, b2_ssem, b2_rsem, f_ssem, f_rsem, e_ssem, e_rsem,
):
    got = (got_first, got_second)
    b1s = (b1_first, b1_second)
    b2s = (b2_first, b2_second)
    s = lax.axis_index("sector")
    q = lax.axis_index("axial")
    y = s // NZ
    z = s % NZ

    def x_peer(k):
        return (s, (q + k) % NAX)

    def y_peer(k):
        return (((y + k) % NY) * NZ + z, q)

    def z_peer(k):
        return (y * NZ + (z + k) % NZ, q)

    def s_peer(k):
        return ((s + k) % NSEC, q)

    def wait_for(ref, sem):
        pltpu.make_async_copy(ref, ref, sem).wait()

    def remote(src, dst, ssem, rsem, device):
        pltpu.make_async_remote_copy(
            src_ref=src, dst_ref=dst, send_sem=ssem, recv_sem=rsem,
            device_id=device, device_id_type=MESH,
        ).start()

    barrier = pltpu.get_barrier_semaphore()
    for k in FAR_FIRST:
        for peer in (y_peer(k), z_peer(k), x_peer(k)):
            pl.semaphore_signal(barrier, inc=1, device_id=peer, device_id_type=MESH)
    for k in (1, NSEC - 1):
        pl.semaphore_signal(barrier, inc=1, device_id=s_peer(k), device_id_type=MESH)

    loads = [
        pltpu.make_async_copy(src, dst, local_sems.at[i])
        for i, (src, dst) in enumerate(
            ((rhs_hbm, rhs_ref), (basis_hbm, basis_ref), (mass_hbm, mass_ref), (bw_hbm, bw_ref))
        )
    ]
    for load in loads:
        load.start()
    solver_copy = pltpu.make_async_copy(solver_hbm.at[0], solver, local_sems.at[4])
    solver_copy.start()

    def inverse_for(to):
        return inverse_hbm.at[:, pl.ds(pl.multiple_of(to * NZ * GS, NZ * GS), NZ * GS)]

    own_copy = pltpu.make_async_copy(inverse_for(y), inverse_y.at[y], local_sems.at[5])
    own_copy.start()

    lane = lax.broadcasted_iota(jnp.int32, (R, GS), 1)
    rotor = lax.broadcasted_iota(jnp.int32, (R, GS), 0)
    lane8 = lax.broadcasted_iota(jnp.int32, (8, GS), 1)
    row8 = lax.broadcasted_iota(jnp.int32, (8, GS), 0)
    rows128 = lax.broadcasted_iota(jnp.int32, (8 * NV, GS), 0) // NV
    for load in loads:
        load.wait()
    rhs = rhs_ref[...]
    r0 = [rhs[:, a, :] for a in range(GA)]
    basis_all = basis_ref[...].astype(F32)
    basis = [basis_all[:, a, :] for a in range(GA)]
    mass = [mass_ref[a : a + 1, :] + 4.0 for a in range(GA)]
    weight = bw_ref[...]
    shift = shift_ref[0]
    shift_z = shift % NZ
    up = (shift // NZ + jnp.where(z < shift_z, 1, 0)) % NY
    up_there = (shift // NZ + jnp.where(z + shift_z >= NZ, 1, 0)) % NY

    def spread(tile, at):
        return jnp.where(rows128 == at, jnp.concatenate([tile] * 8, axis=0), 0.0).astype(BF16)

    def each(tile):
        return jnp.concatenate([tile.astype(F32)] * 8, axis=0).astype(BF16)

    basis_q = jnp.concatenate([spread(t, q) for t in basis], axis=1)

    def coarse_of(field):
        return joined(nt(two_parts(jnp.concatenate(field, axis=1)), basis_q))

    def packed(tile):
        kept = jnp.where(lane // NV == rotor % 8, tile, 0.0)
        return [jnp.sum(kept[8 * h : 8 * h + 8], axis=0, keepdims=True) for h in range(2)]

    def block_transposed(x):
        for d in (4, 2, 1):
            from_above = pltpu.roll(pltpu.roll(x, d, 0), GS - NV * d, 1)
            from_below = pltpu.roll(pltpu.roll(x, 8 - d, 0), NV * d, 1)
            row_bit = (row8 // d) % 2
            block_bit = (lane8 // (NV * d)) % 2
            x = jnp.where(row_bit == block_bit, x, jnp.where(row_bit == 1, from_above, from_below))
        return x

    def edges(field):
        tile = jnp.zeros((R, GS), F32)
        for a in range(GA):
            at = 2 * (a + 1)
            moved = pltpu.roll(field[a], at + 1, 1)
            tile = jnp.where((lane == at) | (lane == at + 1), moved, tile)
        return tile

    def send_halo(n, field):
        h_send[n, 0] = edges(field)
        h_send[n, 1] = field[0]
        h_send[n, 2] = field[GA - 1]
        remote(h_send.at[n, 0], h_recv.at[n, 0], h_ssem.at[n], h_rsem.at[n], s_peer(1))
        remote(h_send.at[n, 0], h_recv.at[n, 1], h_ssem.at[n], h_rsem.at[n], s_peer(NSEC - 1))
        remote(h_send.at[n, 2], h_recv.at[n, 2], h_ssem.at[n], h_rsem.at[n], x_peer(1))
        remote(h_send.at[n, 1], h_recv.at[n, 3], h_ssem.at[n], h_rsem.at[n], x_peer(NAX - 1))

    def get_halo(n):
        wait_for(h_recv.at[n], h_rsem.at[n])
        above = jnp.where(q == 0, 0.0, h_recv[n, 2])
        below = jnp.where(q == NAX - 1, 0.0, h_recv[n, 3])
        return h_recv[n, 0], h_recv[n, 1], above, below

    def local_solve(field, halo):
        left, right, above, below = halo
        stack = [above] + field + [below]
        moved = [pltpu.roll(stack[j], 2 * j + 1, 1) for j in range(GA + 2)]
        zero = jnp.zeros((R, GS), F32)
        parts = []
        for t in range(GA + 3):
            here = moved[t] if t < GA + 2 else zero
            before = moved[t - 1] if t > 0 else zero
            tile = jnp.where(lane == 2 * t - 1, right, before)
            tile = jnp.where(lane == 2 * t, left, tile)
            parts.append(jnp.where(lane > 2 * t, here, tile))
        window = jnp.concatenate(parts, axis=1)
        out = joined(nn(two_parts(window)[:, :NEXT], solver[...]))
        return [out[:, a * GS : (a + 1) * GS] for a in range(GA)]

    def apply_operator(field, halo, band):
        left, right, above, below = halo
        stack = [above] + field + [below]
        image = []
        for a in range(GA):
            u = field[a]
            before = jnp.where(lane == 0, pltpu.roll(left, GS - 2 * (a + 1), 1), pltpu.roll(u, 1, 1))
            after = jnp.where(
                lane == GS - 1, pltpu.roll(right, GS - 1 - (2 * a + 3), 1), pltpu.roll(u, GS - 1, 1)
            )
            value = mass[a] * u - ((stack[a + 2] + stack[a]) + before + after)
            if a == 0:
                value = value + weight * (u - band)
            image.append(value)
        return image

    def send_rows(slots, first, ssem, rsem, peer):
        slots[0] = first
        for k in FAR_FIRST:
            remote(slots.at[0], slots.at[k], ssem, rsem, peer(k))

    def get_rows(slots, sem, at):
        wait_for(slots.at[pl.ds(1, 7)], sem)
        return slots[at]

    def send_band(n, rows):
        send_rows(b1s[n], rows, b1_ssem.at[n], b1_rsem.at[n], z_peer if n == 0 else y_peer)

    def forward_band(n):
        row = get_rows(b1s[n], b1_rsem.at[n], shift_z if n == 0 else up_there)
        send_rows(b2s[n], row, b2_ssem.at[n], b2_rsem.at[n], y_peer if n == 0 else z_peer)

    def get_band(n):
        return get_rows(b2s[n], b2_rsem.at[n], up if n == 0 else shift_z)

    def send_x(coarse):
        x_send[...] = coarse
        for k in FAR_FIRST:
            remote(x_send, x_recv.at[k - 1], x_ssem, x_rsem, x_peer(k))

    def pass_z():
        wait_for(x_recv, x_rsem)
        total = x_send[...]
        for k in range(NAX - 1):
            total = total + x_recv[k]
        z_tiles[z] = total
        for k in FAR_FIRST:
            remote(z_tiles.at[z], z_tiles.at[z], z_ssem, z_rsem, z_peer(k))

    def get_z():
        wait_for(z_tiles.at[pl.ds(0, NZ - 1)], z_rsem)
        own_copy.wait()
        wait_for(inverse_y.at[pl.ds(0, NY - 1)], m_rsem)
        return jnp.concatenate([z_tiles[t] for t in range(NZ)], axis=1)

    def send_plane(field):
        out = joined(nt(two_parts(jnp.concatenate(field, axis=1)), basis_each))
        at = z * NAX + q
        for h, row in enumerate(packed(out)):
            plane[h, pl.ds(at, 1)] = row
        for j in FAR_FIRST + (0,):
            for i in FAR_FIRST + (0,):
                if i or j:
                    remote(
                        plane.at[:, pl.ds(at, 1)], plane.at[:, pl.ds(at, 1)],
                        p_ssem, p_rsem, (y * NZ + (z + j) % NZ, (q + i) % NAX),
                    )

    def get_plane():
        wait_for(plane.at[:, pl.ds(0, NZ * NAX - 1)], p_rsem)
        halves = [
            jnp.concatenate([block_transposed(plane[h, pl.ds(8 * t, 8)]) for t in range(NZ)], axis=1)
            for h in range(2)
        ]
        return jnp.concatenate(halves, axis=0)

    def send_shares(n, gathered):
        matrix = jnp.concatenate([inverse_y[t] for t in range(NY)], axis=0)
        out = joined(nt(two_parts(gathered), matrix))
        for h in range(2):
            share = block_transposed(out[8 * h : 8 * h + 8])
            band = pltpu.roll(share, up_there, 0)
            ahead = jnp.where(z == NZ - 1, pltpu.roll(share, 1, 0), share)
            behind = jnp.where(z == 0, pltpu.roll(share, NY - 1, 0), share)
            for i, own in enumerate((share, ahead, behind)):
                shares[n, i, h] = own
                shares[n, i, 2 + h] = band
        for h in range(4):
            got[n][h, z, pl.ds(y, 1)] = shares[n, 0, h, pl.ds(y, 1)]
        for i in FAR_FIRST + (0,):
            to = (y + i) % NY
            for j in FAR_FIRST + (0,):
                sector = (to * NZ + (z + j) % NZ, q)
                if j in (1, NZ - 1):
                    remote(
                        shares.at[n, 1 if j == 1 else 2, :, pl.ds(to, 1)], got[n].at[:, z, pl.ds(y, 1)],
                        s_ssem.at[n], s_rsem.at[n], sector,
                    )
                elif j:
                    remote(
                        shares.at[n, 0, pl.ds(2, 2), pl.ds(to, 1)], got[n].at[pl.ds(2, 2), z, pl.ds(y, 1)],
                        o_ssem.at[n], o_rsem.at[n], sector,
                    )
                elif i:
                    remote(
                        shares.at[n, 0, :, pl.ds(to, 1)], got[n].at[:, z, pl.ds(y, 1)],
                        r_ssem.at[n], r_rsem.at[n], sector,
                    )
            for side, k in enumerate((1, NAX - 1)):
                remote(
                    shares.at[n, 0, pl.ds(0, 2), pl.ds(to, 1)], beside.at[n, side, :, pl.ds(y, 1)],
                    a_ssem.at[n], a_rsem.at[n], (to * NZ + z, (q + k) % NAX),
                )

    def wait_shares(n, s_sem, o_sem, r_sem, a_sem):
        wait_for(got[n].at[:, pl.ds(0, 2)], s_sem.at[n])
        wait_for(got[n].at[pl.ds(0, 2), pl.ds(0, NZ - 3)], o_sem.at[n])
        wait_for(got[n].at[:, 0, pl.ds(0, NY - 1)], r_sem.at[n])
        wait_for(beside.at[n], a_sem.at[n])

    def unpacked(first, second):
        rows = [jnp.sum(x, axis=0, keepdims=True) for x in (first, second)]
        tile = jnp.concatenate([jnp.broadcast_to(x, (8, GS)) for x in rows], axis=0)
        return jnp.where(lane // NV == rotor % 8, tile, 0.0)

    def get_shares(n):
        wait_shares(n, s_rsem, o_rsem, r_rsem, a_rsem)

        def along_z(at, h=0):
            return unpacked(got[n][h, at], got[n][h + 1, at])

        sides = (
            along_z((z + NZ - 1) % NZ), along_z((z + 1) % NZ),
            unpacked(beside[n, 0, 0], beside[n, 0, 1]), unpacked(beside[n, 1, 0], beside[n, 1, 1]),
        )
        return along_z(z), sides, along_z((z + NZ - shift_z) % NZ, 2)

    def prolong(coarse, rows):
        out = joined(nn(two_parts(coarse), rows))
        return [out[:, i * GS : (i + 1) * GS] for i in range(rows.shape[1] // GS)]

    def inner_products(residual, image):
        cross = residual[0] * image[0]
        square = image[0] * image[0]
        for a in range(1, GA):
            cross = cross + residual[a] * image[a]
            square = square + image[a] * image[a]
        cross = jnp.sum(cross, axis=1, keepdims=True)
        square = jnp.sum(square, axis=1, keepdims=True)
        spread_out = jnp.where(lane == rotor, cross, jnp.where(lane == rotor + R, square, 0.0))
        return jnp.sum(spread_out, axis=0, keepdims=True)

    def send_inner(n, row):
        f_rows[n, pl.ds(NAX - 1, 1)] = row
        for k in FAR_FIRST:
            remote(
                f_rows.at[n, pl.ds(NAX - 1, 1)], f_rows.at[n, pl.ds(k - 1, 1)],
                f_ssem.at[n], f_rsem.at[n], x_peer(k),
            )

    def pass_inner(n):
        wait_for(f_rows.at[n, pl.ds(0, NAX - 1)], f_rsem.at[n])
        e_rows[n, pl.ds(NSEC - 1, 1)] = jnp.sum(f_rows[n], axis=0, keepdims=True)

        for i in FAR_FIRST + (0,):
            for j in FAR_FIRST + (0,):
                if i or j:
                    remote(
                        e_rows.at[n, pl.ds(NSEC - 1, 1)], e_rows.at[n, pl.ds(i * NZ + j - 1, 1)],
                        e_ssem.at[n], e_rsem.at[n], ((y + i) % NY * NZ + (z + j) % NZ, q),
                    )

    def get_step(n):
        wait_for(e_rows.at[n, pl.ds(0, NSEC - 1)], e_rsem.at[n])
        row = jnp.sum(e_rows[n], axis=0, keepdims=True)
        cross = jnp.sum(jnp.where(lane == rotor, row, 0.0), axis=1, keepdims=True)
        square = jnp.sum(jnp.where(lane == rotor + R, row, 0.0), axis=1, keepdims=True)
        return cross / (square + EPSILON)

    coarse_r0 = coarse_of(r0)

    pl.semaphore_wait(barrier, 7 + 7 + 7 + 2)

    send_x(coarse_r0)
    send_halo(0, r0)
    for k in FAR_FIRST:
        remote(inverse_for((y + k) % NY), inverse_y.at[y], m_ssem, m_rsem, y_peer(k))
    send_rows(c1, basis[0].astype(BF16), c1_ssem, c1_rsem, z_peer)
    pass_z()
    send_halo(4, basis)
    basis_each = jnp.concatenate([each(t) for t in basis], axis=1)
    halo_r0 = get_halo(0)
    solver_copy.wait()
    local_r0 = local_solve(r0, halo_r0)
    send_band(0, local_r0[0])
    send_halo(1, local_r0)
    send_rows(c2, get_rows(c1, c1_rsem, shift_z), c2_ssem, c2_rsem, y_peer)
    send_shares(0, get_z())
    forward_band(0)
    basis_sides = [each(t) for t in get_halo(4)]
    halo = get_halo(1)
    band_row = get_band(0)
    band_basis = each(get_rows(c2, c2_rsem, up))

    def with_coarse(field, halo, band_row, n):
        coarse, sides, band = get_shares(n)
        own = [u + v for u, v in zip(field, prolong(coarse, basis_each))]
        around = [u + prolong(v, w)[0] for u, v, w in zip(halo, sides, basis_sides)]
        return own, around, band_row + prolong(band, band_basis)[0]

    corr0, halo, band_row = with_coarse(local_r0, halo, band_row, 0)
    image0 = apply_operator(corr0, halo, band_row)

    send_halo(2, image0)
    send_plane(image0)
    send_inner(0, inner_products(r0, image0))
    local_im = local_solve(image0, get_halo(2))
    send_band(1, local_im[0])
    send_halo(3, local_im)
    pass_inner(0)
    send_shares(1, get_plane())
    forward_band(1)
    step0 = get_step(0)
    res1 = [u - step0 * v for u, v in zip(r0, image0)]
    halo = get_halo(3)
    band_row = get_band(1)
    diff, halo, band_row = with_coarse(local_im, halo, band_row, 1)
    image_diff = apply_operator(diff, halo, band_row)
    image1 = [u - step0 * v for u, v in zip(image0, image_diff)]

    send_inner(1, inner_products(res1, image1))
    pass_inner(1)
    corr1 = [u - step0 * v for u, v in zip(corr0, diff)]
    sol0 = [step0 * u for u in corr0]

    wait_for(inverse_y.at[pl.ds(0, NY - 1)], m_ssem)
    wait_for(c1.at[pl.ds(1, 7)], c1_ssem)
    wait_for(c2.at[pl.ds(1, 7)], c2_ssem)
    wait_for(x_recv, x_ssem)
    wait_for(z_tiles.at[pl.ds(0, NZ - 1)], z_ssem)
    wait_for(plane.at[:, pl.ds(0, NZ * NAX - 1)], p_ssem)
    for n in range(5):
        wait_for(h_recv.at[n], h_ssem.at[n])
    for n in range(2):
        wait_shares(n, s_ssem, o_ssem, r_ssem, a_ssem)
        wait_for(b1s[n].at[pl.ds(1, NY - 1)], b1_ssem.at[n])
        wait_for(b2s[n].at[pl.ds(1, NZ - 1)], b2_ssem.at[n])
        wait_for(f_rows.at[n, pl.ds(0, NAX - 1)], f_ssem.at[n])
        wait_for(e_rows.at[n, pl.ds(0, NSEC - 1)], e_ssem.at[n])

    step1 = get_step(1)
    for a in range(GA):
        out_ref[0, :, a, :] = sol0[a] + step1 * corr1[a]
        out_ref[1, :, a, :] = res1[a] - step1 * image1[a]


def on_device(
    right_side, mass_term, band_weight, band_shift, local_solver, coarse_inverse, coarse_basis
):
    hbm = pl.BlockSpec(memory_space=pltpu.HBM)
    dma = pltpu.SemaphoreType.DMA

    def tiles(*shape):
        return pltpu.VMEM(shape + (GS,), F32)

    both = pl.pallas_call(
        body,
        name="schwarz_steps",
        out_shape=pltpu.VMEM((2,) + right_side.shape, F32),
        in_specs=[hbm, hbm, hbm, pl.BlockSpec(memory_space=pltpu.SMEM), hbm, hbm, hbm],
        out_specs=pl.BlockSpec(memory_space=pltpu.VMEM),
        scratch_shapes=[
            pltpu.VMEM(right_side.shape, F32),
            pltpu.VMEM(mass_term.shape, F32),
            pltpu.VMEM(band_weight.shape, F32),
            pltpu.VMEM(coarse_basis.shape, BF16),
            pltpu.VMEM((NEXT, GA * GS), BF16),
            pltpu.VMEM((NY, NV, NZ * GS), BF16),
            tiles(5, 3, R),
            tiles(5, 4, R),
            tiles(R),
            tiles(NAX - 1, R),
            tiles(NZ, R),
            tiles(2, NZ * NAX),
            tiles(2, 3, 4, NY),
            tiles(2, 2, 2, NY),
            tiles(4, NZ, NY),
            tiles(4, NZ, NY),
            tiles(NY, R),
            tiles(NY, R),
            tiles(NY, R),
            tiles(NZ, R),
            pltpu.VMEM((NZ, NV, GS), BF16),
            pltpu.VMEM((NY, NV, GS), BF16),
            tiles(2, NAX),
            tiles(2, NSEC),
            dma((6,)),
            dma,
            dma,
            dma,
            dma,
            dma,
            dma,
            dma((5,)),
            dma((5,)),
        ]
        + [dma] * 6
        + [dma((2,))] * 16,
        compiler_params=pltpu.CompilerParams(
            collective_id=0, has_side_effects=True, vmem_limit_bytes=60 << 20
        ),
    )(
        right_side, mass_term, band_weight, band_shift, coarse_basis,
        jnp.swapaxes(local_solver, 1, 2), coarse_inverse,
    )
    return both[0], both[1]


def solution(mesh):
    placed = (
        P(None, "axial", "sector"),
        P("axial", "sector"),
        P("axial", "sector"),
        P(),
        P("axial", "sector", None),
        P(("sector", "axial"), None),
        P(None, "axial", "sector"),
    )
    return jax.shard_map(
        on_device,
        mesh=mesh,
        in_specs=placed,
        out_specs=(P(None, "axial", "sector"), P(None, "axial", "sector")),
        check_vma=False,
    )
```
